128 devices in a mesh: gx: 16 (over x, z_hi, core), gy: 4 (over y), gz: 2 (over z_lo).
Axes of the slice: x: 4, y: 4, z: 4 (z_hi: 2, z_lo: 2; z = z_hi * 2 + z_lo), core: 2. Of those that a mesh axis runs over, the one named last changes fastest.
Arguments:
- positions: float32 [3, 32, 8, 4, 128], P(None, 'gx', 'gy', 'gz'), may hold values from 0 to 1
- velocities: float32 [3, 32, 8, 4, 128], P(None, 'gx', 'gy', 'gz'), may hold values from -3 to 3
- spins: float32 [3, 32, 8, 4, 128], P(None, 'gx', 'gy', 'gz'), may hold values from -6 to 6
- radii: float32 [32, 8, 4, 128], P('gx', 'gy', 'gz'), may hold values from 0.08 to 0.13
- counts: int32 [32, 8, 4], P('gx', 'gy', 'gz'), may hold values from 16 to 128
- springs: float32 [3, 4, 32, 8, 4, 128], P(None, None, 'gx', 'gy', 'gz'), may hold values from -0.36 to 0.36
- partners: int32 [4, 32, 8, 4, 128], P(None, 'gx', 'gy', 'gz'), may hold values from -1 to 895, as said below
- cells: int32 [32, 8, 4, 128], P('gx', 'gy', 'gz'), may hold values from 0 to 16383, as said below
- departures: int32 [16, 4, 2, 6, 128], P('gx', 'gy', 'gz'), may hold values from -1 to 1023, as said below
- fluid_velocity: float32 [3, 256, 128, 512], P(None, 'gx', 'gy', 'gz'), may hold values from -6 to 6
- pressure: float32 [256, 128, 512], P('gx', 'gy', 'gz'), may hold values from -6 to 6
- pressure_source: float32 [256, 128, 512], P('gx', 'gy', 'gz'), may hold values from -6 to 6
Outputs:
- new_positions: float32 [3, 32, 8, 4, 128], P(None, 'gx', 'gy', 'gz')
- new_velocities: float32 [3, 32, 8, 4, 128], P(None, 'gx', 'gy', 'gz')
- new_spins: float32 [3, 32, 8, 4, 128], P(None, 'gx', 'gy', 'gz')
- new_springs: float32 [3, 4, 32, 8, 4, 128], P(None, None, 'gx', 'gy', 'gz')
- fluid_force: float32 [3, 256, 128, 512], P(None, 'gx', 'gy', 'gz')
- new_pressure: float32 [256, 128, 512], P('gx', 'gy', 'gz')
- arrived: float32 [16, 4, 2, 22, 6, 128], P('gx', 'gy', 'gz')
- arrived_partners: int32 [16, 4, 2, 4, 6, 128], P('gx', 'gy', 'gz')
The draws below stay inside these ranges and needn't reach their ends.
Inputs may be any that keep to these rules, and one draw needn't show every extreme that they name: `partners`: -1 marks an empty history slot; otherwise the code is bin * 128 + slot with bin 0 for the particle's own bin and 1 to 6 for the bins at -x, +x, -y, +y, -z, +z; a code never names the particle itself. The index of a cell within the particle's own bin's block of 8 x 32 // 2 x 256 // 2 cells, as in the reference program. `departures`: an entry is a local slot index ((bx * 2 + by) * 2 + bz) * 128 + slot, or -1; a slot appears at most once on its device; in each direction the used entries come first; in every draw some device fills all 128 entries of some direction.
All inputs are finite; a program needn't handle non-finite values.
Results may differ from the reference program's by a relative error of at most 0.0003.
Values sent between devices are 32-bit elements; how exact they have to be, the bound alone decides.
A program may use at most 192 MiB of HBM per device.

```python
import math
import jax
import jax.numpy as jnp
from jax import lax

SLOTS = 128
HIST = 4
SUBSTEPS = 2
BX = 2
BY = 2
BZ = 2
FX = 16
FY = 32
FZ = 256
MIG = 128
GBX = 32
GBY = 8
GBZ = 4
NFX = 256
NFY = 128
NFZ = 512


def draw_partners(key, part):
    extent = (HIST, GBX, GBY, GBZ, SLOTS)
    random_keys = jax.random.split(jax.random.fold_in(key, 71), 3)
    neighbour = jax.random.randint(random_keys[0], extent, 0, 7)
    member = jax.random.randint(random_keys[1], extent, 0, SLOTS)
    itself = lax.broadcasted_iota(jnp.int32, extent, 4)
    member = jnp.where((neighbour == 0) & (member == itself), (member + 1) % SLOTS, member)
    active = jax.random.randint(random_keys[2], extent, 0, 3) > 0
    return jnp.where(active, neighbour * SLOTS + member, -1).astype(jnp.int32)


def draw_cells(key, part):
    extent = (GBX, GBY, GBZ, SLOTS)
    random_keys = jax.random.split(jax.random.fold_in(key, 83), 3)
    cell_span = (FX // BX, FY // BY, FZ // BZ)
    coords = []
    for axis_id in range(3):
        coords.append(jax.random.randint(random_keys[axis_id], extent, 0, cell_span[axis_id]))
    return ((coords[0] * cell_span[1] + coords[1]) * cell_span[2] + coords[2]).astype(jnp.int32)


def draw_departures(key, part):
    grid_x = GBX // BX
    grid_y = GBY // BY
    grid_z = GBZ // BZ
    devices_all = grid_x * grid_y * grid_z
    population = BX * BY * BZ * SLOTS
    random_keys = jax.random.split(jax.random.fold_in(key, 97), 3)
    orders = jax.vmap(lambda single: jax.random.permutation(single, population))(jax.random.split(random_keys[0], devices_all))
    chosen = orders[:, :6 * MIG].reshape(devices_all, 6, MIG).astype(jnp.int32)
    filled = jax.random.randint(random_keys[1], (devices_all, 6), 1, MIG + 1)
    busiest = jax.random.randint(random_keys[2], (), 0, devices_all * 6)
    flat_id = jnp.arange(devices_all * 6, dtype=jnp.int32).reshape(devices_all, 6)
    filled = jnp.where(flat_id == busiest, MIG, filled)
    column = lax.broadcasted_iota(jnp.int32, (devices_all, 6, MIG), 2)
    result = jnp.where(column < filled[..., None], chosen, -1)
    return result.reshape(grid_x, grid_y, grid_z, 6, MIG).astype(jnp.int32)


def place_ends(values, key, smallest, largest):
    dims = values.shape
    index_at = [jax.random.randint(jax.random.fold_in(key, axis), (), 0, dims[axis]) for axis in range(len(dims))]
    values = values.at[tuple(index_at)].set(smallest)
    longest = dims.index(max(dims))
    index_at[longest] = (index_at[longest] + 1) % dims[longest]
    return values.at[tuple(index_at)].set(largest)


def shard_levels(stream_key, shape, cuts, smallest, high):
    gain = 1.0
    for dim, parts in cuts:
        steps = jax.random.uniform(jax.random.fold_in(jax.random.fold_in(stream_key, 6), dim), (parts,), jnp.float32, smallest / len(cuts), high / len(cuts))
        gain = gain * jnp.repeat(jnp.exp(steps), shape[dim] // parts).reshape((-1,) + (1,) * (len(shape) - 1 - dim))
    return gain


def bell_draw(own_key, shape, spread, most, cuts=(), kind=jnp.bfloat16):
    values = jax.random.normal(own_key, shape, jnp.float32) * spread
    if len(cuts) > 0:
        values = shard_levels(own_key, shape, cuts, -0.22, 0.18) * values
    return jnp.clip(values, min=-most, max=most).astype(kind)


def setup_inputs(seed: int = 0) -> dict:
    arg_keys = jax.random.split(jax.random.key(seed), 13)
    positions = jnp.clip(1.0 * jax.random.uniform(arg_keys[0], (3, GBX, GBY, GBZ, SLOTS), jnp.float32) ** shard_levels(arg_keys[0], (3, GBX, GBY, GBZ, SLOTS), ((1, 16), (2, 4), (3, 2)), -0.2, 0.2), 0.0, 1.0)
    velocities = bell_draw(arg_keys[1], (3, GBX, GBY, GBZ, SLOTS), 0.5, 3.0, ((1, 16), (2, 4), (3, 2)), jnp.float32)
    spins = bell_draw(arg_keys[2], (3, GBX, GBY, GBZ, SLOTS), 1.0, 6.0, ((1, 16), (2, 4), (3, 2)), jnp.float32)
    radii = jnp.clip(0.08 + 0.049999997 * jax.random.uniform(arg_keys[3], (GBX, GBY, GBZ, SLOTS), jnp.float32) ** shard_levels(arg_keys[3], (GBX, GBY, GBZ, SLOTS), ((0, 16), (1, 4), (2, 2)), -0.2, 0.2), 0.08, 0.13)
    counts = place_ends(jax.random.randint(arg_keys[4], (GBX, GBY, GBZ), SLOTS // 8, SLOTS + 1), jax.random.fold_in(arg_keys[4], 1), SLOTS // 8, SLOTS).astype(jnp.int32)
    springs = bell_draw(arg_keys[5], (3, HIST, GBX, GBY, GBZ, SLOTS), 0.06, 0.36, ((2, 16), (3, 4), (4, 2)), jnp.float32)
    partners = draw_partners(jax.random.fold_in(arg_keys[12], 71), 0)
    cells = draw_cells(jax.random.fold_in(arg_keys[12], 71), 0)
    departures = draw_departures(jax.random.fold_in(arg_keys[12], 71), 0)
    fluid_velocity = bell_draw(arg_keys[9], (3, NFX, NFY, NFZ), 1.0, 6.0, ((1, 16), (2, 4), (3, 2)), jnp.float32)
    pressure = bell_draw(arg_keys[10], (NFX, NFY, NFZ), 1.0, 6.0, ((0, 16), (1, 4), (2, 2)), jnp.float32)
    pressure_source = bell_draw(arg_keys[11], (NFX, NFY, NFZ), 1.0, 6.0, ((0, 16), (1, 4), (2, 2)), jnp.float32)
    return {"positions": positions, "velocities": velocities, "spins": spins, "radii": radii, "counts": counts, "springs": springs, "partners": partners, "cells": cells, "departures": departures, "fluid_velocity": fluid_velocity, "pressure": pressure, "pressure_source": pressure_source}


normal_stiff = 100.0
normal_damp = 2.0
shear_stiff = 30.0
friction = 0.5
time_step = 0.05
drag_coeff = 0.8
gravity = 1.0
soft_length = 0.05
force_floor = 0.5
volume_coeff = 100.0
drag_weight = 1.0
neighbours = ((0, 0, 0), (-1, 0, 0), (1, 0, 0), (0, -1, 0), (0, 1, 0), (0, 0, -1), (0, 0, 1))
shift_table = ((0, -1, 1, 0, 0, 0, 0), (0, 0, 0, -1, 1, 0, 0), (0, 0, 0, 0, 0, -1, 1))

def row_normal(padded, row):
    slab = lax.dynamic_slice_in_dim(padded, row, 3, 1)
    extent_b = slab.shape[2] - 2
    extent_c = slab.shape[3] - 2
    centre = slab[:, 1, 1:1 + extent_b, 1:1 + extent_c]
    totals = [jnp.zeros_like(centre[0]) for axis_id in range(3)]
    for step_x, step_y, step_z in neighbours:
        other = slab[:, 1 + step_x, 1 + step_y:1 + step_y + extent_b, 1 + step_z:1 + step_z + extent_c]
        moves = (step_x, step_y, step_z)
        separation = [centre[axis_id][..., :, None] - other[axis_id][..., None, :] - float(moves[axis_id]) for axis_id in range(3)]
        distance = jnp.sqrt(separation[0] * separation[0] + separation[1] * separation[1] + separation[2] * separation[2] + soft_length ** 2)
        intersection = jnp.maximum(centre[9][..., :, None] + other[9][..., None, :] - distance, 0.0)
        root = jnp.sqrt(intersection)
        approach = sum(((centre[3 + axis_id][..., :, None] - other[3 + axis_id][..., None, :]) * separation[axis_id] for axis_id in range(3))) / distance
        weight = (normal_stiff * intersection * root - normal_damp * root * approach) * other[10][..., None, :] / distance
        totals = [totals[axis_id] + lax.optimization_barrier(jnp.sum(weight * separation[axis_id], axis=-1)) for axis_id in range(3)]
    return jnp.stack(totals)

def normal_forces(padded):
    rows = padded.shape[1] - 2
    stacked = lax.map(lambda row: row_normal(padded, row), jnp.arange(rows, dtype=jnp.int32))
    return jnp.moveaxis(stacked, 0, 1)

def partner_state(padded, codes):
    fields = padded.shape[0]
    extent_b = padded.shape[2]
    extent_c = padded.shape[3]
    slots = padded.shape[4]
    valid = (codes >= 0).astype(jnp.float32)
    code = jnp.maximum(codes, 0)
    which_bin = code // slots
    member = code % slots
    moves = []
    for axis_id in range(3):
        total = jnp.zeros_like(which_bin)
        for number in range(7):
            total = total + jnp.where(which_bin == number, shift_table[axis_id][number], 0).astype(jnp.int32)
        moves.append(total)
    index_a = lax.broadcasted_iota(jnp.int32, codes.shape, 1)
    index_b = lax.broadcasted_iota(jnp.int32, codes.shape, 2)
    index_c = lax.broadcasted_iota(jnp.int32, codes.shape, 3)
    linear = (((index_a + 1 + moves[0]) * extent_b + (index_b + 1 + moves[1])) * extent_c + (index_c + 1 + moves[2])) * slots + member
    flat = padded.reshape(fields, -1)
    picked = jnp.take(flat, linear.reshape(-1).astype(jnp.int32), axis=1).reshape((fields,) + codes.shape)
    return (picked, valid, [move.astype(jnp.float32) for move in moves])

def advance(padded, fluid_u, springs, codes):
    centre = padded[:, 1:-1, 1:-1, 1:-1]
    places = centre[0:3]
    speeds = centre[3:6]
    turning = centre[6:9]
    radius = centre[9]
    normal = normal_forces(padded)
    other, valid, moves = partner_state(padded, codes)
    separation = jnp.stack([places[axis_id][None] - other[axis_id] - moves[axis_id] for axis_id in range(3)])
    distance = jnp.sqrt(lax.optimization_barrier(jnp.sum(separation * separation, axis=0)) + soft_length ** 2)
    unit = separation / distance
    intersection = jnp.maximum(radius[None] + other[9] - distance, 0.0)
    root = jnp.sqrt(intersection)
    relative = speeds[:, None] - other[3:6]
    approach = lax.optimization_barrier(jnp.sum(relative * unit, axis=0))
    pressing = normal_stiff * intersection * root - normal_damp * root * approach
    lever = radius[None] * turning[:, None] + other[9] * other[6:9]
    contact = relative - jnp.cross(lever, unit, axis=0)
    sliding = contact - lax.optimization_barrier(jnp.sum(contact * unit, axis=0)) * unit
    stretched = springs - lax.optimization_barrier(jnp.sum(springs * unit, axis=0)) * unit + time_step * sliding
    length = jnp.sqrt(lax.optimization_barrier(jnp.sum(stretched * stretched, axis=0)))
    limit = jnp.minimum(1.0, friction * jnp.abs(pressing) / jnp.maximum(shear_stiff * length, force_floor))
    new_springs = valid * other[10] * limit * stretched
    shear = -shear_stiff * new_springs
    torque = radius * lax.optimization_barrier(jnp.sum(jnp.cross(shear, unit, axis=0), axis=1))
    safe = jnp.where(radius > 0.0, radius, 1.0)
    mass = (safe / 0.1) ** 3
    inertia = 0.4 * mass * safe * safe
    force = normal + lax.optimization_barrier(jnp.sum(shear, axis=1)) + drag_coeff * (fluid_u - speeds)
    lift = jnp.array([0.0, 0.0, gravity], dtype=jnp.float32).reshape(3, 1, 1, 1, 1)
    new_speeds = speeds + time_step * (force / mass - lift)
    new_turning = turning + time_step * torque / inertia
    new_places = places + time_step * new_speeds
    return (new_places, new_speeds, new_turning, new_springs)

def move_along(block, axis_id, step):
    extent = block.shape[axis_id]
    widths = [(0, 0)] * block.ndim
    if step == 1:
        widths[axis_id] = (1, 0)
        return lax.slice_in_dim(jnp.pad(block, widths), 0, extent, axis=axis_id)
    widths[axis_id] = (0, 1)
    return lax.slice_in_dim(jnp.pad(block, widths), 1, extent + 1, axis=axis_id)

def global_cells(cells):
    span_x = FX // BX
    span_y = FY // BY
    span_z = FZ // BZ
    off_z = cells % span_z
    off_y = cells // span_z % span_y
    off_x = cells // (span_z * span_y)
    corner_x = lax.broadcasted_iota(jnp.int32, cells.shape, 0) * span_x
    corner_y = lax.broadcasted_iota(jnp.int32, cells.shape, 1) * span_y
    corner_z = lax.broadcasted_iota(jnp.int32, cells.shape, 2) * span_z
    whole_x = corner_x + off_x
    whole_y = corner_y + off_y
    whole_z = corner_z + off_z
    return ((whole_x * NFY + whole_y) * NFZ + whole_z).astype(jnp.int32)

def reference(positions, velocities, spins, radii, counts, springs, partners, cells, departures, fluid_velocity, pressure, pressure_source):
    slot_index = lax.broadcasted_iota(jnp.int32, radii.shape, 3)
    live = (slot_index < counts[..., None]).astype(jnp.float32)
    whole_cells = global_cells(cells)
    fluid_u = jnp.take(fluid_velocity.reshape(3, -1), whole_cells.reshape(-1), axis=1).reshape((3,) + cells.shape)
    state = jnp.concatenate([positions, velocities, spins, radii[None], live[None]], 0)
    for step in range(SUBSTEPS):
        padded = jnp.pad(state, ((0, 0), (1, 1), (1, 1), (1, 1), (0, 0)))
        places, speeds, turning, springs = advance(padded, fluid_u, springs, partners)
        state = jnp.concatenate([places, speeds, turning, state[9:11]], 0)
    volume = 4.0 / 3.0 * math.pi * radii ** 3 * live
    values = jnp.concatenate([drag_coeff * (speeds - fluid_u) * live, volume[None]], 0).reshape(4, -1)
    sums = jnp.zeros((4, NFX * NFY * NFZ), jnp.float32).at[:, whole_cells.reshape(-1)].add(values)
    fluid_force = sums[0:3].reshape(3, NFX, NFY, NFZ)
    rhs = pressure_source + volume_coeff * sums[3].reshape(NFX, NFY, NFZ) + drag_weight * fluid_force[2]
    beside_all = jnp.pad(pressure, 1)
    neighbour_sum = beside_all[2:, 1:-1, 1:-1] + beside_all[:-2, 1:-1, 1:-1] + beside_all[1:-1, 2:, 1:-1] + beside_all[1:-1, :-2, 1:-1] + beside_all[1:-1, 1:-1, 2:] + beside_all[1:-1, 1:-1, :-2]
    new_pressure = (neighbour_sum + rhs) / 6.0
    lanes = departures.shape
    device_x = lax.broadcasted_iota(jnp.int32, lanes, 0)
    device_y = lax.broadcasted_iota(jnp.int32, lanes, 1)
    device_z = lax.broadcasted_iota(jnp.int32, lanes, 2)
    index = jnp.maximum(departures, 0)
    member = index % SLOTS
    remain = index // SLOTS
    bin_z = remain % BZ
    bin_y = remain // BZ % BY
    bin_x = remain // (BZ * BY)
    global_x = device_x * BX + bin_x
    global_y = device_y * BY + bin_y
    global_z = device_z * BZ + bin_z
    valid = (departures >= 0).astype(jnp.float32)
    carried = jnp.concatenate([places, speeds, turning, radii[None], springs.reshape((3 * HIST,) + radii.shape)], 0)
    taken = carried[:, global_x, global_y, global_z, member] * valid
    taken_codes = jnp.where(departures >= 0, partners[:, global_x, global_y, global_z, member] + 1, 0).astype(jnp.int32)
    taken = jnp.moveaxis(taken, 0, 3)
    taken_codes = jnp.moveaxis(taken_codes, 0, 3)
    got = []
    got_codes = []
    for direction in range(6):
        step = -1 if direction % 2 == 0 else 1
        got.append(move_along(taken[:, :, :, :, direction], direction // 2, step))
        got_codes.append(move_along(taken_codes[:, :, :, :, direction], direction // 2, step))
    arrived = jnp.stack(got, axis=4)
    arrived_partners = (jnp.stack(got_codes, axis=4) - 1).astype(jnp.int32)
    return (places, speeds, turning, springs, fluid_force, new_pressure, arrived, arrived_partners)
```

```python
import functools
import math

import jax
import jax.numpy as jnp
from jax import lax
from jax.experimental import pallas as pl
from jax.experimental.pallas import tpu as pltpu
from jax.sharding import PartitionSpec as P

SUBSTEPS = 2
HIST = 4
BINS = 8
SLOTS = 128

normal_stiff = 100.0
normal_damp = 2.0
shear_stiff = 30.0
friction = 0.5
time_step = 0.05
drag_coeff = 0.8
gravity = 1.0
soft_length = 0.05
force_floor = 0.5
volume_coeff = 100.0
drag_weight = 1.0

NOBODY = -10.0
TINY = 1e-30
AXES = ("gx", "gy", "gz")
MESH = pl.DeviceIdType.MESH


def neighbour(direction):
    axis = AXES[direction // 2]
    size = lax.axis_size(axis)
    here = lax.axis_index(axis)
    if direction % 2 == 0:
        return {axis: lax.rem(here + size - 1, size)}, here > 0
    return {axis: lax.rem(here + 1, size)}, here < size - 1


def bin_bits():
    row = lax.broadcasted_iota(jnp.int32, (BINS, SLOTS), 0)
    return [lax.shift_right_logical(row, 2 - axis) & 1 for axis in range(3)]


def swapped(value, axis):
    step = 4 >> axis
    if axis == 0:
        return pltpu.roll(value, step, 0)
    upper = bin_bits()[axis] == 1
    return jnp.where(upper, pltpu.roll(value, step, 0), pltpu.roll(value, BINS - step, 0))


def live_mask(counts_ref):
    row = lax.broadcasted_iota(jnp.int32, (BINS, SLOTS), 0)
    slot = lax.broadcasted_iota(jnp.int32, (BINS, SLOTS), 1)
    limit = jnp.zeros((BINS, SLOTS), jnp.int32)
    for b in range(BINS):
        limit = jnp.where(row == b, counts_ref[b], limit)
    return slot < limit


def halves(value):
    high = value.astype(jnp.bfloat16).astype(jnp.float32)
    return high, value - high


def one_hot(index_row):
    rows = lax.broadcasted_iota(jnp.int32, (SLOTS, SLOTS), 0)
    return rows == index_row


def cross(a, b):
    return [
        a[1] * b[2] - a[2] * b[1],
        a[2] * b[0] - a[0] * b[2],
        a[0] * b[1] - a[1] * b[0],
    ]


def dot(a, b):
    return a[0] * b[0] + a[1] * b[1] + a[2] * b[2]


def pair_pass(columns_ref, table_ref, tables, sums_ref, first):
    def chunk(c, carry):
        start = pl.multiple_of(c * 8, 8)
        tile = columns_ref[pl.ds(start, 8), :]
        lane = lax.broadcasted_iota(jnp.int32, (8, SLOTS), 1)
        if first:
            result = jnp.zeros((8, SLOTS), jnp.float32)
        else:
            result = sums_ref[pl.ds(start, 8), :]
        for b in range(BINS):
            mine = [
                jnp.broadcast_to(tile[:, f * 8 + b : f * 8 + b + 1], (8, SLOTS)) for f in range(7)
            ]
            total = None
            for t in tables:
                other = [
                    jnp.broadcast_to(table_ref[t, f, b : b + 1, :], (8, SLOTS))
                    for f in (0, 1, 2, 3, 4, 5, 9)
                ]
                sep = [mine[i] - other[i] for i in range(3)]
                square = dot(sep, sep) + soft_length**2
                inverse = lax.rsqrt(square)
                overlap = mine[6] + other[6] - square * inverse
                delta = jnp.maximum(overlap, 0.0)
                root = delta * lax.rsqrt(jnp.maximum(overlap, TINY))
                vrel = [mine[3 + i] - other[3 + i] for i in range(3)]
                approach = dot(vrel, sep) * inverse
                weight = ((normal_stiff / normal_damp) * delta - approach) * (root * inverse)
                term = [weight * sep[i] for i in range(3)]
                total = term if total is None else [total[i] + term[i] for i in range(3)]
            for i in range(3):
                column = jnp.sum(total[i], axis=1, keepdims=True)
                fresh = result + column if not first else jnp.broadcast_to(column, (8, SLOTS))
                result = jnp.where(lane == i * 8 + b, fresh, result)
        sums_ref[pl.ds(start, 8), :] = result
        return carry

    lax.fori_loop(0, SLOTS // 8, chunk, 0)


def gathered(table_ref, tables, which, masks, member, got):
    for f in range(10):
        value = got[f]
        for t in tables:
            picked = jnp.take_along_axis(
                table_ref[t, f], member, axis=1, mode="promise_in_bounds"
            )
            value = jnp.where(masks[t], picked, value)
        got[f] = value
    return got


def particles(
    pos_ref,
    vel_ref,
    spin_ref,
    radii_ref,
    counts_ref,
    springs_ref,
    partners_ref,
    cells_ref,
    departures_ref,
    gas_hbm,
    pressure_hbm,
    state_out,
    springs_out,
    gas_out,
    moved_out,
    face_x_out,
    face_y_out,
    face_z_out,
    gas_ref,
    pressure_ref,
    table_ref,
    columns_ref,
    sums_ref,
    own_ref,
    halo_ref,
    own_2_ref,
    halo_2_ref,
    picked_ref,
    gone_ref,
    come_ref,
    send_y_ref,
    send_z_ref,
    face_x_ref,
    face_y_ref,
    face_z_ref,
    local_sem,
    send_sem,
    recv_sem,
):
    gas_copy = pltpu.make_async_copy(gas_hbm, gas_ref, local_sem.at[0])
    pressure_copy = pltpu.make_async_copy(pressure_hbm, pressure_ref, local_sem.at[1])
    gas_copy.start()
    pressure_copy.start()

    there = [neighbour(d) for d in range(6)]

    barrier = pltpu.get_barrier_semaphore()
    for d in range(6):

        @pl.when(there[d][1])
        def _():
            pl.semaphore_signal(barrier, inc=1, device_id=there[d][0], device_id_type=MESH)

    def halo_copy(d):
        return pltpu.make_async_remote_copy(
            src_ref=own_ref,
            dst_ref=halo_ref.at[d ^ 1],
            send_sem=send_sem.at[0, d],
            recv_sem=recv_sem.at[0, d ^ 1],
            device_id=there[d][0],
            device_id_type=MESH,
        )

    def halo_copy_2(d):
        return pltpu.make_async_remote_copy(
            src_ref=own_2_ref,
            dst_ref=halo_2_ref.at[d ^ 1],
            send_sem=send_sem.at[1, d],
            recv_sem=recv_sem.at[1, d ^ 1],
            device_id=there[d][0],
            device_id_type=MESH,
        )

    def moved_copy(d):
        return pltpu.make_async_remote_copy(
            src_ref=gone_ref.at[d],
            dst_ref=come_ref.at[d],
            send_sem=send_sem.at[2, d],
            recv_sem=recv_sem.at[2, d],
            device_id=there[d][0],
            device_id_type=MESH,
        )

    def face_copy(d):
        side = d % 2
        if d < 2:
            source = pressure_ref.at[0 if side == 0 else pressure_ref.shape[0] - 1]
            target = face_x_ref.at[1 - side]
        elif d < 4:
            source, target = send_y_ref.at[side], face_y_ref.at[1 - side]
        else:
            source, target = send_z_ref.at[side], face_z_ref.at[1 - side]
        return pltpu.make_async_remote_copy(
            src_ref=source,
            dst_ref=target,
            send_sem=send_sem.at[3, d],
            recv_sem=recv_sem.at[3, d ^ 1],
            device_id=there[d][0],
            device_id_type=MESH,
        )

    live = live_mask(counts_ref)
    radius = radii_ref[...]
    partner_radius = jnp.where(live, radius, NOBODY)
    for i in range(3):
        own_ref[i] = pos_ref[i]
        own_ref[3 + i] = vel_ref[i]
        own_ref[6 + i] = spin_ref[i]
    own_ref[9] = partner_radius

    for s in range(6):

        @pl.when(jnp.logical_not(there[s][1]))
        def _():
            halo_ref[s] = jnp.zeros((10, BINS, SLOTS), jnp.float32)
            halo_ref[s, 9] = jnp.full((BINS, SLOTS), NOBODY, jnp.float32)
            halo_2_ref[s] = jnp.zeros((9, BINS, SLOTS), jnp.float32)
            come_ref[s ^ 1] = jnp.zeros((32, SLOTS), jnp.float32)
            face = (face_x_ref, face_y_ref, face_z_ref)[s // 2]
            face[s % 2] = jnp.zeros(face.shape[1:], jnp.float32)

    pl.semaphore_wait(barrier, sum(there[d][1].astype(jnp.int32) for d in range(6)))

    for d in range(6):

        @pl.when(there[d][1])
        def _():
            halo_copy(d).start()

    pressure_copy.wait()
    cells_x, cells_y, cells_z = pressure_ref.shape
    lane = lax.broadcasted_iota(jnp.int32, (cells_y, SLOTS), 1)
    for side in range(2):
        send_y_ref[side] = pressure_ref[:, 0 if side == 0 else cells_y - 1, :]
        face = jnp.zeros((cells_y, SLOTS), jnp.float32)
        for x in range(cells_x):
            if side == 0:
                column = pressure_ref[x, :, 0:SLOTS][:, 0:1]
            else:
                column = pressure_ref[x, :, cells_z - SLOTS : cells_z][:, SLOTS - 1 : SLOTS]
            face = jnp.where(lane == x, jnp.broadcast_to(column, (cells_y, SLOTS)), face)
        send_z_ref[side] = face
    for d in range(6):

        @pl.when(there[d][1])
        def _():
            face_copy(d).start()

    bits = bin_bits()
    code = [partners_ref[k] for k in range(HIST)]
    valid = [jnp.where(code[k] >= 0, 1.0, 0.0) for k in range(HIST)]
    member = [jnp.maximum(code[k], 0) & (SLOTS - 1) for k in range(HIST)]
    which = [lax.shift_right_logical(jnp.maximum(code[k], 0), 7) for k in range(HIST)]

    def masks_of(k):
        found = [which[k] == 0]
        for axis in range(3):
            found.append(which[k] == 2 * axis + 2 - bits[axis])
        for axis in range(3):
            found.append(which[k] == 2 * axis + 1 + bits[axis])
        return found

    safe = jnp.where(radius > 0.0, radius, 1.0)
    mass = safe * 10.0
    mass = mass * mass * mass
    inertia = 0.4 * mass * safe * safe

    def inner_tables(fields):
        for f in range(10):
            table_ref[0, f] = fields[f]
            for axis in range(3):
                value = swapped(fields[f], axis)
                if f == axis:
                    value = value + jnp.where(bits[axis] == 0, 1.0, -1.0)
                table_ref[1 + axis, f] = value
        columns_ref[...] = jnp.concatenate(
            [fields[f] for f in range(6)] + [radius, jnp.zeros((72, SLOTS), jnp.float32)], axis=0
        ).T

    def outer_tables(ref, count):
        for axis in range(3):
            for f in range(count):
                value = jnp.where(
                    bits[axis] == 0,
                    swapped(ref[2 * axis, f], axis),
                    swapped(ref[2 * axis + 1, f], axis),
                )
                if f == axis:
                    value = value + jnp.where(bits[axis] == 0, -1.0, 1.0)
                table_ref[4 + axis, f] = value

    zero = jnp.zeros((BINS, SLOTS), jnp.float32)
    for step in range(SUBSTEPS):
        source = own_ref if step == 0 else own_2_ref
        fields = [source[f] for f in range(9)] + [partner_radius]
        inner_tables(fields)
        pair_pass(columns_ref, table_ref, (0, 1, 2, 3), sums_ref, True)

        if step == 0:
            gas_copy.wait()
            for b in range(BINS):
                bx, by, bz = b // 4, b // 2 % 2, b % 2
                size_x, size_y = cells_x // 2, cells_y // 2
                block = gas_ref[
                    :,
                    bx * size_x : (bx + 1) * size_x,
                    by * size_y : (by + 1) * size_y,
                    bz * SLOTS : (bz + 1) * SLOTS,
                ].reshape(3 * SLOTS, SLOTS)
                cell = cells_ref[b : b + 1, :]
                high, low = halves(block)
                left = jnp.concatenate(
                    [high.astype(jnp.bfloat16), low.astype(jnp.bfloat16)], axis=1
                )
                lanes = jnp.where(one_hot(cell & (SLOTS - 1)), 1.0, 0.0).astype(jnp.bfloat16)
                right = jnp.concatenate([lanes, lanes], axis=0)
                product = jnp.dot(left, right, preferred_element_type=jnp.float32)
                rows = one_hot(lax.shift_right_logical(cell, 7))
                for i in range(3):
                    gas_out[i, b : b + 1, :] = jnp.sum(
                        jnp.where(rows, product[i * SLOTS : (i + 1) * SLOTS], 0.0),
                        axis=0,
                        keepdims=True,
                    )

        for d in range(6):

            @pl.when(there[d][1])
            def _():
                (halo_copy if step == 0 else halo_copy_2)(d ^ 1).wait_recv()

        outer_tables(halo_ref if step == 0 else halo_2_ref, 10 if step == 0 else 9)
        pair_pass(columns_ref, table_ref, (4, 5, 6), sums_ref, False)
        normal = sums_ref[...].T

        places, speeds, turning = fields[0:3], fields[3:6], fields[6:9]
        spring_source = springs_ref if step == 0 else springs_out
        shear_sum = [zero] * 3
        torque_sum = [zero] * 3
        for k in range(HIST):
            other = gathered(
                table_ref, range(7), which[k], masks_of(k), member[k], [zero] * 10
            )
            sep = [places[i] - other[i] for i in range(3)]
            square = dot(sep, sep) + soft_length**2
            inverse = lax.rsqrt(square)
            unit = [sep[i] * inverse for i in range(3)]
            overlap = radius + other[9] - square * inverse
            delta = jnp.maximum(overlap, 0.0)
            root = delta * lax.rsqrt(jnp.maximum(overlap, TINY))
            relative = [speeds[i] - other[3 + i] for i in range(3)]
            approach = dot(relative, unit)
            pressing = root * (normal_stiff * delta - normal_damp * approach)
            lever = [radius * turning[i] + other[9] * other[6 + i] for i in range(3)]
            spun = cross(lever, unit)
            contact = [relative[i] - spun[i] for i in range(3)]
            along = dot(contact, unit)
            sliding = [contact[i] - along * unit[i] for i in range(3)]
            spring = [spring_source[i * HIST + k] for i in range(3)]
            tilt = dot(spring, unit)
            stretched = [
                spring[i] - tilt * unit[i] + time_step * sliding[i] for i in range(3)
            ]
            length = jnp.sqrt(dot(stretched, stretched))
            limit = jnp.minimum(
                1.0, friction * jnp.abs(pressing) / jnp.maximum(shear_stiff * length, force_floor)
            )
            scale = valid[k] * limit
            fresh = [scale * stretched[i] for i in range(3)]
            shear = [-shear_stiff * fresh[i] for i in range(3)]
            twist = cross(shear, unit)
            for i in range(3):
                springs_out[i * HIST + k] = fresh[i]
            shear_sum = [shear_sum[i] + shear[i] for i in range(3)]
            torque_sum = [torque_sum[i] + twist[i] for i in range(3)]

        for i in range(3):
            push = normal_damp * normal[i * 8 : i * 8 + 8, :] + shear_sum[i]
            push = push + drag_coeff * (gas_out[i] - speeds[i])
            speed = speeds[i] + time_step * (push / mass - (gravity if i == 2 else 0.0))
            spin = turning[i] + time_step * (radius * torque_sum[i]) / inertia
            target = own_2_ref if step == 0 else state_out
            target[3 + i] = speed
            target[6 + i] = spin
            target[i] = places[i] + time_step * speed
        if step == 0:
            for d in range(6):

                @pl.when(there[d][1])
                def _():
                    halo_copy_2(d).start()

    for f in range(9):
        picked_ref[:, f, :] = state_out[f]
    picked_ref[:, 9, :] = radius
    for f in range(3 * HIST):
        picked_ref[:, 10 + f, :] = springs_out[f]
    for k in range(HIST):
        picked_ref[:, 22 + k, :] = (code[k] + 1).astype(jnp.float32)
    for f in range(26, 32):
        picked_ref[:, f, :] = zero
    for d in range(6):
        entry = jnp.broadcast_to(departures_ref[d : d + 1, :], (8, SLOTS))
        slot = entry & (SLOTS - 1)
        home = lax.shift_right_arithmetic(entry, 7)
        for g in range(4):
            value = zero
            for b in range(BINS):
                taken = jnp.take_along_axis(
                    picked_ref[b, g * 8 : g * 8 + 8, :], slot, axis=1, mode="promise_in_bounds"
                )
                value = jnp.where(home == b, taken, value)
            gone_ref[d, g * 8 : g * 8 + 8, :] = value

        @pl.when(there[d][1])
        def _():
            moved_copy(d).start()

    for d in range(6):

        @pl.when(there[d][1])
        def _():
            halo_copy(d).wait_send()
            halo_copy_2(d).wait_send()
            face_copy(d).wait_send()
            face_copy(d ^ 1).wait_recv()

    face_x_out[...] = face_x_ref[...]
    face_y_out[...] = face_y_ref[...]
    face_z_out[...] = face_z_ref[...]

    for d in range(6):

        @pl.when(there[d][1])
        def _():
            moved_copy(d).wait_send()
            moved_copy(d ^ 1).wait_recv()

    moved_out[...] = come_ref[...]


def finish(
    state_ref,
    springs_ref,
    gas_ref,
    radii_ref,
    counts_ref,
    cells_ref,
    moved_ref,
    pressure_ref,
    source_ref,
    face_x_ref,
    face_y_ref,
    face_z_ref,
    pos_out,
    vel_out,
    spin_out,
    springs_out,
    force_out,
    pressure_out,
    arrived_out,
    codes_out,
):
    for i in range(3):
        pos_out[i] = state_ref[i]
        vel_out[i] = state_ref[3 + i]
        spin_out[i] = state_ref[6 + i]
    springs_out[...] = springs_ref[...]
    for d in range(6):
        arrived_out[:, d, :] = moved_ref[d, 0:22, :]
        codes_out[:, d, :] = moved_ref[d, 22:26, :].astype(jnp.int32) - 1

    cells_x, cells_y, cells_z = pressure_ref.shape
    row = lax.broadcasted_iota(jnp.int32, (cells_y, cells_z), 0)
    lane = lax.broadcasted_iota(jnp.int32, (cells_y, cells_z), 1)
    for x in range(cells_x):
        here = pressure_ref[x]
        total = pressure_ref[x - 1] if x > 0 else face_x_ref[0]
        total = total + (pressure_ref[x + 1] if x < cells_x - 1 else face_x_ref[1])
        total = total + jnp.where(row == 0, face_y_ref[0, x : x + 1, :], pltpu.roll(here, 1, 0))
        total = total + jnp.where(
            row == cells_y - 1, face_y_ref[1, x : x + 1, :], pltpu.roll(here, cells_y - 1, 0)
        )
        total = total + jnp.where(
            lane == 0,
            jnp.broadcast_to(face_z_ref[0][:, x : x + 1], here.shape),
            pltpu.roll(here, 1, 1),
        )
        total = total + jnp.where(
            lane == cells_z - 1,
            jnp.broadcast_to(face_z_ref[1][:, x : x + 1], here.shape),
            pltpu.roll(here, cells_z - 1, 1),
        )
        pressure_out[x] = total + source_ref[x]

    live = jnp.where(live_mask(counts_ref), 1.0, 0.0)
    radius = radii_ref[...]
    values = [drag_coeff * (state_ref[3 + i] - gas_ref[i]) * live for i in range(3)]
    values.append(4.0 / 3.0 * math.pi * (radius * radius * radius) * live)
    values = [halves(value) for value in values]
    size_x, size_y = cells_x // 2, cells_y // 2
    for b in range(BINS):
        bx, by, bz = b // 4, b // 2 % 2, b % 2
        block = (
            slice(bx * size_x, (bx + 1) * size_x),
            slice(by * size_y, (by + 1) * size_y),
            slice(bz * SLOTS, (bz + 1) * SLOTS),
        )
        cell = cells_ref[b : b + 1, :]
        rows = one_hot(lax.shift_right_logical(cell, 7))
        lanes = jnp.where(one_hot(cell & (SLOTS - 1)), 1.0, 0.0).astype(jnp.bfloat16)
        right = jnp.concatenate([lanes, lanes], axis=1)
        left = jnp.concatenate(
            [
                jnp.concatenate(
                    [
                        jnp.where(rows, part[b : b + 1, :], 0.0).astype(jnp.bfloat16)
                        for part in value
                    ],
                    axis=1,
                )
                for value in values
            ],
            axis=0,
        )
        product = lax.dot_general(
            left, right, (((1,), (1,)), ((), ())), preferred_element_type=jnp.float32
        )
        parts = [
            product[i * SLOTS : (i + 1) * SLOTS].reshape(size_x, size_y, SLOTS) for i in range(4)
        ]
        for i in range(3):
            force_out[(i,) + block] = parts[i]
        pressure_out[block] = (
            pressure_out[block] + volume_coeff * parts[3] + drag_weight * parts[2]
        ) / 6.0


def body(
    positions,
    velocities,
    spins,
    radii,
    counts,
    springs,
    partners,
    cells,
    departures,
    fluid_velocity,
    pressure,
    pressure_source,
):
    cells_x, cells_y, cells_z = pressure.shape
    f32 = jnp.float32
    vmem = pl.BlockSpec(memory_space=pltpu.VMEM)
    smem = pl.BlockSpec(memory_space=pltpu.SMEM)
    anywhere = pl.BlockSpec(memory_space=pl.ANY)
    shape = jax.ShapeDtypeStruct
    rows = (BINS, SLOTS)
    radii_rows = radii.reshape(rows)
    cells_rows = cells.reshape(rows)
    counts_row = counts.reshape(BINS)
    state, new_springs, gas, moved, face_x, face_y, face_z = pl.pallas_call(
        particles,
        out_shape=(
            shape((9,) + rows, f32),
            shape((3 * HIST,) + rows, f32),
            shape((3,) + rows, f32),
            shape((6, 32, SLOTS), f32),
            shape((2, cells_y, cells_z), f32),
            shape((2, cells_x, cells_z), f32),
            shape((2, cells_y, SLOTS), f32),
        ),
        in_specs=[vmem] * 4 + [smem] + [vmem] * 4 + [anywhere] * 2,
        out_specs=(vmem,) * 7,
        scratch_shapes=[
            pltpu.VMEM(fluid_velocity.shape, f32),
            pltpu.VMEM(pressure.shape, f32),
            pltpu.VMEM((7, 10) + rows, f32),
            pltpu.VMEM((SLOTS, SLOTS), f32),
            pltpu.VMEM((SLOTS, SLOTS), f32),
            pltpu.VMEM((10,) + rows, f32),
            pltpu.VMEM((6, 10) + rows, f32),
            pltpu.VMEM((9,) + rows, f32),
            pltpu.VMEM((6, 9) + rows, f32),
            pltpu.VMEM((BINS, 32, SLOTS), f32),
            pltpu.VMEM((6, 32, SLOTS), f32),
            pltpu.VMEM((6, 32, SLOTS), f32),
            pltpu.VMEM((2, cells_x, cells_z), f32),
            pltpu.VMEM((2, cells_y, SLOTS), f32),
            pltpu.VMEM((2, cells_y, cells_z), f32),
            pltpu.VMEM((2, cells_x, cells_z), f32),
            pltpu.VMEM((2, cells_y, SLOTS), f32),
            pltpu.SemaphoreType.DMA((2,)),
            pltpu.SemaphoreType.DMA((4, 6)),
            pltpu.SemaphoreType.DMA((4, 6)),
        ],
        compiler_params=pltpu.CompilerParams(
            collective_id=0, has_side_effects=True, vmem_limit_bytes=32 * 1024 * 1024
        ),
    )(
        positions.reshape((3,) + rows),
        velocities.reshape((3,) + rows),
        spins.reshape((3,) + rows),
        radii_rows,
        counts_row,
        springs.reshape((3 * HIST,) + rows),
        partners.reshape((HIST,) + rows),
        cells_rows,
        departures.reshape(6, SLOTS),
        fluid_velocity,
        pressure,
    )
    places, speeds, turning, last_springs, force, new_pressure, arrived, codes = pl.pallas_call(
        finish,
        out_shape=(
            shape((3,) + rows, f32),
            shape((3,) + rows, f32),
            shape((3,) + rows, f32),
            shape((3 * HIST,) + rows, f32),
            shape(fluid_velocity.shape, f32),
            shape(pressure.shape, f32),
            shape((22, 6, SLOTS), f32),
            shape((4, 6, SLOTS), jnp.int32),
        ),
        in_specs=[vmem] * 4 + [smem] + [vmem] * 7,
        out_specs=(vmem,) * 8,
        compiler_params=pltpu.CompilerParams(vmem_limit_bytes=32 * 1024 * 1024),
    )(
        state,
        new_springs,
        gas,
        radii_rows,
        counts_row,
        cells_rows,
        moved,
        pressure,
        pressure_source,
        face_x,
        face_y,
        face_z,
    )
    return (
        places.reshape(positions.shape),
        speeds.reshape(positions.shape),
        turning.reshape(positions.shape),
        last_springs.reshape(springs.shape),
        force,
        new_pressure,
        arrived[None, None, None],
        codes[None, None, None],
    )


def solution(mesh):
    return jax.shard_map(
        body,
        mesh=mesh,
        in_specs=(
            P(None, "gx", "gy", "gz", None),
            P(None, "gx", "gy", "gz", None),
            P(None, "gx", "gy", "gz", None),
            P("gx", "gy", "gz", None),
            P("gx", "gy", "gz"),
            P(None, None, "gx", "gy", "gz", None),
            P(None, "gx", "gy", "gz", None),
            P("gx", "gy", "gz", None),
            P("gx", "gy", "gz", None, None),
            P(None, "gx", "gy", "gz"),
            P("gx", "gy", "gz"),
            P("gx", "gy", "gz"),
        ),
        out_specs=(
            P(None, "gx", "gy", "gz", None),
            P(None, "gx", "gy", "gz", None),
            P(None, "gx", "gy", "gz", None),
            P(None, None, "gx", "gy", "gz", None),
            P(None, "gx", "gy", "gz"),
            P("gx", "gy", "gz"),
            P("gx", "gy", "gz", None, None, None),
            P("gx", "gy", "gz", None, None, None),
        ),
        check_vma=False,
    )
```

```python
import functools
import math

import jax
import jax.numpy as jnp
from jax import lax
from jax.experimental import pallas as pl
from jax.experimental.pallas import tpu as pltpu
from jax.sharding import PartitionSpec as P

SUBSTEPS = 2
HIST = 4
BINS = 8
SLOTS = 128
VMEM_LIMIT = 64 * 1024 * 1024

normal_stiff = 100.0
normal_damp = 2.0
shear_stiff = 30.0
friction = 0.5
time_step = 0.05
drag_coeff = 0.8
gravity = 1.0
soft_length = 0.05
force_floor = 0.5
volume_coeff = 100.0
drag_weight = 1.0

NOBODY = -10.0
TINY = 1e-30
AXES = ("gx", "gy", "gz")
MESH = pl.DeviceIdType.MESH


def neighbour(direction):
    axis = AXES[direction // 2]
    size = lax.axis_size(axis)
    here = lax.axis_index(axis)
    if direction % 2 == 0:
        return {axis: lax.rem(here + size - 1, size)}, here > 0
    return {axis: lax.rem(here + 1, size)}, here < size - 1


def bin_bits():
    row = lax.broadcasted_iota(jnp.int32, (BINS, SLOTS), 0)
    return [lax.shift_right_logical(row, 2 - axis) & 1 for axis in range(3)]


def swapped(value, axis):
    step = 4 >> axis
    if axis == 0:
        return pltpu.roll(value, step, 0)
    upper = bin_bits()[axis] == 1
    return jnp.where(upper, pltpu.roll(value, step, 0), pltpu.roll(value, BINS - step, 0))


def live_mask(counts_ref):
    row = lax.broadcasted_iota(jnp.int32, (BINS, SLOTS), 0)
    slot = lax.broadcasted_iota(jnp.int32, (BINS, SLOTS), 1)
    limit = jnp.zeros((BINS, SLOTS), jnp.int32)
    for b in range(BINS):
        limit = jnp.where(row == b, counts_ref[b // 4, b // 2 % 2, b % 2], limit)
    return slot < limit


def halves(value):
    high = value.astype(jnp.bfloat16).astype(jnp.float32)
    return high, value - high


def one_hot(index_row):
    rows = lax.broadcasted_iota(jnp.int32, (SLOTS, SLOTS), 0)
    return rows == index_row


def cross(a, b):
    return [
        a[1] * b[2] - a[2] * b[1],
        a[2] * b[0] - a[0] * b[2],
        a[0] * b[1] - a[1] * b[0],
    ]


def dot(a, b):
    return a[0] * b[0] + a[1] * b[1] + a[2] * b[2]


def pair_pass(columns_ref, mine_ref, table_ref, tables, sums_ref, first):
    def chunk(c, carry):
        start = pl.multiple_of(c * 8, 8)
        rows = pl.ds(start, 8)
        tile = columns_ref[rows, :] if first else None
        for b in range(BINS):
            if first:
                mine = [
                    jnp.broadcast_to(tile[:, f * 8 + b : f * 8 + b + 1], (8, SLOTS))
                    for f in range(7)
                ]
                for f in range(7):
                    mine_ref[f, b, rows, :] = mine[f]
                total = None
            else:
                mine = [mine_ref[f, b, rows, :] for f in range(7)]
                total = [sums_ref[i, b, rows, :] for i in range(3)]
            for t in tables:
                other = [
                    jnp.broadcast_to(table_ref[t, f, b : b + 1, :], (8, SLOTS))
                    for f in (0, 1, 2, 3, 4, 5, 9)
                ]
                sep = [mine[i] - other[i] for i in range(3)]
                square = dot(sep, sep) + soft_length**2
                inverse = lax.rsqrt(square)
                overlap = mine[6] + other[6] - square * inverse
                delta = jnp.maximum(overlap, 0.0)
                root = delta * lax.rsqrt(jnp.maximum(overlap, TINY))
                vrel = [mine[3 + i] - other[3 + i] for i in range(3)]
                approach = dot(vrel, sep) * inverse
                weight = ((normal_stiff / normal_damp) * delta - approach) * (root * inverse)
                term = [weight * sep[i] for i in range(3)]
                total = term if total is None else [total[i] + term[i] for i in range(3)]
            for i in range(3):
                sums_ref[i, b, rows, :] = total[i]
        return carry

    lax.fori_loop(0, SLOTS // 8, chunk, 0)


def lane_sums(sums_ref, i):
    row = lax.broadcasted_iota(jnp.int32, (BINS, 2 * SLOTS), 0)
    total = jnp.zeros((BINS, SLOTS), jnp.float32)
    for b in range(BINS):
        high, low = halves(sums_ref[i, b])
        right = jnp.concatenate([high.astype(jnp.bfloat16), low.astype(jnp.bfloat16)], axis=1)
        left = jnp.where(row == b, 1.0, 0.0).astype(jnp.bfloat16)
        total = total + lax.dot_general(
            left, right, (((1,), (1,)), ((), ())), preferred_element_type=jnp.float32
        )
    return total


def gathered(table_ref, tables, which, masks, member, got):
    for f in range(10):
        value = got[f]
        for t in tables:
            picked = jnp.take_along_axis(
                table_ref[t, f], member, axis=1, mode="promise_in_bounds"
            )
            value = jnp.where(masks[t], picked, value)
        got[f] = value
    return got


def particles(
    counts_ref,
    pos_hbm,
    vel_hbm,
    spin_hbm,
    radii_hbm,
    springs_hbm,
    partners_hbm,
    cells_hbm,
    departures_hbm,
    gas_hbm,
    pressure_hbm,
    state_hbm,
    new_springs_hbm,
    u_hbm,
    moved_hbm,
    face_x_hbm,
    face_y_hbm,
    face_z_hbm,
    state_out,
    springs_out,
    gas_out,
    pos_ref,
    vel_ref,
    spin_ref,
    radii_ref,
    springs_ref,
    partners_ref,
    cells_ref,
    departures_ref,
    gas_ref,
    pressure_ref,
    table_ref,
    columns_ref,
    mine_ref,
    sums_ref,
    own_ref,
    halo_ref,
    own_2_ref,
    halo_2_ref,
    picked_ref,
    gone_ref,
    come_ref,
    send_y_ref,
    send_z_ref,
    face_x_ref,
    face_y_ref,
    face_z_ref,
    local_sem,
    store_sem,
    send_sem,
    recv_sem,
):
    loads = [
        pltpu.make_async_copy(source, target, local_sem.at[n])
        for n, (source, target) in enumerate(
            (
                (pos_hbm, pos_ref),
                (vel_hbm, vel_ref),
                (spin_hbm, spin_ref),
                (radii_hbm, radii_ref),
                (pressure_hbm, pressure_ref),
                (partners_hbm, partners_ref),
                (springs_hbm, springs_ref),
                (cells_hbm, cells_ref),
                (departures_hbm, departures_ref),
                (gas_hbm, gas_ref),
            )
        )
    ]
    for load in loads:
        load.start()

    there = [neighbour(d) for d in range(6)]

    barrier = pltpu.get_barrier_semaphore()
    for d in range(6):

        @pl.when(there[d][1])
        def _():
            pl.semaphore_signal(barrier, inc=1, device_id=there[d][0], device_id_type=MESH)

    def halo_copy(d):
        return pltpu.make_async_remote_copy(
            src_ref=own_ref,
            dst_ref=halo_ref.at[d ^ 1],
            send_sem=send_sem.at[0, d],
            recv_sem=recv_sem.at[0, d ^ 1],
            device_id=there[d][0],
            device_id_type=MESH,
        )

    def halo_copy_2(d):
        return pltpu.make_async_remote_copy(
            src_ref=own_2_ref,
            dst_ref=halo_2_ref.at[d ^ 1],
            send_sem=send_sem.at[1, d],
            recv_sem=recv_sem.at[1, d ^ 1],
            device_id=there[d][0],
            device_id_type=MESH,
        )

    def moved_copy(d):
        return pltpu.make_async_remote_copy(
            src_ref=gone_ref.at[d],
            dst_ref=come_ref.at[d],
            send_sem=send_sem.at[2, d],
            recv_sem=recv_sem.at[2, d],
            device_id=there[d][0],
            device_id_type=MESH,
        )

    def face_copy(d):
        side = d % 2
        if d < 2:
            source = pressure_ref.at[0 if side == 0 else pressure_ref.shape[0] - 1]
            target = face_x_ref.at[1 - side]
        elif d < 4:
            source, target = send_y_ref.at[side], face_y_ref.at[1 - side]
        else:
            source, target = send_z_ref.at[side], face_z_ref.at[1 - side]
        return pltpu.make_async_remote_copy(
            src_ref=source,
            dst_ref=target,
            send_sem=send_sem.at[3, d],
            recv_sem=recv_sem.at[3, d ^ 1],
            device_id=there[d][0],
            device_id_type=MESH,
        )

    for load in loads[:4]:
        load.wait()
    live = live_mask(counts_ref)
    radius = radii_ref[...]
    partner_radius = jnp.where(live, radius, NOBODY)
    for i in range(3):
        own_ref[i] = pos_ref[i]
        own_ref[3 + i] = vel_ref[i]
        own_ref[6 + i] = spin_ref[i]
    own_ref[9] = partner_radius

    for s in range(6):

        @pl.when(jnp.logical_not(there[s][1]))
        def _():
            halo_ref[s] = jnp.zeros((10, BINS, SLOTS), jnp.float32)
            halo_ref[s, 9] = jnp.full((BINS, SLOTS), NOBODY, jnp.float32)
            halo_2_ref[s] = jnp.zeros((9, BINS, SLOTS), jnp.float32)
            come_ref[s ^ 1] = jnp.zeros((32, SLOTS), jnp.float32)
            face = (face_x_ref, face_y_ref, face_z_ref)[s // 2]
            face[s % 2] = jnp.zeros(face.shape[1:], jnp.float32)

    pl.semaphore_wait(barrier, sum(there[d][1].astype(jnp.int32) for d in range(6)))

    for d in range(6):

        @pl.when(there[d][1])
        def _():
            halo_copy(d).start()

    for load in loads[4:9]:
        load.wait()
    cells_x, cells_y, cells_z = pressure_ref.shape
    lane = lax.broadcasted_iota(jnp.int32, (cells_y, SLOTS), 1)
    for side in range(2):
        send_y_ref[side] = pressure_ref[:, 0 if side == 0 else cells_y - 1, :]
        face = jnp.zeros((cells_y, SLOTS), jnp.float32)
        for x in range(cells_x):
            if side == 0:
                column = pressure_ref[x, :, 0:SLOTS][:, 0:1]
            else:
                column = pressure_ref[x, :, cells_z - SLOTS : cells_z][:, SLOTS - 1 : SLOTS]
            face = jnp.where(lane == x, jnp.broadcast_to(column, (cells_y, SLOTS)), face)
        send_z_ref[side] = face
    for d in range(6):

        @pl.when(there[d][1])
        def _():
            face_copy(d).start()

    bits = bin_bits()
    code = [partners_ref[k] for k in range(HIST)]
    valid = [jnp.where(code[k] >= 0, 1.0, 0.0) for k in range(HIST)]
    member = [jnp.maximum(code[k], 0) & (SLOTS - 1) for k in range(HIST)]
    which = [lax.shift_right_logical(jnp.maximum(code[k], 0), 7) for k in range(HIST)]

    def masks_of(k):
        found = [which[k] == 0]
        for axis in range(3):
            found.append(which[k] == 2 * axis + 2 - bits[axis])
        for axis in range(3):
            found.append(which[k] == 2 * axis + 1 + bits[axis])
        return found

    safe = jnp.where(radius > 0.0, radius, 1.0)
    mass = safe * 10.0
    mass = mass * mass * mass
    inertia = 0.4 * mass * safe * safe

    def inner_tables(fields):
        for f in range(10):
            table_ref[0, f] = fields[f]
            for axis in range(3):
                value = swapped(fields[f], axis)
                if f == axis:
                    value = value + jnp.where(bits[axis] == 0, 1.0, -1.0)
                table_ref[1 + axis, f] = value
        columns_ref[...] = jnp.concatenate(
            [fields[f] for f in range(6)] + [radius, jnp.zeros((72, SLOTS), jnp.float32)], axis=0
        ).T

    def outer_tables(ref, count):
        for axis in range(3):
            for f in range(count):
                value = jnp.where(
                    bits[axis] == 0,
                    swapped(ref[2 * axis, f], axis),
                    swapped(ref[2 * axis + 1, f], axis),
                )
                if f == axis:
                    value = value + jnp.where(bits[axis] == 0, -1.0, 1.0)
                table_ref[4 + axis, f] = value

    zero = jnp.zeros((BINS, SLOTS), jnp.float32)
    for step in range(SUBSTEPS):
        source = own_ref if step == 0 else own_2_ref
        fields = [source[f] for f in range(9)] + [partner_radius]
        inner_tables(fields)
        pair_pass(columns_ref, mine_ref, table_ref, (0, 1, 2, 3), sums_ref, True)

        if step == 0:
            loads[9].wait()
            for b in range(BINS):
                bx, by, bz = b // 4, b // 2 % 2, b % 2
                size_x, size_y = cells_x // 2, cells_y // 2
                block = gas_ref[
                    :,
                    bx * size_x : (bx + 1) * size_x,
                    by * size_y : (by + 1) * size_y,
                    bz * SLOTS : (bz + 1) * SLOTS,
                ].reshape(3 * SLOTS, SLOTS)
                cell = cells_ref[b : b + 1, :]
                high, low = halves(block)
                left = jnp.concatenate(
                    [high.astype(jnp.bfloat16), low.astype(jnp.bfloat16)], axis=1
                )
                lanes = jnp.where(one_hot(cell & (SLOTS - 1)), 1.0, 0.0).astype(jnp.bfloat16)
                right = jnp.concatenate([lanes, lanes], axis=0)
                product = jnp.dot(left, right, preferred_element_type=jnp.float32)
                rows = one_hot(lax.shift_right_logical(cell, 7))
                for i in range(3):
                    gas_out[i, b : b + 1, :] = jnp.sum(
                        jnp.where(rows, product[i * SLOTS : (i + 1) * SLOTS], 0.0),
                        axis=0,
                        keepdims=True,
                    )

        for d in range(6):

            @pl.when(there[d][1])
            def _():
                (halo_copy if step == 0 else halo_copy_2)(d ^ 1).wait_recv()

        outer_tables(halo_ref if step == 0 else halo_2_ref, 10 if step == 0 else 9)
        pair_pass(columns_ref, mine_ref, table_ref, (4, 5, 6), sums_ref, False)
        normal = [lane_sums(sums_ref, i) for i in range(3)]

        places, speeds, turning = fields[0:3], fields[3:6], fields[6:9]
        spring_source = springs_ref if step == 0 else springs_out
        shear_sum = [zero] * 3
        torque_sum = [zero] * 3
        for k in range(HIST):
            other = gathered(
                table_ref, range(7), which[k], masks_of(k), member[k], [zero] * 10
            )
            sep = [places[i] - other[i] for i in range(3)]
            square = dot(sep, sep) + soft_length**2
            inverse = lax.rsqrt(square)
            unit = [sep[i] * inverse for i in range(3)]
            overlap = radius + other[9] - square * inverse
            delta = jnp.maximum(overlap, 0.0)
            root = delta * lax.rsqrt(jnp.maximum(overlap, TINY))
            relative = [speeds[i] - other[3 + i] for i in range(3)]
            approach = dot(relative, unit)
            pressing = root * (normal_stiff * delta - normal_damp * approach)
            lever = [radius * turning[i] + other[9] * other[6 + i] for i in range(3)]
            spun = cross(lever, unit)
            contact = [relative[i] - spun[i] for i in range(3)]
            along = dot(contact, unit)
            sliding = [contact[i] - along * unit[i] for i in range(3)]
            spring = [spring_source[i * HIST + k] for i in range(3)]
            tilt = dot(spring, unit)
            stretched = [
                spring[i] - tilt * unit[i] + time_step * sliding[i] for i in range(3)
            ]
            length = jnp.sqrt(dot(stretched, stretched))
            limit = jnp.minimum(
                1.0, friction * jnp.abs(pressing) / jnp.maximum(shear_stiff * length, force_floor)
            )
            scale = valid[k] * limit
            fresh = [scale * stretched[i] for i in range(3)]
            shear = [-shear_stiff * fresh[i] for i in range(3)]
            twist = cross(shear, unit)
            for i in range(3):
                springs_out[i * HIST + k] = fresh[i]
            shear_sum = [shear_sum[i] + shear[i] for i in range(3)]
            torque_sum = [torque_sum[i] + twist[i] for i in range(3)]

        for i in range(3):
            push = normal_damp * normal[i] + shear_sum[i]
            push = push + drag_coeff * (gas_out[i] - speeds[i])
            speed = speeds[i] + time_step * (push / mass - (gravity if i == 2 else 0.0))
            spin = turning[i] + time_step * (radius * torque_sum[i]) / inertia
            target = own_2_ref if step == 0 else state_out
            target[3 + i] = speed
            target[6 + i] = spin
            target[i] = places[i] + time_step * speed
        if step == 0:
            for d in range(6):

                @pl.when(there[d][1])
                def _():
                    halo_copy_2(d).start()

    stores = [
        pltpu.make_async_copy(source, target, store_sem.at[n])
        for n, (source, target) in enumerate(
            (
                (state_out, state_hbm),
                (springs_out, new_springs_hbm),
                (gas_out, u_hbm),
                (face_x_ref, face_x_hbm),
                (face_y_ref, face_y_hbm),
                (face_z_ref, face_z_hbm),
                (come_ref, moved_hbm),
            )
        )
    ]
    for store in stores[:3]:
        store.start()

    for f in range(9):
        picked_ref[:, f, :] = state_out[f]
    picked_ref[:, 9, :] = radius
    for f in range(3 * HIST):
        picked_ref[:, 10 + f, :] = springs_out[f]
    for k in range(HIST):
        picked_ref[:, 22 + k, :] = (code[k] + 1).astype(jnp.float32)
    for f in range(26, 32):
        picked_ref[:, f, :] = zero
    for d in range(6):
        entry = jnp.broadcast_to(departures_ref[d], (8, SLOTS))
        slot = entry & (SLOTS - 1)
        home = lax.shift_right_arithmetic(entry, 7)
        for g in range(4):
            value = zero
            for b in range(BINS):
                taken = jnp.take_along_axis(
                    picked_ref[b, g * 8 : g * 8 + 8, :], slot, axis=1, mode="promise_in_bounds"
                )
                value = jnp.where(home == b, taken, value)
            gone_ref[d, g * 8 : g * 8 + 8, :] = value

        @pl.when(there[d][1])
        def _():
            moved_copy(d).start()

    for d in range(6):

        @pl.when(there[d][1])
        def _():
            halo_copy(d).wait_send()
            halo_copy_2(d).wait_send()
            face_copy(d).wait_send()
            face_copy(d ^ 1).wait_recv()

    for store in stores[3:6]:
        store.start()

    for d in range(6):

        @pl.when(there[d][1])
        def _():
            moved_copy(d).wait_send()
            moved_copy(d ^ 1).wait_recv()

    stores[6].start()
    for store in stores:
        store.wait()


def finish(
    counts_ref,
    state_hbm,
    springs_hbm,
    gas_hbm,
    radii_hbm,
    cells_hbm,
    moved_hbm,
    pressure_hbm,
    source_hbm,
    face_x_hbm,
    face_y_hbm,
    face_z_hbm,
    pos_out,
    vel_out,
    spin_out,
    springs_out,
    force_out,
    pressure_out,
    arrived_out,
    codes_out,
    speed_ref,
    gas_ref,
    radii_ref,
    cells_ref,
    moved_ref,
    pressure_ref,
    source_ref,
    face_x_ref,
    face_y_ref,
    face_z_ref,
    force_ref,
    result_ref,
    arrived_ref,
    codes_ref,
    load_sem,
    store_sem,
):
    loads = [
        pltpu.make_async_copy(source, target, load_sem.at[n])
        for n, (source, target) in enumerate(
            (
                (state_hbm.at[3:6], speed_ref),
                (gas_hbm, gas_ref),
                (radii_hbm, radii_ref),
                (cells_hbm, cells_ref),
                (pressure_hbm, pressure_ref),
                (source_hbm, source_ref),
                (face_x_hbm, face_x_ref),
                (face_y_hbm, face_y_ref),
                (face_z_hbm, face_z_ref),
                (moved_hbm, moved_ref),
            )
        )
    ]
    for load in loads:
        load.start()
    stores = [
        pltpu.make_async_copy(source, target, store_sem.at[n])
        for n, (source, target) in enumerate(
            (
                (state_hbm.at[0:3], pos_out),
                (state_hbm.at[3:6], vel_out),
                (state_hbm.at[6:9], spin_out),
                (springs_hbm, springs_out),
                (arrived_ref, arrived_out),
                (codes_ref, codes_out),
                (result_ref, pressure_out),
            )
        )
    ]
    stores += [
        pltpu.make_async_copy(
            force_ref.at[:, 8 * n : 8 * n + 8], force_out.at[:, 8 * n : 8 * n + 8], store_sem.at[7 + n]
        )
        for n in range(2)
    ]
    for store in stores[:4]:
        store.start()

    for load in loads[:4]:
        load.wait()
    size_x, size_y = pressure_ref.shape[0] // 2, pressure_ref.shape[1] // 2
    live = jnp.where(live_mask(counts_ref), 1.0, 0.0)
    radius = radii_ref[...]
    values = [drag_coeff * (speed_ref[i] - gas_ref[i]) * live for i in range(3)]
    values.append(4.0 / 3.0 * math.pi * (radius * radius * radius) * live)
    values = [halves(value) for value in values]
    for b in range(BINS):
        bx, by, bz = b // 4, b // 2 % 2, b % 2
        block = (
            slice(bx * size_x, (bx + 1) * size_x),
            slice(by * size_y, (by + 1) * size_y),
            slice(bz * SLOTS, (bz + 1) * SLOTS),
        )
        cell = cells_ref[b : b + 1, :]
        rows = one_hot(lax.shift_right_logical(cell, 7))
        lanes = jnp.where(one_hot(cell & (SLOTS - 1)), 1.0, 0.0).astype(jnp.bfloat16)
        right = jnp.concatenate([lanes, lanes], axis=1)
        left = jnp.concatenate(
            [
                jnp.concatenate(
                    [
                        jnp.where(rows, part[b : b + 1, :], 0.0).astype(jnp.bfloat16)
                        for part in value
                    ],
                    axis=1,
                )
                for value in values
            ],
            axis=0,
        )
        product = lax.dot_general(
            left, right, (((1,), (1,)), ((), ())), preferred_element_type=jnp.float32
        )
        parts = [
            product[i * SLOTS : (i + 1) * SLOTS].reshape(size_x, size_y, SLOTS) for i in range(4)
        ]
        for i in range(3):
            force_ref[(i,) + block] = parts[i]
        result_ref[block] = volume_coeff * parts[3] + drag_weight * parts[2]
        if b % 4 == 3:
            stores[7 + b // 4].start()

    for load in loads[4:]:
        load.wait()
    cells_x, cells_y, cells_z = pressure_ref.shape
    row = lax.broadcasted_iota(jnp.int32, (cells_y, cells_z), 0)
    lane = lax.broadcasted_iota(jnp.int32, (cells_y, cells_z), 1)
    for x in range(cells_x):
        here = pressure_ref[x]
        total = pressure_ref[x - 1] if x > 0 else face_x_ref[0]
        total = total + (pressure_ref[x + 1] if x < cells_x - 1 else face_x_ref[1])
        total = total + jnp.where(row == 0, face_y_ref[0, x : x + 1, :], pltpu.roll(here, 1, 0))
        total = total + jnp.where(
            row == cells_y - 1, face_y_ref[1, x : x + 1, :], pltpu.roll(here, cells_y - 1, 0)
        )
        total = total + jnp.where(
            lane == 0,
            jnp.broadcast_to(face_z_ref[0][:, x : x + 1], here.shape),
            pltpu.roll(here, 1, 1),
        )
        total = total + jnp.where(
            lane == cells_z - 1,
            jnp.broadcast_to(face_z_ref[1][:, x : x + 1], here.shape),
            pltpu.roll(here, cells_z - 1, 1),
        )
        result_ref[x] = (total + source_ref[x] + result_ref[x]) / 6.0

    stores[6].start()

    for d in range(6):
        codes_ref[d] = moved_ref[d, 22:26, :].astype(jnp.int32) - 1
        for f in range(22):
            arrived_ref[f * 6 + d] = moved_ref[d, f : f + 1, :]
    stores[4].start()
    stores[5].start()
    for store in stores:
        store.wait()


def body(
    positions,
    velocities,
    spins,
    radii,
    counts,
    springs,
    partners,
    cells,
    departures,
    fluid_velocity,
    pressure,
    pressure_source,
):
    cells_x, cells_y, cells_z = pressure.shape
    f32 = jnp.float32
    smem = pl.BlockSpec(memory_space=pltpu.SMEM)
    far = pl.BlockSpec(memory_space=pltpu.HBM)
    shape = jax.ShapeDtypeStruct
    rows = (BINS, SLOTS)
    radii_rows = radii.reshape(rows)
    cells_rows = cells.reshape(rows)
    state, new_springs, gas, moved, face_x, face_y, face_z = pl.pallas_call(
        particles,
        out_shape=(
            shape((9,) + rows, f32),
            shape((3 * HIST,) + rows, f32),
            shape((3,) + rows, f32),
            shape((6, 32, SLOTS), f32),
            shape((2, cells_y, cells_z), f32),
            shape((2, cells_x, cells_z), f32),
            shape((2, cells_y, SLOTS), f32),
        ),
        in_specs=[smem] + [far] * 10,
        out_specs=(far,) * 7,
        scratch_shapes=[
            pltpu.VMEM((9,) + rows, f32),
            pltpu.VMEM((3 * HIST,) + rows, f32),
            pltpu.VMEM((3,) + rows, f32),
            pltpu.VMEM((3,) + rows, f32),
            pltpu.VMEM((3,) + rows, f32),
            pltpu.VMEM((3,) + rows, f32),
            pltpu.VMEM(rows, f32),
            pltpu.VMEM((3 * HIST,) + rows, f32),
            pltpu.VMEM((HIST,) + rows, jnp.int32),
            pltpu.VMEM(rows, jnp.int32),
            pltpu.VMEM((6, 1, SLOTS), jnp.int32),
            pltpu.VMEM(fluid_velocity.shape, f32),
            pltpu.VMEM(pressure.shape, f32),
            pltpu.VMEM((7, 10) + rows, f32),
            pltpu.VMEM((SLOTS, SLOTS), f32),
            pltpu.VMEM((7, BINS, SLOTS, SLOTS), f32),
            pltpu.VMEM((3, BINS, SLOTS, SLOTS), f32),
            pltpu.VMEM((10,) + rows, f32),
            pltpu.VMEM((6, 10) + rows, f32),
            pltpu.VMEM((9,) + rows, f32),
            pltpu.VMEM((6, 9) + rows, f32),
            pltpu.VMEM((BINS, 32, SLOTS), f32),
            pltpu.VMEM((6, 32, SLOTS), f32),
            pltpu.VMEM((6, 32, SLOTS), f32),
            pltpu.VMEM((2, cells_x, cells_z), f32),
            pltpu.VMEM((2, cells_y, SLOTS), f32),
            pltpu.VMEM((2, cells_y, cells_z), f32),
            pltpu.VMEM((2, cells_x, cells_z), f32),
            pltpu.VMEM((2, cells_y, SLOTS), f32),
            pltpu.SemaphoreType.DMA((10,)),
            pltpu.SemaphoreType.DMA((7,)),
            pltpu.SemaphoreType.DMA((4, 6)),
            pltpu.SemaphoreType.DMA((4, 6)),
        ],
        compiler_params=pltpu.CompilerParams(
            collective_id=0, has_side_effects=True, vmem_limit_bytes=VMEM_LIMIT
        ),
    )(
        counts,
        positions.reshape((3,) + rows),
        velocities.reshape((3,) + rows),
        spins.reshape((3,) + rows),
        radii_rows,
        springs.reshape((3 * HIST,) + rows),
        partners.reshape((HIST,) + rows),
        cells_rows,
        departures.reshape(6, 1, SLOTS),
        fluid_velocity,
        pressure,
    )
    places, speeds, turning, last_springs, force, new_pressure, arrived, codes = pl.pallas_call(
        finish,
        out_shape=(
            shape((3,) + rows, f32),
            shape((3,) + rows, f32),
            shape((3,) + rows, f32),
            shape((3 * HIST,) + rows, f32),
            shape(fluid_velocity.shape, f32),
            shape(pressure.shape, f32),
            shape((132, 1, SLOTS), f32),
            shape((6, 4, SLOTS), jnp.int32),
        ),
        in_specs=[smem] + [far] * 11,
        out_specs=(far,) * 8,
        scratch_shapes=[
            pltpu.VMEM((3,) + rows, f32),
            pltpu.VMEM((3,) + rows, f32),
            pltpu.VMEM(rows, f32),
            pltpu.VMEM(rows, jnp.int32),
            pltpu.VMEM((6, 32, SLOTS), f32),
            pltpu.VMEM(pressure.shape, f32),
            pltpu.VMEM(pressure.shape, f32),
            pltpu.VMEM((2, cells_y, cells_z), f32),
            pltpu.VMEM((2, cells_x, cells_z), f32),
            pltpu.VMEM((2, cells_y, SLOTS), f32),
            pltpu.VMEM(fluid_velocity.shape, f32),
            pltpu.VMEM(pressure.shape, f32),
            pltpu.VMEM((132, 1, SLOTS), f32),
            pltpu.VMEM((6, 4, SLOTS), jnp.int32),
            pltpu.SemaphoreType.DMA((10,)),
            pltpu.SemaphoreType.DMA((9,)),
        ],
        compiler_params=pltpu.CompilerParams(vmem_limit_bytes=VMEM_LIMIT),
    )(
        counts,
        state,
        new_springs,
        gas,
        radii_rows,
        cells_rows,
        moved,
        pressure,
        pressure_source,
        face_x,
        face_y,
        face_z,
    )
    return (
        places.reshape(positions.shape),
        speeds.reshape(positions.shape),
        turning.reshape(positions.shape),
        last_springs.reshape(springs.shape),
        force,
        new_pressure,
        arrived.reshape(1, 1, 1, 22, 6, SLOTS),
        jnp.swapaxes(codes, 0, 1)[None, None, None],
    )


def solution(mesh):
    return jax.shard_map(
        body,
        mesh=mesh,
        in_specs=(
            P(None, "gx", "gy", "gz", None),
            P(None, "gx", "gy", "gz", None),
            P(None, "gx", "gy", "gz", None),
            P("gx", "gy", "gz", None),
            P("gx", "gy", "gz"),
            P(None, None, "gx", "gy", "gz", None),
            P(None, "gx", "gy", "gz", None),
            P("gx", "gy", "gz", None),
            P("gx", "gy", "gz", None, None),
            P(None, "gx", "gy", "gz"),
            P("gx", "gy", "gz"),
            P("gx", "gy", "gz"),
        ),
        out_specs=(
            P(None, "gx", "gy", "gz", None),
            P(None, "gx", "gy", "gz", None),
            P(None, "gx", "gy", "gz", None),
            P(None, None, "gx", "gy", "gz", None),
            P(None, "gx", "gy", "gz"),
            P("gx", "gy", "gz"),
            P("gx", "gy", "gz", None, None, None),
            P("gx", "gy", "gz", None, None, None),
        ),
        check_vma=False,
    )
```

```python
import functools
import math

import jax
import jax.numpy as jnp
from jax import lax
from jax.experimental import pallas as pl
from jax.experimental.pallas import tpu as pltpu
from jax.sharding import PartitionSpec as P

SUBSTEPS = 2
HIST = 4
BINS = 8
SLOTS = 128
VMEM_LIMIT = 64 * 1024 * 1024

normal_stiff = 100.0
normal_damp = 2.0
shear_stiff = 30.0
friction = 0.5
time_step = 0.05
drag_coeff = 0.8
gravity = 1.0
soft_length = 0.05
force_floor = 0.5
volume_coeff = 100.0
drag_weight = 1.0

NOBODY = -10.0
TINY = 1e-30
AXES = ("gx", "gy", "gz")
MESH = pl.DeviceIdType.MESH


def neighbour(direction):
    axis = AXES[direction // 2]
    size = lax.axis_size(axis)
    here = lax.axis_index(axis)
    if direction % 2 == 0:
        return {axis: lax.rem(here + size - 1, size)}, here > 0
    return {axis: lax.rem(here + 1, size)}, here < size - 1


def bin_bits():
    row = lax.broadcasted_iota(jnp.int32, (BINS, SLOTS), 0)
    return [lax.shift_right_logical(row, 2 - axis) & 1 for axis in range(3)]


def swapped(value, axis):
    step = 4 >> axis
    if axis == 0:
        return pltpu.roll(value, step, 0)
    upper = bin_bits()[axis] == 1
    return jnp.where(upper, pltpu.roll(value, step, 0), pltpu.roll(value, BINS - step, 0))


def live_mask(counts_ref):
    row = lax.broadcasted_iota(jnp.int32, (BINS, SLOTS), 0)
    slot = lax.broadcasted_iota(jnp.int32, (BINS, SLOTS), 1)
    limit = jnp.zeros((BINS, SLOTS), jnp.int32)
    for b in range(BINS):
        limit = jnp.where(row == b, counts_ref[b // 4, b // 2 % 2, b % 2], limit)
    return slot < limit


def halves(value):
    high = value.astype(jnp.bfloat16).astype(jnp.float32)
    return high, value - high


def one_hot(index_row):
    rows = lax.broadcasted_iota(jnp.int32, (SLOTS, SLOTS), 0)
    return rows == index_row


def cross(a, b):
    return [
        a[1] * b[2] - a[2] * b[1],
        a[2] * b[0] - a[0] * b[2],
        a[0] * b[1] - a[1] * b[0],
    ]


def dot(a, b):
    return a[0] * b[0] + a[1] * b[1] + a[2] * b[2]


def pair_pass(columns_ref, mine_ref, table_ref, tables, sums_ref, first):
    def chunk(c, carry):
        start = pl.multiple_of(c * 8, 8)
        rows = pl.ds(start, 8)
        tile = columns_ref[rows, :] if first else None
        for b in range(BINS):
            if first:
                mine = [
                    jnp.broadcast_to(tile[:, f * 8 + b : f * 8 + b + 1], (8, SLOTS))
                    for f in range(7)
                ]
                for f in range(7):
                    mine_ref[f, b, rows, :] = mine[f]
                total = None
            else:
                mine = [mine_ref[f, b, rows, :] for f in range(7)]
                total = [sums_ref[i, b, rows, :] for i in range(3)]
            for t in tables:
                other = [
                    jnp.broadcast_to(table_ref[t, f, b : b + 1, :], (8, SLOTS))
                    for f in (0, 1, 2, 3, 4, 5, 9)
                ]
                sep = [mine[i] - other[i] for i in range(3)]
                square = dot(sep, sep) + soft_length**2
                inverse = lax.rsqrt(square)
                overlap = mine[6] + other[6] - square * inverse
                delta = jnp.maximum(overlap, 0.0)
                root = delta * lax.rsqrt(jnp.maximum(overlap, TINY))
                vrel = [mine[3 + i] - other[3 + i] for i in range(3)]
                approach = dot(vrel, sep) * inverse
                weight = ((normal_stiff / normal_damp) * delta - approach) * (root * inverse)
                term = [weight * sep[i] for i in range(3)]
                total = term if total is None else [total[i] + term[i] for i in range(3)]
            for i in range(3):
                sums_ref[i, b, rows, :] = total[i]
        return carry

    lax.fori_loop(0, SLOTS // 8, chunk, 0)


def lane_sums(sums_ref, i):
    row = lax.broadcasted_iota(jnp.int32, (BINS, 2 * SLOTS), 0)
    total = jnp.zeros((BINS, SLOTS), jnp.float32)
    for b in range(BINS):
        high, low = halves(sums_ref[i, b])
        right = jnp.concatenate([high.astype(jnp.bfloat16), low.astype(jnp.bfloat16)], axis=1)
        left = jnp.where(row == b, 1.0, 0.0).astype(jnp.bfloat16)
        total = total + lax.dot_general(
            left, right, (((1,), (1,)), ((), ())), preferred_element_type=jnp.float32
        )
    return total


def gathered(table_ref, tables, which, masks, member, got):
    for f in range(10):
        value = got[f]
        for t in tables:
            picked = jnp.take_along_axis(
                table_ref[t, f], member, axis=1, mode="promise_in_bounds"
            )
            value = jnp.where(masks[t], picked, value)
        got[f] = value
    return got


def particles(
    counts_ref,
    pos_hbm,
    vel_hbm,
    spin_hbm,
    radii_hbm,
    springs_hbm,
    partners_hbm,
    cells_hbm,
    departures_hbm,
    gas_hbm,
    pressure_hbm,
    source_hbm,
    places_out,
    speeds_out,
    turning_out,
    new_springs_out,
    force_out,
    result_out,
    arrived_out,
    codes_out,
    state_out,
    springs_out,
    gas_out,
    pos_ref,
    vel_ref,
    spin_ref,
    radii_ref,
    springs_ref,
    partners_ref,
    cells_ref,
    departures_ref,
    gas_ref,
    pressure_ref,
    source_ref,
    force_ref,
    result_ref,
    arrived_ref,
    codes_ref,
    table_ref,
    columns_ref,
    mine_ref,
    sums_ref,
    own_ref,
    halo_ref,
    own_2_ref,
    halo_2_ref,
    picked_ref,
    gone_ref,
    come_ref,
    send_y_ref,
    send_z_ref,
    face_x_ref,
    face_y_ref,
    face_z_ref,
    local_sem,
    store_sem,
    send_sem,
    recv_sem,
):
    loads = [
        pltpu.make_async_copy(source, target, local_sem.at[n])
        for n, (source, target) in enumerate(
            (
                (pos_hbm, pos_ref),
                (vel_hbm, vel_ref),
                (spin_hbm, spin_ref),
                (radii_hbm, radii_ref),
                (pressure_hbm, pressure_ref),
                (partners_hbm, partners_ref),
                (springs_hbm, springs_ref),
                (cells_hbm, cells_ref),
                (departures_hbm, departures_ref),
                (gas_hbm, gas_ref),
                (source_hbm, source_ref),
            )
        )
    ]
    for load in loads:
        load.start()

    there = [neighbour(d) for d in range(6)]

    barrier = pltpu.get_barrier_semaphore()
    for d in range(6):

        @pl.when(there[d][1])
        def _():
            pl.semaphore_signal(barrier, inc=1, device_id=there[d][0], device_id_type=MESH)

    def halo_copy(d):
        return pltpu.make_async_remote_copy(
            src_ref=own_ref,
            dst_ref=halo_ref.at[d ^ 1],
            send_sem=send_sem.at[0, d],
            recv_sem=recv_sem.at[0, d ^ 1],
            device_id=there[d][0],
            device_id_type=MESH,
        )

    def halo_copy_2(d):
        return pltpu.make_async_remote_copy(
            src_ref=own_2_ref,
            dst_ref=halo_2_ref.at[d ^ 1],
            send_sem=send_sem.at[1, d],
            recv_sem=recv_sem.at[1, d ^ 1],
            device_id=there[d][0],
            device_id_type=MESH,
        )

    def moved_copy(d):
        return pltpu.make_async_remote_copy(
            src_ref=gone_ref.at[d],
            dst_ref=come_ref.at[d],
            send_sem=send_sem.at[2, d],
            recv_sem=recv_sem.at[2, d],
            device_id=there[d][0],
            device_id_type=MESH,
        )

    def face_copy(d):
        side = d % 2
        if d < 2:
            source = pressure_ref.at[0 if side == 0 else pressure_ref.shape[0] - 1]
            target = face_x_ref.at[1 - side]
        elif d < 4:
            source, target = send_y_ref.at[side], face_y_ref.at[1 - side]
        else:
            source, target = send_z_ref.at[side], face_z_ref.at[1 - side]
        return pltpu.make_async_remote_copy(
            src_ref=source,
            dst_ref=target,
            send_sem=send_sem.at[3, d],
            recv_sem=recv_sem.at[3, d ^ 1],
            device_id=there[d][0],
            device_id_type=MESH,
        )

    for load in loads[:4]:
        load.wait()
    live = live_mask(counts_ref)
    radius = radii_ref[...]
    partner_radius = jnp.where(live, radius, NOBODY)
    for i in range(3):
        own_ref[i] = pos_ref[i]
        own_ref[3 + i] = vel_ref[i]
        own_ref[6 + i] = spin_ref[i]
    own_ref[9] = partner_radius

    for s in range(6):

        @pl.when(jnp.logical_not(there[s][1]))
        def _():
            halo_ref[s] = jnp.zeros((10, BINS, SLOTS), jnp.float32)
            halo_ref[s, 9] = jnp.full((BINS, SLOTS), NOBODY, jnp.float32)
            halo_2_ref[s] = jnp.zeros((9, BINS, SLOTS), jnp.float32)
            come_ref[s ^ 1] = jnp.zeros((32, SLOTS), jnp.float32)
            face = (face_x_ref, face_y_ref, face_z_ref)[s // 2]
            face[s % 2] = jnp.zeros(face.shape[1:], jnp.float32)

    for load in loads[4:9]:
        load.wait()
    cells_x, cells_y, cells_z = pressure_ref.shape
    lane = lax.broadcasted_iota(jnp.int32, (cells_y, SLOTS), 1)
    for side in range(2):
        send_y_ref[side] = pressure_ref[:, 0 if side == 0 else cells_y - 1, :]
        face = jnp.zeros((cells_y, SLOTS), jnp.float32)
        for x in range(cells_x):
            if side == 0:
                column = pressure_ref[x, :, 0:SLOTS][:, 0:1]
            else:
                column = pressure_ref[x, :, cells_z - SLOTS : cells_z][:, SLOTS - 1 : SLOTS]
            face = jnp.where(lane == x, jnp.broadcast_to(column, (cells_y, SLOTS)), face)
        send_z_ref[side] = face
    bits = bin_bits()
    code = [partners_ref[k] for k in range(HIST)]
    valid = [jnp.where(code[k] >= 0, 1.0, 0.0) for k in range(HIST)]
    member = [jnp.maximum(code[k], 0) & (SLOTS - 1) for k in range(HIST)]
    which = [lax.shift_right_logical(jnp.maximum(code[k], 0), 7) for k in range(HIST)]

    def masks_of(k):
        found = [which[k] == 0]
        for axis in range(3):
            found.append(which[k] == 2 * axis + 2 - bits[axis])
        for axis in range(3):
            found.append(which[k] == 2 * axis + 1 + bits[axis])
        return found

    safe = jnp.where(radius > 0.0, radius, 1.0)
    mass = safe * 10.0
    mass = mass * mass * mass
    inertia = 0.4 * mass * safe * safe

    def inner_tables(fields):
        for f in range(10):
            table_ref[0, f] = fields[f]
            for axis in range(3):
                value = swapped(fields[f], axis)
                if f == axis:
                    value = value + jnp.where(bits[axis] == 0, 1.0, -1.0)
                table_ref[1 + axis, f] = value
        columns_ref[...] = jnp.concatenate(
            [fields[f] for f in range(6)] + [radius, jnp.zeros((72, SLOTS), jnp.float32)], axis=0
        ).T

    def outer_tables(ref, count):
        for axis in range(3):
            for f in range(count):
                value = jnp.where(
                    bits[axis] == 0,
                    swapped(ref[2 * axis, f], axis),
                    swapped(ref[2 * axis + 1, f], axis),
                )
                if f == axis:
                    value = value + jnp.where(bits[axis] == 0, -1.0, 1.0)
                table_ref[4 + axis, f] = value

    inner_tables([own_ref[f] for f in range(10)])
    pl.semaphore_wait(barrier, sum(there[d][1].astype(jnp.int32) for d in range(6)))

    for d in range(6):

        @pl.when(there[d][1])
        def _():
            halo_copy(d).start()

    for d in range(6):

        @pl.when(there[d][1])
        def _():
            face_copy(d).start()

    zero = jnp.zeros((BINS, SLOTS), jnp.float32)
    for step in range(SUBSTEPS):
        source = own_ref if step == 0 else own_2_ref
        fields = [source[f] for f in range(9)] + [partner_radius]
        if step > 0:
            inner_tables(fields)
        pair_pass(columns_ref, mine_ref, table_ref, (0, 1, 2, 3), sums_ref, True)

        if step == 0:
            loads[9].wait()
            for b in range(BINS):
                bx, by, bz = b // 4, b // 2 % 2, b % 2
                size_x, size_y = cells_x // 2, cells_y // 2
                block = gas_ref[
                    :,
                    bx * size_x : (bx + 1) * size_x,
                    by * size_y : (by + 1) * size_y,
                    bz * SLOTS : (bz + 1) * SLOTS,
                ].reshape(3 * SLOTS, SLOTS)
                cell = cells_ref[b : b + 1, :]
                high, low = halves(block)
                left = jnp.concatenate(
                    [high.astype(jnp.bfloat16), low.astype(jnp.bfloat16)], axis=1
                )
                lanes = jnp.where(one_hot(cell & (SLOTS - 1)), 1.0, 0.0).astype(jnp.bfloat16)
                right = jnp.concatenate([lanes, lanes], axis=0)
                product = jnp.dot(left, right, preferred_element_type=jnp.float32)
                rows = one_hot(lax.shift_right_logical(cell, 7))
                for i in range(3):
                    gas_out[i, b : b + 1, :] = jnp.sum(
                        jnp.where(rows, product[i * SLOTS : (i + 1) * SLOTS], 0.0),
                        axis=0,
                        keepdims=True,
                    )

        for d in range(6):

            @pl.when(there[d][1])
            def _():
                (halo_copy if step == 0 else halo_copy_2)(d ^ 1).wait_recv()

        outer_tables(halo_ref if step == 0 else halo_2_ref, 10 if step == 0 else 9)
        pair_pass(columns_ref, mine_ref, table_ref, (4, 5, 6), sums_ref, False)
        normal = [lane_sums(sums_ref, i) for i in range(3)]

        places, speeds, turning = fields[0:3], fields[3:6], fields[6:9]
        spring_source = springs_ref if step == 0 else springs_out
        shear_sum = [zero] * 3
        torque_sum = [zero] * 3
        for k in range(HIST):
            other = gathered(
                table_ref, range(7), which[k], masks_of(k), member[k], [zero] * 10
            )
            sep = [places[i] - other[i] for i in range(3)]
            square = dot(sep, sep) + soft_length**2
            inverse = lax.rsqrt(square)
            unit = [sep[i] * inverse for i in range(3)]
            overlap = radius + other[9] - square * inverse
            delta = jnp.maximum(overlap, 0.0)
            root = delta * lax.rsqrt(jnp.maximum(overlap, TINY))
            relative = [speeds[i] - other[3 + i] for i in range(3)]
            approach = dot(relative, unit)
            pressing = root * (normal_stiff * delta - normal_damp * approach)
            lever = [radius * turning[i] + other[9] * other[6 + i] for i in range(3)]
            spun = cross(lever, unit)
            contact = [relative[i] - spun[i] for i in range(3)]
            along = dot(contact, unit)
            sliding = [contact[i] - along * unit[i] for i in range(3)]
            spring = [spring_source[i * HIST + k] for i in range(3)]
            tilt = dot(spring, unit)
            stretched = [
                spring[i] - tilt * unit[i] + time_step * sliding[i] for i in range(3)
            ]
            length = jnp.sqrt(dot(stretched, stretched))
            limit = jnp.minimum(
                1.0, friction * jnp.abs(pressing) / jnp.maximum(shear_stiff * length, force_floor)
            )
            scale = valid[k] * limit
            fresh = [scale * stretched[i] for i in range(3)]
            shear = [-shear_stiff * fresh[i] for i in range(3)]
            twist = cross(shear, unit)
            for i in range(3):
                springs_out[i * HIST + k] = fresh[i]
            shear_sum = [shear_sum[i] + shear[i] for i in range(3)]
            torque_sum = [torque_sum[i] + twist[i] for i in range(3)]

        for i in range(3):
            push = normal_damp * normal[i] + shear_sum[i]
            push = push + drag_coeff * (gas_out[i] - speeds[i])
            speed = speeds[i] + time_step * (push / mass - (gravity if i == 2 else 0.0))
            spin = turning[i] + time_step * (radius * torque_sum[i]) / inertia
            target = own_2_ref if step == 0 else state_out
            target[3 + i] = speed
            target[6 + i] = spin
            target[i] = places[i] + time_step * speed
        if step == 0:
            for d in range(6):

                @pl.when(there[d][1])
                def _():
                    halo_copy_2(d).start()

    stores = [
        pltpu.make_async_copy(source, target, store_sem.at[n])
        for n, (source, target) in enumerate(
            (
                (state_out.at[0:3], places_out),
                (state_out.at[3:6], speeds_out),
                (state_out.at[6:9], turning_out),
                (springs_out, new_springs_out),
                (force_ref, force_out),
                (result_ref, result_out),
                (arrived_ref, arrived_out),
                (codes_ref, codes_out),
            )
        )
    ]
    for store in stores[:4]:
        store.start()

    for f in range(9):
        picked_ref[:, f, :] = state_out[f]
    picked_ref[:, 9, :] = radius
    for f in range(3 * HIST):
        picked_ref[:, 10 + f, :] = springs_out[f]
    for k in range(HIST):
        picked_ref[:, 22 + k, :] = (code[k] + 1).astype(jnp.float32)
    for f in range(26, 32):
        picked_ref[:, f, :] = zero
    for d in range(6):
        entry = jnp.broadcast_to(departures_ref[d], (8, SLOTS))
        slot = entry & (SLOTS - 1)
        home = lax.shift_right_arithmetic(entry, 7)
        for g in range(4):
            value = zero
            for b in range(BINS):
                taken = jnp.take_along_axis(
                    picked_ref[b, g * 8 : g * 8 + 8, :], slot, axis=1, mode="promise_in_bounds"
                )
                value = jnp.where(home == b, taken, value)
            gone_ref[d, g * 8 : g * 8 + 8, :] = value

        @pl.when(there[d][1])
        def _():
            moved_copy(d).start()

    deposit(counts_ref, radii_ref, cells_ref, state_out, gas_out, force_ref, result_ref)
    stores[4].start()
    for d in range(6):

        @pl.when(there[d][1])
        def _():
            halo_copy(d).wait_send()
            halo_copy_2(d).wait_send()
            face_copy(d).wait_send()
            face_copy(d ^ 1).wait_recv()

    loads[10].wait()
    sweep(pressure_ref, source_ref, face_x_ref, face_y_ref, face_z_ref, result_ref)
    stores[5].start()
    for d in range(6):

        @pl.when(there[d][1])
        def _():
            moved_copy(d).wait_send()
            moved_copy(d ^ 1).wait_recv()

    for d in range(6):
        codes_ref[d] = come_ref[d, 22:26, :].astype(jnp.int32) - 1
        for f in range(22):
            arrived_ref[f * 6 + d] = come_ref[d, f : f + 1, :]
    for store in stores[6:]:
        store.start()
    for store in stores:
        store.wait()


def deposit(counts_ref, radii_ref, cells_ref, state_ref, gas_ref, force_ref, result_ref):
    size_x, size_y = result_ref.shape[0] // 2, result_ref.shape[1] // 2
    live = jnp.where(live_mask(counts_ref), 1.0, 0.0)
    radius = radii_ref[...]
    values = [drag_coeff * (state_ref[3 + i] - gas_ref[i]) * live for i in range(3)]
    values.append(4.0 / 3.0 * math.pi * (radius * radius * radius) * live)
    values = [halves(value) for value in values]
    for b in range(BINS):
        bx, by, bz = b // 4, b // 2 % 2, b % 2
        block = (
            slice(bx * size_x, (bx + 1) * size_x),
            slice(by * size_y, (by + 1) * size_y),
            slice(bz * SLOTS, (bz + 1) * SLOTS),
        )
        cell = cells_ref[b : b + 1, :]
        rows = one_hot(lax.shift_right_logical(cell, 7))
        lanes = jnp.where(one_hot(cell & (SLOTS - 1)), 1.0, 0.0).astype(jnp.bfloat16)
        right = jnp.concatenate([lanes, lanes], axis=1)
        left = jnp.concatenate(
            [
                jnp.concatenate(
                    [
                        jnp.where(rows, part[b : b + 1, :], 0.0).astype(jnp.bfloat16)
                        for part in value
                    ],
                    axis=1,
                )
                for value in values
            ],
            axis=0,
        )
        product = lax.dot_general(
            left, right, (((1,), (1,)), ((), ())), preferred_element_type=jnp.float32
        )
        parts = [
            product[i * SLOTS : (i + 1) * SLOTS].reshape(size_x, size_y, SLOTS) for i in range(4)
        ]
        for i in range(3):
            force_ref[(i,) + block] = parts[i]
        result_ref[block] = volume_coeff * parts[3] + drag_weight * parts[2]


def sweep(pressure_ref, source_ref, face_x_ref, face_y_ref, face_z_ref, result_ref):
    cells_x, cells_y, cells_z = pressure_ref.shape
    row = lax.broadcasted_iota(jnp.int32, (cells_y, cells_z), 0)
    lane = lax.broadcasted_iota(jnp.int32, (cells_y, cells_z), 1)
    for x in range(cells_x):
        here = pressure_ref[x]
        total = pressure_ref[x - 1] if x > 0 else face_x_ref[0]
        total = total + (pressure_ref[x + 1] if x < cells_x - 1 else face_x_ref[1])
        total = total + jnp.where(row == 0, face_y_ref[0, x : x + 1, :], pltpu.roll(here, 1, 0))
        total = total + jnp.where(
            row == cells_y - 1, face_y_ref[1, x : x + 1, :], pltpu.roll(here, cells_y - 1, 0)
        )
        total = total + jnp.where(
            lane == 0,
            jnp.broadcast_to(face_z_ref[0][:, x : x + 1], here.shape),
            pltpu.roll(here, 1, 1),
        )
        total = total + jnp.where(
            lane == cells_z - 1,
            jnp.broadcast_to(face_z_ref[1][:, x : x + 1], here.shape),
            pltpu.roll(here, cells_z - 1, 1),
        )
        result_ref[x] = (total + source_ref[x] + result_ref[x]) / 6.0


def finish(*refs):
    sources, targets, held = refs[0:8], refs[8:16], refs[16:24]
    load_sem, store_sem = refs[24:26]
    parts = [(4, i) for i in range(3)] + [(n, None) for n in (5, 3, 6, 0, 1, 2, 7)]

    def piece(ref, part):
        return ref if part is None else ref.at[part]

    loads, stores = [], []
    for m, (n, part) in enumerate(parts):
        middle = piece(held[n], part)
        loads.append(pltpu.make_async_copy(piece(sources[n], part), middle, load_sem.at[m]))
        stores.append(pltpu.make_async_copy(middle, piece(targets[n], part), store_sem.at[m]))
    for load in loads:
        load.start()
    for load, store in zip(loads, stores):
        load.wait()
        store.start()
    for store in stores:
        store.wait()


def body(
    positions,
    velocities,
    spins,
    radii,
    counts,
    springs,
    partners,
    cells,
    departures,
    fluid_velocity,
    pressure,
    pressure_source,
):
    cells_x, cells_y, cells_z = pressure.shape
    f32 = jnp.float32
    smem = pl.BlockSpec(memory_space=pltpu.SMEM)
    far = pl.BlockSpec(memory_space=pltpu.HBM)
    shape = jax.ShapeDtypeStruct
    rows = (BINS, SLOTS)
    results = (
        shape((3,) + rows, f32),
        shape((3,) + rows, f32),
        shape((3,) + rows, f32),
        shape((3 * HIST,) + rows, f32),
        shape(fluid_velocity.shape, f32),
        shape(pressure.shape, f32),
        shape((132, 1, SLOTS), f32),
        shape((6, 4, SLOTS), jnp.int32),
    )
    made = pl.pallas_call(
        particles,
        out_shape=results,
        in_specs=[smem] + [far] * 11,
        out_specs=(far,) * 8,
        scratch_shapes=[
            pltpu.VMEM((9,) + rows, f32),
            pltpu.VMEM((3 * HIST,) + rows, f32),
            pltpu.VMEM((3,) + rows, f32),
            pltpu.VMEM((3,) + rows, f32),
            pltpu.VMEM((3,) + rows, f32),
            pltpu.VMEM((3,) + rows, f32),
            pltpu.VMEM(rows, f32),
            pltpu.VMEM((3 * HIST,) + rows, f32),
            pltpu.VMEM((HIST,) + rows, jnp.int32),
            pltpu.VMEM(rows, jnp.int32),
            pltpu.VMEM((6, 1, SLOTS), jnp.int32),
            pltpu.VMEM(fluid_velocity.shape, f32),
            pltpu.VMEM(pressure.shape, f32),
            pltpu.VMEM(pressure.shape, f32),
            pltpu.VMEM(fluid_velocity.shape, f32),
            pltpu.VMEM(pressure.shape, f32),
            pltpu.VMEM((132, 1, SLOTS), f32),
            pltpu.VMEM((6, 4, SLOTS), jnp.int32),
            pltpu.VMEM((7, 10) + rows, f32),
            pltpu.VMEM((SLOTS, SLOTS), f32),
            pltpu.VMEM((7, BINS, SLOTS, SLOTS), f32),
            pltpu.VMEM((3, BINS, SLOTS, SLOTS), f32),
            pltpu.VMEM((10,) + rows, f32),
            pltpu.VMEM((6, 10) + rows, f32),
            pltpu.VMEM((9,) + rows, f32),
            pltpu.VMEM((6, 9) + rows, f32),
            pltpu.VMEM((BINS, 32, SLOTS), f32),
            pltpu.VMEM((6, 32, SLOTS), f32),
            pltpu.VMEM((6, 32, SLOTS), f32),
            pltpu.VMEM((2, cells_x, cells_z), f32),
            pltpu.VMEM((2, cells_y, SLOTS), f32),
            pltpu.VMEM((2, cells_y, cells_z), f32),
            pltpu.VMEM((2, cells_x, cells_z), f32),
            pltpu.VMEM((2, cells_y, SLOTS), f32),
            pltpu.SemaphoreType.DMA((11,)),
            pltpu.SemaphoreType.DMA((9,)),
            pltpu.SemaphoreType.DMA((4, 6)),
            pltpu.SemaphoreType.DMA((4, 6)),
        ],
        compiler_params=pltpu.CompilerParams(
            collective_id=0, has_side_effects=True, vmem_limit_bytes=VMEM_LIMIT
        ),
    )(
        counts,
        positions.reshape((3,) + rows),
        velocities.reshape((3,) + rows),
        spins.reshape((3,) + rows),
        radii.reshape(rows),
        springs.reshape((3 * HIST,) + rows),
        partners.reshape((HIST,) + rows),
        cells.reshape(rows),
        departures.reshape(6, 1, SLOTS),
        fluid_velocity,
        pressure,
        pressure_source,
    )
    places, speeds, turning, last_springs, force, new_pressure, arrived, codes = pl.pallas_call(
        finish,
        out_shape=results,
        in_specs=[far] * 8,
        out_specs=(far,) * 8,
        scratch_shapes=[pltpu.VMEM(result.shape, result.dtype) for result in results]
        + [pltpu.SemaphoreType.DMA((10,)), pltpu.SemaphoreType.DMA((10,))],
        compiler_params=pltpu.CompilerParams(vmem_limit_bytes=VMEM_LIMIT),
    )(*made)
    return (
        places.reshape(positions.shape),
        speeds.reshape(positions.shape),
        turning.reshape(positions.shape),
        last_springs.reshape(springs.shape),
        force,
        new_pressure,
        arrived.reshape(1, 1, 1, 22, 6, SLOTS),
        jnp.swapaxes(codes, 0, 1)[None, None, None],
    )


def solution(mesh):
    return jax.shard_map(
        body,
        mesh=mesh,
        in_specs=(
            P(None, "gx", "gy", "gz", None),
            P(None, "gx", "gy", "gz", None),
            P(None, "gx", "gy", "gz", None),
            P("gx", "gy", "gz", None),
            P("gx", "gy", "gz"),
            P(None, None, "gx", "gy", "gz", None),
            P(None, "gx", "gy", "gz", None),
            P("gx", "gy", "gz", None),
            P("gx", "gy", "gz", None, None),
            P(None, "gx", "gy", "gz"),
            P("gx", "gy", "gz"),
            P("gx", "gy", "gz"),
        ),
        out_specs=(
            P(None, "gx", "gy", "gz", None),
            P(None, "gx", "gy", "gz", None),
            P(None, "gx", "gy", "gz", None),
            P(None, None, "gx", "gy", "gz", None),
            P(None, "gx", "gy", "gz"),
            P("gx", "gy", "gz"),
            P("gx", "gy", "gz", None, None, None),
            P("gx", "gy", "gz", None, None, None),
        ),
        check_vma=False,
    )
```

```python
import functools
import math

import jax
import jax.numpy as jnp
from jax import lax
from jax.experimental import pallas as pl
from jax.experimental.pallas import tpu as pltpu
from jax.sharding import PartitionSpec as P

SUBSTEPS = 2
HIST = 4
BINS = 8
SLOTS = 128
VMEM_LIMIT = 64 * 1024 * 1024

normal_stiff = 100.0
normal_damp = 2.0
shear_stiff = 30.0
friction = 0.5
time_step = 0.05
drag_coeff = 0.8
gravity = 1.0
soft_length = 0.05
force_floor = 0.5
volume_coeff = 100.0
drag_weight = 1.0

NOBODY = -10.0
TINY = 1e-30
SPEED_SCALE = normal_damp / normal_stiff
AXES = ("gx", "gy", "gz")
MESH = pl.DeviceIdType.MESH


def neighbour(direction):
    axis = AXES[direction // 2]
    size = lax.axis_size(axis)
    here = lax.axis_index(axis)
    if direction % 2 == 0:
        return {axis: lax.rem(here + size - 1, size)}, here > 0
    return {axis: lax.rem(here + 1, size)}, here < size - 1


def bin_bits():
    row = lax.broadcasted_iota(jnp.int32, (BINS, SLOTS), 0)
    return [lax.shift_right_logical(row, 2 - axis) & 1 for axis in range(3)]


def swapped(value, axis):
    step = 4 >> axis
    if axis == 0:
        return pltpu.roll(value, step, 0)
    upper = bin_bits()[axis] == 1
    return jnp.where(upper, pltpu.roll(value, step, 0), pltpu.roll(value, BINS - step, 0))


def live_mask(counts_ref):
    row = lax.broadcasted_iota(jnp.int32, (BINS, SLOTS), 0)
    slot = lax.broadcasted_iota(jnp.int32, (BINS, SLOTS), 1)
    limit = jnp.zeros((BINS, SLOTS), jnp.int32)
    for b in range(BINS):
        limit = jnp.where(row == b, counts_ref[b // 4, b // 2 % 2, b % 2], limit)
    return slot < limit


def halves(value):
    high = value.astype(jnp.bfloat16).astype(jnp.float32)
    return high, value - high


def one_hot(index_row):
    rows = lax.broadcasted_iota(jnp.int32, (SLOTS, SLOTS), 0)
    return rows == index_row


def cross(a, b):
    return [
        a[1] * b[2] - a[2] * b[1],
        a[2] * b[0] - a[0] * b[2],
        a[0] * b[1] - a[1] * b[0],
    ]


def dot(a, b):
    return a[0] * b[0] + a[1] * b[1] + a[2] * b[2]


def spread(table_ref, radii_ref, mine_ref, b):
    for f in range(7):
        row = radii_ref[b : b + 1, :] if f == 6 else table_ref[0, f, b : b + 1, :]
        if f in (3, 4, 5):
            row = row * SPEED_SCALE
        mine_ref[f, b] = jnp.broadcast_to(row, (SLOTS, SLOTS)).T


def bin_pairs(mine_ref, table_ref, scaled_ref, tables, sums_ref, first, b):
    row = pl.ds(b, 1)
    for c in range(SLOTS // 8):
        rows = slice(c * 8, c * 8 + 8)
        mine = [mine_ref[f, b, rows, :] for f in range(7)]
        total = None if first else [sums_ref[i, b, rows, :] for i in range(3)]
        for t in tables:
            other = [
                jnp.broadcast_to(ref[t, f, row, :], (8, SLOTS))
                for ref, f in (
                    (table_ref, 0),
                    (table_ref, 1),
                    (table_ref, 2),
                    (scaled_ref, 0),
                    (scaled_ref, 1),
                    (scaled_ref, 2),
                    (table_ref, 9),
                )
            ]
            sep = [mine[i] - other[i] for i in range(3)]
            square = dot(sep, sep) + soft_length**2
            inverse = lax.rsqrt(square)
            overlap = mine[6] + other[6] - square * inverse
            delta = jnp.maximum(overlap, 0.0)
            root = delta * lax.rsqrt(jnp.maximum(overlap, TINY))
            vrel = [mine[3 + i] - other[3 + i] for i in range(3)]
            approach = dot(vrel, sep) * inverse
            weight = (delta - approach) * (root * inverse)
            term = [weight * sep[i] for i in range(3)]
            total = term if total is None else [total[i] + term[i] for i in range(3)]
        for i in range(3):
            sums_ref[i, b, rows, :] = total[i]


def inner_pairs(radii_ref, mine_ref, table_ref, scaled_ref, sums_ref):
    spread(table_ref, radii_ref, mine_ref, 0)
    for b in range(BINS):
        if b < BINS - 1:
            spread(table_ref, radii_ref, mine_ref, b + 1)
        bin_pairs(mine_ref, table_ref, scaled_ref, (0, 1, 2, 3), sums_ref, True, b)


def outer_pairs(mine_ref, table_ref, scaled_ref, sums_ref):
    def one(b, carry):
        bin_pairs(mine_ref, table_ref, scaled_ref, (4, 5, 6), sums_ref, False, b)
        return carry

    lax.fori_loop(0, BINS, one, 0)


def lane_sums(sums_ref, i):
    row = lax.broadcasted_iota(jnp.int32, (BINS, 2 * SLOTS), 0)
    total = jnp.zeros((BINS, SLOTS), jnp.float32)
    for b in range(BINS):
        high, low = halves(sums_ref[i, b])
        right = jnp.concatenate([high.astype(jnp.bfloat16), low.astype(jnp.bfloat16)], axis=1)
        left = jnp.where(row == b, 1.0, 0.0).astype(jnp.bfloat16)
        total = total + lax.dot_general(
            left, right, (((1,), (1,)), ((), ())), preferred_element_type=jnp.float32
        )
    return total


def gathered(table_ref, tables, which, masks, member, got):
    for f in range(10):
        value = got[f]
        for t in tables:
            picked = jnp.take_along_axis(
                table_ref[t, f], member, axis=1, mode="promise_in_bounds"
            )
            value = jnp.where(masks[t], picked, value)
        got[f] = value
    return got


def particles(
    counts_ref,
    pos_hbm,
    vel_hbm,
    spin_hbm,
    radii_hbm,
    springs_hbm,
    partners_hbm,
    cells_hbm,
    departures_hbm,
    gas_hbm,
    pressure_hbm,
    source_hbm,
    places_out,
    speeds_out,
    turning_out,
    new_springs_out,
    force_out,
    result_out,
    arrived_out,
    codes_out,
    state_out,
    springs_out,
    gas_out,
    pos_ref,
    vel_ref,
    spin_ref,
    radii_ref,
    springs_ref,
    partners_ref,
    cells_ref,
    departures_ref,
    gas_ref,
    pressure_ref,
    source_ref,
    force_ref,
    result_ref,
    arrived_ref,
    codes_ref,
    table_ref,
    scaled_ref,
    mine_ref,
    sums_ref,
    own_ref,
    halo_ref,
    own_2_ref,
    halo_2_ref,
    picked_ref,
    gone_ref,
    come_ref,
    send_y_ref,
    send_z_ref,
    face_x_ref,
    face_y_ref,
    face_z_ref,
    local_sem,
    store_sem,
    send_sem,
    recv_sem,
):
    loads = [
        pltpu.make_async_copy(source, target, local_sem.at[n])
        for n, (source, target) in enumerate(
            (
                (pos_hbm, pos_ref),
                (vel_hbm, vel_ref),
                (spin_hbm, spin_ref),
                (radii_hbm, radii_ref),
                (pressure_hbm, pressure_ref),
                (partners_hbm, partners_ref),
                (springs_hbm, springs_ref),
                (cells_hbm, cells_ref),
                (departures_hbm, departures_ref),
                (gas_hbm, gas_ref),
                (source_hbm, source_ref),
            )
        )
    ]
    for load in loads:
        load.start()

    there = [neighbour(d) for d in range(6)]

    barrier = pltpu.get_barrier_semaphore()
    for d in range(6):

        @pl.when(there[d][1])
        def _():
            pl.semaphore_signal(barrier, inc=1, device_id=there[d][0], device_id_type=MESH)

    def halo_copy(d):
        return pltpu.make_async_remote_copy(
            src_ref=own_ref,
            dst_ref=halo_ref.at[d ^ 1],
            send_sem=send_sem.at[0, d],
            recv_sem=recv_sem.at[0, d ^ 1],
            device_id=there[d][0],
            device_id_type=MESH,
        )

    def halo_copy_2(d):
        return pltpu.make_async_remote_copy(
            src_ref=own_2_ref,
            dst_ref=halo_2_ref.at[d ^ 1],
            send_sem=send_sem.at[1, d],
            recv_sem=recv_sem.at[1, d ^ 1],
            device_id=there[d][0],
            device_id_type=MESH,
        )

    def moved_copy(d):
        return pltpu.make_async_remote_copy(
            src_ref=gone_ref.at[d],
            dst_ref=come_ref.at[d],
            send_sem=send_sem.at[2, d],
            recv_sem=recv_sem.at[2, d],
            device_id=there[d][0],
            device_id_type=MESH,
        )

    def face_copy(d):
        side = d % 2
        if d < 2:
            source = pressure_ref.at[0 if side == 0 else pressure_ref.shape[0] - 1]
            target = face_x_ref.at[1 - side]
        elif d < 4:
            source, target = send_y_ref.at[side], face_y_ref.at[1 - side]
        else:
            source, target = send_z_ref.at[side], face_z_ref.at[1 - side]
        return pltpu.make_async_remote_copy(
            src_ref=source,
            dst_ref=target,
            send_sem=send_sem.at[3, d],
            recv_sem=recv_sem.at[3, d ^ 1],
            device_id=there[d][0],
            device_id_type=MESH,
        )

    for load in loads[:4]:
        load.wait()
    live = live_mask(counts_ref)
    radius = radii_ref[...]
    partner_radius = jnp.where(live, radius, NOBODY)
    for i in range(3):
        own_ref[i] = pos_ref[i]
        own_ref[3 + i] = vel_ref[i]
        own_ref[6 + i] = spin_ref[i]
    own_ref[9] = partner_radius

    for s in range(6):

        @pl.when(jnp.logical_not(there[s][1]))
        def _():
            halo_ref[s] = jnp.zeros((10, BINS, SLOTS), jnp.float32)
            halo_ref[s, 9] = jnp.full((BINS, SLOTS), NOBODY, jnp.float32)
            halo_2_ref[s] = jnp.zeros((9, BINS, SLOTS), jnp.float32)
            come_ref[s ^ 1] = jnp.zeros((32, SLOTS), jnp.float32)
            face = (face_x_ref, face_y_ref, face_z_ref)[s // 2]
            face[s % 2] = jnp.zeros(face.shape[1:], jnp.float32)

    for load in loads[4:9]:
        load.wait()
    cells_x, cells_y, cells_z = pressure_ref.shape
    lane = lax.broadcasted_iota(jnp.int32, (cells_y, SLOTS), 1)
    for side in range(2):
        send_y_ref[side] = pressure_ref[:, 0 if side == 0 else cells_y - 1, :]
        face = jnp.zeros((cells_y, SLOTS), jnp.float32)
        for x in range(cells_x):
            if side == 0:
                column = pressure_ref[x, :, 0:SLOTS][:, 0:1]
            else:
                column = pressure_ref[x, :, cells_z - SLOTS : cells_z][:, SLOTS - 1 : SLOTS]
            face = jnp.where(lane == x, jnp.broadcast_to(column, (cells_y, SLOTS)), face)
        send_z_ref[side] = face
    bits = bin_bits()
    code = [partners_ref[k] for k in range(HIST)]
    valid = [jnp.where(code[k] >= 0, 1.0, 0.0) for k in range(HIST)]
    member = [jnp.maximum(code[k], 0) & (SLOTS - 1) for k in range(HIST)]
    which = [lax.shift_right_logical(jnp.maximum(code[k], 0), 7) for k in range(HIST)]

    def masks_of(k):
        found = [which[k] == 0]
        for axis in range(3):
            found.append(which[k] == 2 * axis + 2 - bits[axis])
        for axis in range(3):
            found.append(which[k] == 2 * axis + 1 + bits[axis])
        return found

    safe = jnp.where(radius > 0.0, radius, 1.0)
    mass = safe * 10.0
    mass = mass * mass * mass
    inertia = 0.4 * mass * safe * safe

    def inner_tables(fields):
        for f in range(10):
            table_ref[0, f] = fields[f]
            for axis in range(3):
                value = swapped(fields[f], axis)
                if f == axis:
                    value = value + jnp.where(bits[axis] == 0, 1.0, -1.0)
                table_ref[1 + axis, f] = value
        for t in range(4):
            for i in range(3):
                scaled_ref[t, i] = table_ref[t, 3 + i] * SPEED_SCALE

    def outer_tables(ref, count):
        for axis in range(3):
            for f in range(count):
                value = jnp.where(
                    bits[axis] == 0,
                    swapped(ref[2 * axis, f], axis),
                    swapped(ref[2 * axis + 1, f], axis),
                )
                if f == axis:
                    value = value + jnp.where(bits[axis] == 0, -1.0, 1.0)
                table_ref[4 + axis, f] = value
                if f in (3, 4, 5):
                    scaled_ref[4 + axis, f - 3] = value * SPEED_SCALE

    inner_tables([own_ref[f] for f in range(10)])
    pl.semaphore_wait(barrier, sum(there[d][1].astype(jnp.int32) for d in range(6)))

    for d in range(6):

        @pl.when(there[d][1])
        def _():
            halo_copy(d).start()

    for d in range(6):

        @pl.when(there[d][1])
        def _():
            face_copy(d).start()

    zero = jnp.zeros((BINS, SLOTS), jnp.float32)
    for step in range(SUBSTEPS):
        source = own_ref if step == 0 else own_2_ref
        fields = [source[f] for f in range(9)] + [partner_radius]
        if step > 0:
            inner_tables(fields)
        inner_pairs(radii_ref, mine_ref, table_ref, scaled_ref, sums_ref)

        if step == 0:
            loads[9].wait()
            for b in range(BINS):
                bx, by, bz = b // 4, b // 2 % 2, b % 2
                size_x, size_y = cells_x // 2, cells_y // 2
                block = gas_ref[
                    :,
                    bx * size_x : (bx + 1) * size_x,
                    by * size_y : (by + 1) * size_y,
                    bz * SLOTS : (bz + 1) * SLOTS,
                ].reshape(3 * SLOTS, SLOTS)
                cell = cells_ref[b : b + 1, :]
                high, low = halves(block)
                left = jnp.concatenate(
                    [high.astype(jnp.bfloat16), low.astype(jnp.bfloat16)], axis=1
                )
                lanes = jnp.where(one_hot(cell & (SLOTS - 1)), 1.0, 0.0).astype(jnp.bfloat16)
                right = jnp.concatenate([lanes, lanes], axis=0)
                product = jnp.dot(left, right, preferred_element_type=jnp.float32)
                rows = one_hot(lax.shift_right_logical(cell, 7))
                for i in range(3):
                    gas_out[i, b : b + 1, :] = jnp.sum(
                        jnp.where(rows, product[i * SLOTS : (i + 1) * SLOTS], 0.0),
                        axis=0,
                        keepdims=True,
                    )

        for d in range(6):

            @pl.when(there[d][1])
            def _():
                (halo_copy if step == 0 else halo_copy_2)(d ^ 1).wait_recv()

        outer_tables(halo_ref if step == 0 else halo_2_ref, 10 if step == 0 else 9)
        outer_pairs(mine_ref, table_ref, scaled_ref, sums_ref)
        normal = [lane_sums(sums_ref, i) for i in range(3)]

        places, speeds, turning = fields[0:3], fields[3:6], fields[6:9]
        spring_source = springs_ref if step == 0 else springs_out
        shear_sum = [zero] * 3
        torque_sum = [zero] * 3
        for k in range(HIST):
            other = gathered(
                table_ref, range(7), which[k], masks_of(k), member[k], [zero] * 10
            )
            sep = [places[i] - other[i] for i in range(3)]
            square = dot(sep, sep) + soft_length**2
            inverse = lax.rsqrt(square)
            unit = [sep[i] * inverse for i in range(3)]
            overlap = radius + other[9] - square * inverse
            delta = jnp.maximum(overlap, 0.0)
            root = delta * lax.rsqrt(jnp.maximum(overlap, TINY))
            relative = [speeds[i] - other[3 + i] for i in range(3)]
            approach = dot(relative, unit)
            pressing = root * (normal_stiff * delta - normal_damp * approach)
            lever = [radius * turning[i] + other[9] * other[6 + i] for i in range(3)]
            spun = cross(lever, unit)
            contact = [relative[i] - spun[i] for i in range(3)]
            along = dot(contact, unit)
            sliding = [contact[i] - along * unit[i] for i in range(3)]
            spring = [spring_source[i * HIST + k] for i in range(3)]
            tilt = dot(spring, unit)
            stretched = [
                spring[i] - tilt * unit[i] + time_step * sliding[i] for i in range(3)
            ]
            length = jnp.sqrt(dot(stretched, stretched))
            limit = jnp.minimum(
                1.0, friction * jnp.abs(pressing) / jnp.maximum(shear_stiff * length, force_floor)
            )
            scale = valid[k] * limit
            fresh = [scale * stretched[i] for i in range(3)]
            shear = [-shear_stiff * fresh[i] for i in range(3)]
            twist = cross(shear, unit)
            for i in range(3):
                springs_out[i * HIST + k] = fresh[i]
            shear_sum = [shear_sum[i] + shear[i] for i in range(3)]
            torque_sum = [torque_sum[i] + twist[i] for i in range(3)]

        for i in range(3):
            push = normal_stiff * normal[i] + shear_sum[i]
            push = push + drag_coeff * (gas_out[i] - speeds[i])
            speed = speeds[i] + time_step * (push / mass - (gravity if i == 2 else 0.0))
            spin = turning[i] + time_step * (radius * torque_sum[i]) / inertia
            target = own_2_ref if step == 0 else state_out
            target[3 + i] = speed
            target[6 + i] = spin
            target[i] = places[i] + time_step * speed
        if step == 0:
            for d in range(6):

                @pl.when(there[d][1])
                def _():
                    halo_copy_2(d).start()

    stores = [
        pltpu.make_async_copy(source, target, store_sem.at[n])
        for n, (source, target) in enumerate(
            (
                (state_out.at[0:3], places_out),
                (state_out.at[3:6], speeds_out),
                (state_out.at[6:9], turning_out),
                (springs_out, new_springs_out),
                (force_ref, force_out),
                (result_ref, result_out),
                (arrived_ref, arrived_out),
                (codes_ref, codes_out),
            )
        )
    ]
    for store in stores[:4]:
        store.start()

    for f in range(9):
        picked_ref[:, f, :] = state_out[f]
    picked_ref[:, 9, :] = radius
    for f in range(3 * HIST):
        picked_ref[:, 10 + f, :] = springs_out[f]
    for k in range(HIST):
        picked_ref[:, 22 + k, :] = (code[k] + 1).astype(jnp.float32)
    for f in range(26, 32):
        picked_ref[:, f, :] = zero
    for d in range(6):
        entry = jnp.broadcast_to(departures_ref[d], (8, SLOTS))
        slot = entry & (SLOTS - 1)
        home = lax.shift_right_arithmetic(entry, 7)
        for g in range(4):
            value = zero
            for b in range(BINS):
                taken = jnp.take_along_axis(
                    picked_ref[b, g * 8 : g * 8 + 8, :], slot, axis=1, mode="promise_in_bounds"
                )
                value = jnp.where(home == b, taken, value)
            gone_ref[d, g * 8 : g * 8 + 8, :] = value

        @pl.when(there[d][1])
        def _():
            moved_copy(d).start()

    deposit(counts_ref, radii_ref, cells_ref, state_out, gas_out, force_ref, result_ref)
    stores[4].start()
    for d in range(6):

        @pl.when(there[d][1])
        def _():
            halo_copy(d).wait_send()
            halo_copy_2(d).wait_send()
            face_copy(d).wait_send()
            face_copy(d ^ 1).wait_recv()

    loads[10].wait()
    sweep(pressure_ref, source_ref, face_x_ref, face_y_ref, face_z_ref, result_ref)
    stores[5].start()
    for d in range(6):

        @pl.when(there[d][1])
        def _():
            moved_copy(d).wait_send()
            moved_copy(d ^ 1).wait_recv()

    for d in range(6):
        codes_ref[d] = come_ref[d, 22:26, :].astype(jnp.int32) - 1
        for f in range(22):
            arrived_ref[f * 6 + d] = come_ref[d, f : f + 1, :]
    for store in stores[6:]:
        store.start()
    for store in stores:
        store.wait()


def deposit(counts_ref, radii_ref, cells_ref, state_ref, gas_ref, force_ref, result_ref):
    size_x, size_y = result_ref.shape[0] // 2, result_ref.shape[1] // 2
    live = jnp.where(live_mask(counts_ref), 1.0, 0.0)
    radius = radii_ref[...]
    values = [drag_coeff * (state_ref[3 + i] - gas_ref[i]) * live for i in range(3)]
    values.append(4.0 / 3.0 * math.pi * (radius * radius * radius) * live)
    values = [halves(value) for value in values]
    for b in range(BINS):
        bx, by, bz = b // 4, b // 2 % 2, b % 2
        block = (
            slice(bx * size_x, (bx + 1) * size_x),
            slice(by * size_y, (by + 1) * size_y),
            slice(bz * SLOTS, (bz + 1) * SLOTS),
        )
        cell = cells_ref[b : b + 1, :]
        rows = one_hot(lax.shift_right_logical(cell, 7))
        lanes = jnp.where(one_hot(cell & (SLOTS - 1)), 1.0, 0.0).astype(jnp.bfloat16)
        right = jnp.concatenate([lanes, lanes], axis=1)
        left = jnp.concatenate(
            [
                jnp.concatenate(
                    [
                        jnp.where(rows, part[b : b + 1, :], 0.0).astype(jnp.bfloat16)
                        for part in value
                    ],
                    axis=1,
                )
                for value in values
            ],
            axis=0,
        )
        product = lax.dot_general(
            left, right, (((1,), (1,)), ((), ())), preferred_element_type=jnp.float32
        )
        parts = [
            product[i * SLOTS : (i + 1) * SLOTS].reshape(size_x, size_y, SLOTS) for i in range(4)
        ]
        for i in range(3):
            force_ref[(i,) + block] = parts[i]
        result_ref[block] = volume_coeff * parts[3] + drag_weight * parts[2]


def sweep(pressure_ref, source_ref, face_x_ref, face_y_ref, face_z_ref, result_ref):
    cells_x, cells_y, cells_z = pressure_ref.shape
    row = lax.broadcasted_iota(jnp.int32, (cells_y, cells_z), 0)
    lane = lax.broadcasted_iota(jnp.int32, (cells_y, cells_z), 1)
    for x in range(cells_x):
        here = pressure_ref[x]
        total = pressure_ref[x - 1] if x > 0 else face_x_ref[0]
        total = total + (pressure_ref[x + 1] if x < cells_x - 1 else face_x_ref[1])
        total = total + jnp.where(row == 0, face_y_ref[0, x : x + 1, :], pltpu.roll(here, 1, 0))
        total = total + jnp.where(
            row == cells_y - 1, face_y_ref[1, x : x + 1, :], pltpu.roll(here, cells_y - 1, 0)
        )
        total = total + jnp.where(
            lane == 0,
            jnp.broadcast_to(face_z_ref[0][:, x : x + 1], here.shape),
            pltpu.roll(here, 1, 1),
        )
        total = total + jnp.where(
            lane == cells_z - 1,
            jnp.broadcast_to(face_z_ref[1][:, x : x + 1], here.shape),
            pltpu.roll(here, cells_z - 1, 1),
        )
        result_ref[x] = (total + source_ref[x] + result_ref[x]) / 6.0


def finish(*refs):
    sources, targets, held = refs[0:8], refs[8:16], refs[16:24]
    load_sem, store_sem = refs[24:26]
    parts = [(4, i) for i in range(3)] + [(n, None) for n in (5, 3, 6, 0, 1, 2, 7)]

    def piece(ref, part):
        return ref if part is None else ref.at[part]

    loads, stores = [], []
    for m, (n, part) in enumerate(parts):
        middle = piece(held[n], part)
        loads.append(pltpu.make_async_copy(piece(sources[n], part), middle, load_sem.at[m]))
        stores.append(pltpu.make_async_copy(middle, piece(targets[n], part), store_sem.at[m]))
    for load in loads:
        load.start()
    for load, store in zip(loads, stores):
        load.wait()
        store.start()
    for store in stores:
        store.wait()


def body(
    positions,
    velocities,
    spins,
    radii,
    counts,
    springs,
    partners,
    cells,
    departures,
    fluid_velocity,
    pressure,
    pressure_source,
):
    cells_x, cells_y, cells_z = pressure.shape
    f32 = jnp.float32
    smem = pl.BlockSpec(memory_space=pltpu.SMEM)
    far = pl.BlockSpec(memory_space=pltpu.HBM)
    shape = jax.ShapeDtypeStruct
    rows = (BINS, SLOTS)
    results = (
        shape((3,) + rows, f32),
        shape((3,) + rows, f32),
        shape((3,) + rows, f32),
        shape((3 * HIST,) + rows, f32),
        shape(fluid_velocity.shape, f32),
        shape(pressure.shape, f32),
        shape((132, 1, SLOTS), f32),
        shape((6, 4, SLOTS), jnp.int32),
    )
    made = pl.pallas_call(
        particles,
        out_shape=results,
        in_specs=[smem] + [far] * 11,
        out_specs=(far,) * 8,
        scratch_shapes=[
            pltpu.VMEM((9,) + rows, f32),
            pltpu.VMEM((3 * HIST,) + rows, f32),
            pltpu.VMEM((3,) + rows, f32),
            pltpu.VMEM((3,) + rows, f32),
            pltpu.VMEM((3,) + rows, f32),
            pltpu.VMEM((3,) + rows, f32),
            pltpu.VMEM(rows, f32),
            pltpu.VMEM((3 * HIST,) + rows, f32),
            pltpu.VMEM((HIST,) + rows, jnp.int32),
            pltpu.VMEM(rows, jnp.int32),
            pltpu.VMEM((6, 1, SLOTS), jnp.int32),
            pltpu.VMEM(fluid_velocity.shape, f32),
            pltpu.VMEM(pressure.shape, f32),
            pltpu.VMEM(pressure.shape, f32),
            pltpu.VMEM(fluid_velocity.shape, f32),
            pltpu.VMEM(pressure.shape, f32),
            pltpu.VMEM((132, 1, SLOTS), f32),
            pltpu.VMEM((6, 4, SLOTS), jnp.int32),
            pltpu.VMEM((7, 10) + rows, f32),
            pltpu.VMEM((7, 3) + rows, f32),
            pltpu.VMEM((7, BINS, SLOTS, SLOTS), f32),
            pltpu.VMEM((3, BINS, SLOTS, SLOTS), f32),
            pltpu.VMEM((10,) + rows, f32),
            pltpu.VMEM((6, 10) + rows, f32),
            pltpu.VMEM((9,) + rows, f32),
            pltpu.VMEM((6, 9) + rows, f32),
            pltpu.VMEM((BINS, 32, SLOTS), f32),
            pltpu.VMEM((6, 32, SLOTS), f32),
            pltpu.VMEM((6, 32, SLOTS), f32),
            pltpu.VMEM((2, cells_x, cells_z), f32),
            pltpu.VMEM((2, cells_y, SLOTS), f32),
            pltpu.VMEM((2, cells_y, cells_z), f32),
            pltpu.VMEM((2, cells_x, cells_z), f32),
            pltpu.VMEM((2, cells_y, SLOTS), f32),
            pltpu.SemaphoreType.DMA((11,)),
            pltpu.SemaphoreType.DMA((9,)),
            pltpu.SemaphoreType.DMA((4, 6)),
            pltpu.SemaphoreType.DMA((4, 6)),
        ],
        compiler_params=pltpu.CompilerParams(
            collective_id=0, has_side_effects=True, vmem_limit_bytes=VMEM_LIMIT
        ),
    )(
        counts,
        positions.reshape((3,) + rows),
        velocities.reshape((3,) + rows),
        spins.reshape((3,) + rows),
        radii.reshape(rows),
        springs.reshape((3 * HIST,) + rows),
        partners.reshape((HIST,) + rows),
        cells.reshape(rows),
        departures.reshape(6, 1, SLOTS),
        fluid_velocity,
        pressure,
        pressure_source,
    )
    places, speeds, turning, last_springs, force, new_pressure, arrived, codes = pl.pallas_call(
        finish,
        out_shape=results,
        in_specs=[far] * 8,
        out_specs=(far,) * 8,
        scratch_shapes=[pltpu.VMEM(result.shape, result.dtype) for result in results]
        + [pltpu.SemaphoreType.DMA((10,)), pltpu.SemaphoreType.DMA((10,))],
        compiler_params=pltpu.CompilerParams(vmem_limit_bytes=VMEM_LIMIT),
    )(*made)
    return (
        places.reshape(positions.shape),
        speeds.reshape(positions.shape),
        turning.reshape(positions.shape),
        last_springs.reshape(springs.shape),
        force,
        new_pressure,
        arrived.reshape(1, 1, 1, 22, 6, SLOTS),
        jnp.swapaxes(codes, 0, 1)[None, None, None],
    )


def solution(mesh):
    return jax.shard_map(
        body,
        mesh=mesh,
        in_specs=(
            P(None, "gx", "gy", "gz", None),
            P(None, "gx", "gy", "gz", None),
            P(None, "gx", "gy", "gz", None),
            P("gx", "gy", "gz", None),
            P("gx", "gy", "gz"),
            P(None, None, "gx", "gy", "gz", None),
            P(None, "gx", "gy", "gz", None),
            P("gx", "gy", "gz", None),
            P("gx", "gy", "gz", None, None),
            P(None, "gx", "gy", "gz"),
            P("gx", "gy", "gz"),
            P("gx", "gy", "gz"),
        ),
        out_specs=(
            P(None, "gx", "gy", "gz", None),
            P(None, "gx", "gy", "gz", None),
            P(None, "gx", "gy", "gz", None),
            P(None, None, "gx", "gy", "gz", None),
            P(None, "gx", "gy", "gz"),
            P("gx", "gy", "gz"),
            P("gx", "gy", "gz", None, None, None),
            P("gx", "gy", "gz", None, None, None),
        ),
        check_vma=False,
    )
```

```python
import functools
import math

import jax
import jax.numpy as jnp
from jax import lax
from jax.experimental import pallas as pl
from jax.experimental.pallas import tpu as pltpu
from jax.sharding import PartitionSpec as P

SUBSTEPS = 2
HIST = 4
BINS = 8
SLOTS = 128
VMEM_LIMIT = 64 * 1024 * 1024

normal_stiff = 100.0
normal_damp = 2.0
shear_stiff = 30.0
friction = 0.5
time_step = 0.05
drag_coeff = 0.8
gravity = 1.0
soft_length = 0.05
force_floor = 0.5
volume_coeff = 100.0
drag_weight = 1.0

NOBODY = -10.0
TINY = 1e-30
SPEED_SCALE = normal_damp / normal_stiff
AXES = ("gx", "gy", "gz")
MESH = pl.DeviceIdType.MESH


def neighbour(direction):
    axis = AXES[direction // 2]
    size = lax.axis_size(axis)
    here = lax.axis_index(axis)
    if direction % 2 == 0:
        return {axis: lax.rem(here + size - 1, size)}, here > 0
    return {axis: lax.rem(here + 1, size)}, here < size - 1


def bin_bits():
    row = lax.broadcasted_iota(jnp.int32, (BINS, SLOTS), 0)
    return [lax.shift_right_logical(row, 2 - axis) & 1 for axis in range(3)]


def swapped(value, axis):
    step = 4 >> axis
    if axis == 0:
        return pltpu.roll(value, step, 0)
    upper = bin_bits()[axis] == 1
    return jnp.where(upper, pltpu.roll(value, step, 0), pltpu.roll(value, BINS - step, 0))


def live_mask(counts_ref):
    row = lax.broadcasted_iota(jnp.int32, (BINS, SLOTS), 0)
    slot = lax.broadcasted_iota(jnp.int32, (BINS, SLOTS), 1)
    limit = jnp.zeros((BINS, SLOTS), jnp.int32)
    for b in range(BINS):
        limit = jnp.where(row == b, counts_ref[b // 4, b // 2 % 2, b % 2], limit)
    return slot < limit


def halves(value):
    high = value.astype(jnp.bfloat16).astype(jnp.float32)
    return high, value - high


def one_hot(index_row):
    rows = lax.broadcasted_iota(jnp.int32, (SLOTS, SLOTS), 0)
    return rows == index_row


def cross(a, b):
    return [
        a[1] * b[2] - a[2] * b[1],
        a[2] * b[0] - a[0] * b[2],
        a[0] * b[1] - a[1] * b[0],
    ]


def dot(a, b):
    return a[0] * b[0] + a[1] * b[1] + a[2] * b[2]


def spread(table_ref, radii_ref, mine_ref, b):
    for f in range(7):
        row = radii_ref[b : b + 1, :] if f == 6 else table_ref[0, f, b : b + 1, :]
        if f in (3, 4, 5):
            row = row * SPEED_SCALE
        mine_ref[f, b] = jnp.broadcast_to(row, (SLOTS, SLOTS)).T


def bin_pairs(mine_ref, table_ref, scaled_ref, tables, sums_ref, first, b):
    row = pl.ds(b, 1)
    for c in range(SLOTS // 8):
        rows = slice(c * 8, c * 8 + 8)
        mine = [mine_ref[f, b, rows, :] for f in range(7)]
        total = None if first else [sums_ref[i, b, rows, :] for i in range(3)]
        for t in tables:
            other = [
                jnp.broadcast_to(ref[t, f, row, :], (8, SLOTS))
                for ref, f in (
                    (table_ref, 0),
                    (table_ref, 1),
                    (table_ref, 2),
                    (scaled_ref, 0),
                    (scaled_ref, 1),
                    (scaled_ref, 2),
                    (table_ref, 9),
                )
            ]
            sep = [mine[i] - other[i] for i in range(3)]
            square = dot(sep, sep) + soft_length**2
            inverse = lax.rsqrt(square)
            overlap = mine[6] + other[6] - square * inverse
            delta = jnp.maximum(overlap, 0.0)
            root = delta * lax.rsqrt(jnp.maximum(overlap, TINY))
            vrel = [mine[3 + i] - other[3 + i] for i in range(3)]
            approach = dot(vrel, sep) * inverse
            weight = (delta - approach) * (root * inverse)
            term = [weight * sep[i] for i in range(3)]
            total = term if total is None else [total[i] + term[i] for i in range(3)]
        for i in range(3):
            sums_ref[i, b, rows, :] = total[i]


def inner_pairs(radii_ref, mine_ref, table_ref, scaled_ref, sums_ref):
    spread(table_ref, radii_ref, mine_ref, 0)
    for b in range(BINS):
        if b < BINS - 1:
            spread(table_ref, radii_ref, mine_ref, b + 1)
        bin_pairs(mine_ref, table_ref, scaled_ref, (0, 1, 2, 3), sums_ref, True, b)


def outer_pairs(mine_ref, table_ref, scaled_ref, sums_ref):
    def one(b, carry):
        bin_pairs(mine_ref, table_ref, scaled_ref, (4, 5, 6), sums_ref, False, b)
        return carry

    lax.fori_loop(0, BINS, one, 0)


def lane_sums(sums_ref, i):
    row = lax.broadcasted_iota(jnp.int32, (BINS, 2 * SLOTS), 0)
    total = jnp.zeros((BINS, SLOTS), jnp.float32)
    for b in range(BINS):
        high, low = halves(sums_ref[i, b])
        right = jnp.concatenate([high.astype(jnp.bfloat16), low.astype(jnp.bfloat16)], axis=1)
        left = jnp.where(row == b, 1.0, 0.0).astype(jnp.bfloat16)
        total = total + lax.dot_general(
            left, right, (((1,), (1,)), ((), ())), preferred_element_type=jnp.float32
        )
    return total


def gathered(table_ref, tables, which, masks, member, got):
    for f in range(10):
        value = got[f]
        for t in tables:
            picked = jnp.take_along_axis(
                table_ref[t, f], member, axis=1, mode="promise_in_bounds"
            )
            value = jnp.where(masks[t], picked, value)
        got[f] = value
    return got


def particles(
    counts_hbm,
    pos_hbm,
    vel_hbm,
    spin_hbm,
    radii_hbm,
    springs_hbm,
    partners_hbm,
    cells_hbm,
    departures_hbm,
    gas_hbm,
    pressure_hbm,
    source_hbm,
    places_out,
    speeds_out,
    turning_out,
    new_springs_out,
    force_out,
    result_out,
    arrived_out,
    codes_out,
    state_out,
    springs_out,
    gas_out,
    counts_ref,
    pos_ref,
    vel_ref,
    spin_ref,
    radii_ref,
    springs_ref,
    partners_ref,
    cells_ref,
    departures_ref,
    gas_ref,
    pressure_ref,
    source_ref,
    force_ref,
    result_ref,
    arrived_ref,
    codes_ref,
    table_ref,
    scaled_ref,
    mine_ref,
    sums_ref,
    own_ref,
    own_2_ref,
    packed_ref,
    halo_ref,
    picked_ref,
    gone_ref,
    come_ref,
    send_y_ref,
    send_z_ref,
    face_x_ref,
    face_y_ref,
    face_z_ref,
    local_sem,
    store_sem,
    send_sem,
    recv_sem,
):
    loads = [
        pltpu.make_async_copy(source, target, local_sem.at[n])
        for n, (source, target) in enumerate(
            (
                (pos_hbm, pos_ref),
                (vel_hbm, vel_ref),
                (spin_hbm, spin_ref),
                (radii_hbm, radii_ref),
                (counts_hbm, counts_ref),
                (pressure_hbm, pressure_ref),
                (partners_hbm, partners_ref),
                (springs_hbm, springs_ref),
                (cells_hbm, cells_ref),
                (departures_hbm, departures_ref),
                (gas_hbm, gas_ref),
                (source_hbm, source_ref),
            )
        )
    ]
    for load in loads:
        load.start()

    there = [neighbour(d) for d in range(6)]

    barrier = pltpu.get_barrier_semaphore()
    for d in range(6):

        @pl.when(there[d][1])
        def _():
            pl.semaphore_signal(barrier, inc=1, device_id=there[d][0], device_id_type=MESH)

    def halo_copy(step, d):
        return pltpu.make_async_remote_copy(
            src_ref=packed_ref.at[step, d],
            dst_ref=halo_ref.at[step, d ^ 1],
            send_sem=send_sem.at[step, d],
            recv_sem=recv_sem.at[step, d ^ 1],
            device_id=there[d][0],
            device_id_type=MESH,
        )

    def moved_copy(d):
        return pltpu.make_async_remote_copy(
            src_ref=gone_ref.at[d],
            dst_ref=come_ref.at[d],
            send_sem=send_sem.at[2, d],
            recv_sem=recv_sem.at[2, d],
            device_id=there[d][0],
            device_id_type=MESH,
        )

    def face_copy(d):
        side = d % 2
        if d < 2:
            source = pressure_ref.at[0 if side == 0 else pressure_ref.shape[0] - 1]
            target = face_x_ref.at[1 - side]
        elif d < 4:
            source, target = send_y_ref.at[side], face_y_ref.at[1 - side]
        else:
            source, target = send_z_ref.at[side], face_z_ref.at[1 - side]
        return pltpu.make_async_remote_copy(
            src_ref=source,
            dst_ref=target,
            send_sem=send_sem.at[3, d],
            recv_sem=recv_sem.at[3, d ^ 1],
            device_id=there[d][0],
            device_id_type=MESH,
        )

    for load in loads[:5]:
        load.wait()
    live = live_mask(counts_ref)
    radius = radii_ref[...]
    partner_radius = jnp.where(live, radius, NOBODY)
    for i in range(3):
        own_ref[i] = pos_ref[i]
        own_ref[3 + i] = vel_ref[i]
        own_ref[6 + i] = spin_ref[i]
    bits = bin_bits()

    def send_halo(step, fields):
        for d in range(6):
            axis = d // 2
            for n in range(5):
                packed_ref[step, d, n] = jnp.where(
                    bits[axis] == d % 2, fields[2 * n], swapped(fields[2 * n + 1], axis)
                )
        if step == 0:
            pl.semaphore_wait(barrier, sum(there[d][1].astype(jnp.int32) for d in range(6)))
        for d in range(6):

            @pl.when(there[d][1])
            def _():
                halo_copy(step, d).start()


    for s in range(6):

        @pl.when(jnp.logical_not(there[s][1]))
        def _():
            for step in range(SUBSTEPS):
                halo_ref[step, s] = jnp.zeros((5, BINS, SLOTS), jnp.float32)
                halo_ref[step, s, 4] = jnp.full((BINS, SLOTS), NOBODY, jnp.float32)
            come_ref[s ^ 1] = jnp.zeros((32, SLOTS), jnp.float32)
            face = (face_x_ref, face_y_ref, face_z_ref)[s // 2]
            face[s % 2] = jnp.zeros(face.shape[1:], jnp.float32)

    send_halo(0, [own_ref[f] for f in range(9)] + [partner_radius])
    for load in loads[5:10]:
        load.wait()
    code = [partners_ref[k] for k in range(HIST)]
    valid = [jnp.where(code[k] >= 0, 1.0, 0.0) for k in range(HIST)]
    member = [jnp.maximum(code[k], 0) & (SLOTS - 1) for k in range(HIST)]
    which = [lax.shift_right_logical(jnp.maximum(code[k], 0), 7) for k in range(HIST)]

    def masks_of(k):
        found = [which[k] == 0]
        for axis in range(3):
            found.append(which[k] == 2 * axis + 2 - bits[axis])
        for axis in range(3):
            found.append(which[k] == 2 * axis + 1 + bits[axis])
        return found

    safe = jnp.where(radius > 0.0, radius, 1.0)
    mass = safe * 10.0
    mass = mass * mass * mass
    inertia = 0.4 * mass * safe * safe

    def inner_tables(fields):
        for f in range(10):
            table_ref[0, f] = fields[f]
            for axis in range(3):
                value = swapped(fields[f], axis)
                if f == axis:
                    value = value + jnp.where(bits[axis] == 0, 1.0, -1.0)
                table_ref[1 + axis, f] = value
        for t in range(4):
            for i in range(3):
                scaled_ref[t, i] = table_ref[t, 3 + i] * SPEED_SCALE

    def outer_tables(step):
        for axis in range(3):
            for n in range(5):
                low, high = halo_ref[step, 2 * axis, n], halo_ref[step, 2 * axis + 1, n]
                first = jnp.where(bits[axis] == 0, swapped(low, axis), swapped(high, axis))
                second = jnp.where(bits[axis] == 0, low, high)
                for f, value in ((2 * n, first), (2 * n + 1, second)):
                    if f == axis:
                        value = value + jnp.where(bits[axis] == 0, -1.0, 1.0)
                    table_ref[4 + axis, f] = value
                    if f in (3, 4, 5):
                        scaled_ref[4 + axis, f - 3] = value * SPEED_SCALE

    cells_x, cells_y, cells_z = pressure_ref.shape

    def send_faces():
        lane = lax.broadcasted_iota(jnp.int32, (cells_y, SLOTS), 1)
        for side in range(2):
            send_y_ref[side] = pressure_ref[:, 0 if side == 0 else cells_y - 1, :]
            face = jnp.zeros((cells_y, SLOTS), jnp.float32)
            for x in range(cells_x):
                if side == 0:
                    column = pressure_ref[x, :, 0:SLOTS][:, 0:1]
                else:
                    column = pressure_ref[x, :, cells_z - SLOTS : cells_z][:, SLOTS - 1 : SLOTS]
                face = jnp.where(lane == x, jnp.broadcast_to(column, (cells_y, SLOTS)), face)
            send_z_ref[side] = face
        for d in range(6):

            @pl.when(there[d][1])
            def _():
                face_copy(d).start()

    zero = jnp.zeros((BINS, SLOTS), jnp.float32)
    for step in range(SUBSTEPS):
        source = own_ref if step == 0 else own_2_ref
        fields = [source[f] for f in range(9)] + [partner_radius]
        inner_tables(fields)
        inner_pairs(radii_ref, mine_ref, table_ref, scaled_ref, sums_ref)

        if step == 0:
            send_faces()
            loads[10].wait()
            for b in range(BINS):
                bx, by, bz = b // 4, b // 2 % 2, b % 2
                size_x, size_y = cells_x // 2, cells_y // 2
                block = gas_ref[
                    :,
                    bx * size_x : (bx + 1) * size_x,
                    by * size_y : (by + 1) * size_y,
                    bz * SLOTS : (bz + 1) * SLOTS,
                ].reshape(3 * SLOTS, SLOTS)
                cell = cells_ref[b : b + 1, :]
                high, low = halves(block)
                left = jnp.concatenate(
                    [high.astype(jnp.bfloat16), low.astype(jnp.bfloat16)], axis=1
                )
                lanes = jnp.where(one_hot(cell & (SLOTS - 1)), 1.0, 0.0).astype(jnp.bfloat16)
                right = jnp.concatenate([lanes, lanes], axis=0)
                product = jnp.dot(left, right, preferred_element_type=jnp.float32)
                rows = one_hot(lax.shift_right_logical(cell, 7))
                for i in range(3):
                    gas_out[i, b : b + 1, :] = jnp.sum(
                        jnp.where(rows, product[i * SLOTS : (i + 1) * SLOTS], 0.0),
                        axis=0,
                        keepdims=True,
                    )

        if step == 1:
            for d in range(6):

                @pl.when(there[d][1])
                def _():
                    face_copy(d ^ 1).wait_recv()

            loads[11].wait()
            sweep(pressure_ref, source_ref, face_x_ref, face_y_ref, face_z_ref, result_ref)

        for d in range(6):

            @pl.when(there[d][1])
            def _():
                halo_copy(step, d ^ 1).wait_recv()

        outer_tables(step)
        outer_pairs(mine_ref, table_ref, scaled_ref, sums_ref)
        normal = [lane_sums(sums_ref, i) for i in range(3)]

        places, speeds, turning = fields[0:3], fields[3:6], fields[6:9]
        spring_source = springs_ref if step == 0 else springs_out
        shear_sum = [zero] * 3
        torque_sum = [zero] * 3
        for k in range(HIST):
            other = gathered(
                table_ref, range(7), which[k], masks_of(k), member[k], [zero] * 10
            )
            sep = [places[i] - other[i] for i in range(3)]
            square = dot(sep, sep) + soft_length**2
            inverse = lax.rsqrt(square)
            unit = [sep[i] * inverse for i in range(3)]
            overlap = radius + other[9] - square * inverse
            delta = jnp.maximum(overlap, 0.0)
            root = delta * lax.rsqrt(jnp.maximum(overlap, TINY))
            relative = [speeds[i] - other[3 + i] for i in range(3)]
            approach = dot(relative, unit)
            pressing = root * (normal_stiff * delta - normal_damp * approach)
            lever = [radius * turning[i] + other[9] * other[6 + i] for i in range(3)]
            spun = cross(lever, unit)
            contact = [relative[i] - spun[i] for i in range(3)]
            along = dot(contact, unit)
            sliding = [contact[i] - along * unit[i] for i in range(3)]
            spring = [spring_source[i * HIST + k] for i in range(3)]
            tilt = dot(spring, unit)
            stretched = [
                spring[i] - tilt * unit[i] + time_step * sliding[i] for i in range(3)
            ]
            length = jnp.sqrt(dot(stretched, stretched))
            limit = jnp.minimum(
                1.0, friction * jnp.abs(pressing) / jnp.maximum(shear_stiff * length, force_floor)
            )
            scale = valid[k] * limit
            fresh = [scale * stretched[i] for i in range(3)]
            shear = [-shear_stiff * fresh[i] for i in range(3)]
            twist = cross(shear, unit)
            for i in range(3):
                springs_out[i * HIST + k] = fresh[i]
            shear_sum = [shear_sum[i] + shear[i] for i in range(3)]
            torque_sum = [torque_sum[i] + twist[i] for i in range(3)]

        for i in range(3):
            push = normal_stiff * normal[i] + shear_sum[i]
            push = push + drag_coeff * (gas_out[i] - speeds[i])
            speed = speeds[i] + time_step * (push / mass - (gravity if i == 2 else 0.0))
            spin = turning[i] + time_step * (radius * torque_sum[i]) / inertia
            target = own_2_ref if step == 0 else state_out
            target[3 + i] = speed
            target[6 + i] = spin
            target[i] = places[i] + time_step * speed
        if step == 0:
            send_halo(1, [own_2_ref[f] for f in range(9)] + [partner_radius])

    stores = [
        pltpu.make_async_copy(source, target, store_sem.at[n])
        for n, (source, target) in enumerate(
            (
                (state_out.at[0:3], places_out),
                (state_out.at[3:6], speeds_out),
                (state_out.at[6:9], turning_out),
                (springs_out, new_springs_out),
                (force_ref, force_out),
                (result_ref, result_out),
                (arrived_ref, arrived_out),
                (codes_ref, codes_out),
            )
        )
    ]
    for store in stores[:4]:
        store.start()

    for f in range(9):
        picked_ref[:, f, :] = state_out[f]
    picked_ref[:, 9, :] = radius
    for f in range(3 * HIST):
        picked_ref[:, 10 + f, :] = springs_out[f]
    for k in range(HIST):
        picked_ref[:, 22 + k, :] = (code[k] + 1).astype(jnp.float32)
    for f in range(26, 32):
        picked_ref[:, f, :] = zero
    for d in range(6):
        entry = jnp.broadcast_to(departures_ref[d], (8, SLOTS))
        slot = entry & (SLOTS - 1)
        home = lax.shift_right_arithmetic(entry, 7)
        for g in range(4):
            value = zero
            for b in range(BINS):
                taken = jnp.take_along_axis(
                    picked_ref[b, g * 8 : g * 8 + 8, :], slot, axis=1, mode="promise_in_bounds"
                )
                value = jnp.where(home == b, taken, value)
            gone_ref[d, g * 8 : g * 8 + 8, :] = value

        @pl.when(there[d][1])
        def _():
            moved_copy(d).start()

    deposit(counts_ref, radii_ref, cells_ref, state_out, gas_out, force_ref, result_ref)
    stores[4].start()
    stores[5].start()
    for d in range(6):

        @pl.when(there[d][1])
        def _():
            for step in range(SUBSTEPS):
                halo_copy(step, d).wait_send()
            face_copy(d).wait_send()
            moved_copy(d).wait_send()
            moved_copy(d ^ 1).wait_recv()

    for d in range(6):
        codes_ref[d] = come_ref[d, 22:26, :].astype(jnp.int32) - 1
        for f in range(22):
            arrived_ref[f * 6 + d] = come_ref[d, f : f + 1, :]
    for store in stores[6:]:
        store.start()
    for store in stores:
        store.wait()


def deposit(counts_ref, radii_ref, cells_ref, state_ref, gas_ref, force_ref, result_ref):
    size_x, size_y = result_ref.shape[0] // 2, result_ref.shape[1] // 2
    live = jnp.where(live_mask(counts_ref), 1.0, 0.0)
    radius = radii_ref[...]
    values = [drag_coeff * (state_ref[3 + i] - gas_ref[i]) * live for i in range(3)]
    values.append(4.0 / 3.0 * math.pi * (radius * radius * radius) * live)
    values = [halves(value) for value in values]
    for b in range(BINS):
        bx, by, bz = b // 4, b // 2 % 2, b % 2
        block = (
            slice(bx * size_x, (bx + 1) * size_x),
            slice(by * size_y, (by + 1) * size_y),
            slice(bz * SLOTS, (bz + 1) * SLOTS),
        )
        cell = cells_ref[b : b + 1, :]
        rows = one_hot(lax.shift_right_logical(cell, 7))
        lanes = jnp.where(one_hot(cell & (SLOTS - 1)), 1.0, 0.0).astype(jnp.bfloat16)
        right = jnp.concatenate([lanes, lanes], axis=1)
        left = jnp.concatenate(
            [
                jnp.concatenate(
                    [
                        jnp.where(rows, part[b : b + 1, :], 0.0).astype(jnp.bfloat16)
                        for part in value
                    ],
                    axis=1,
                )
                for value in values
            ],
            axis=0,
        )
        product = lax.dot_general(
            left, right, (((1,), (1,)), ((), ())), preferred_element_type=jnp.float32
        )
        parts = [
            product[i * SLOTS : (i + 1) * SLOTS].reshape(size_x, size_y, SLOTS) for i in range(4)
        ]
        for i in range(3):
            force_ref[(i,) + block] = parts[i]
        result_ref[block] = (
            result_ref[block] + volume_coeff * parts[3] + drag_weight * parts[2]
        ) / 6.0


def sweep(pressure_ref, source_ref, face_x_ref, face_y_ref, face_z_ref, result_ref):
    cells_x, cells_y, cells_z = pressure_ref.shape
    row = lax.broadcasted_iota(jnp.int32, (cells_y, cells_z), 0)
    lane = lax.broadcasted_iota(jnp.int32, (cells_y, cells_z), 1)
    for x in range(cells_x):
        here = pressure_ref[x]
        total = pressure_ref[x - 1] if x > 0 else face_x_ref[0]
        total = total + (pressure_ref[x + 1] if x < cells_x - 1 else face_x_ref[1])
        total = total + jnp.where(row == 0, face_y_ref[0, x : x + 1, :], pltpu.roll(here, 1, 0))
        total = total + jnp.where(
            row == cells_y - 1, face_y_ref[1, x : x + 1, :], pltpu.roll(here, cells_y - 1, 0)
        )
        total = total + jnp.where(
            lane == 0,
            jnp.broadcast_to(face_z_ref[0][:, x : x + 1], here.shape),
            pltpu.roll(here, 1, 1),
        )
        total = total + jnp.where(
            lane == cells_z - 1,
            jnp.broadcast_to(face_z_ref[1][:, x : x + 1], here.shape),
            pltpu.roll(here, cells_z - 1, 1),
        )
        result_ref[x] = total + source_ref[x]


def finish(*refs):
    sources, targets, held = refs[0:8], refs[8:16], refs[16:24]
    load_sem, store_sem = refs[24:26]
    parts = [(4, i) for i in range(3)] + [(n, None) for n in (5, 3, 6, 0, 1, 2, 7)]

    def piece(ref, part):
        return ref if part is None else ref.at[part]

    loads, stores = [], []
    for m, (n, part) in enumerate(parts):
        middle = piece(held[n], part)
        loads.append(pltpu.make_async_copy(piece(sources[n], part), middle, load_sem.at[m]))
        stores.append(pltpu.make_async_copy(middle, piece(targets[n], part), store_sem.at[m]))
    for load in loads:
        load.start()
    for load, store in zip(loads, stores):
        load.wait()
        store.start()
    for store in stores:
        store.wait()


def body(
    positions,
    velocities,
    spins,
    radii,
    counts,
    springs,
    partners,
    cells,
    departures,
    fluid_velocity,
    pressure,
    pressure_source,
):
    cells_x, cells_y, cells_z = pressure.shape
    f32 = jnp.float32
    far = pl.BlockSpec(memory_space=pltpu.HBM)
    shape = jax.ShapeDtypeStruct
    rows = (BINS, SLOTS)
    results = (
        shape((3,) + rows, f32),
        shape((3,) + rows, f32),
        shape((3,) + rows, f32),
        shape((3 * HIST,) + rows, f32),
        shape(fluid_velocity.shape, f32),
        shape(pressure.shape, f32),
        shape((132, 1, SLOTS), f32),
        shape((6, 4, SLOTS), jnp.int32),
    )
    made = pl.pallas_call(
        particles,
        out_shape=results,
        in_specs=[far] * 12,
        out_specs=(far,) * 8,
        scratch_shapes=[
            pltpu.VMEM((9,) + rows, f32),
            pltpu.VMEM((3 * HIST,) + rows, f32),
            pltpu.VMEM((3,) + rows, f32),
            pltpu.SMEM(counts.shape, jnp.int32),
            pltpu.VMEM((3,) + rows, f32),
            pltpu.VMEM((3,) + rows, f32),
            pltpu.VMEM((3,) + rows, f32),
            pltpu.VMEM(rows, f32),
            pltpu.VMEM((3 * HIST,) + rows, f32),
            pltpu.VMEM((HIST,) + rows, jnp.int32),
            pltpu.VMEM(rows, jnp.int32),
            pltpu.VMEM((6, 1, SLOTS), jnp.int32),
            pltpu.VMEM(fluid_velocity.shape, f32),
            pltpu.VMEM(pressure.shape, f32),
            pltpu.VMEM(pressure.shape, f32),
            pltpu.VMEM(fluid_velocity.shape, f32),
            pltpu.VMEM(pressure.shape, f32),
            pltpu.VMEM((132, 1, SLOTS), f32),
            pltpu.VMEM((6, 4, SLOTS), jnp.int32),
            pltpu.VMEM((7, 10) + rows, f32),
            pltpu.VMEM((7, 3) + rows, f32),
            pltpu.VMEM((7, BINS, SLOTS, SLOTS), f32),
            pltpu.VMEM((3, BINS, SLOTS, SLOTS), f32),
            pltpu.VMEM((9,) + rows, f32),
            pltpu.VMEM((9,) + rows, f32),
            pltpu.VMEM((SUBSTEPS, 6, 5) + rows, f32),
            pltpu.VMEM((SUBSTEPS, 6, 5) + rows, f32),
            pltpu.VMEM((BINS, 32, SLOTS), f32),
            pltpu.VMEM((6, 32, SLOTS), f32),
            pltpu.VMEM((6, 32, SLOTS), f32),
            pltpu.VMEM((2, cells_x, cells_z), f32),
            pltpu.VMEM((2, cells_y, SLOTS), f32),
            pltpu.VMEM((2, cells_y, cells_z), f32),
            pltpu.VMEM((2, cells_x, cells_z), f32),
            pltpu.VMEM((2, cells_y, SLOTS), f32),
            pltpu.SemaphoreType.DMA((12,)),
            pltpu.SemaphoreType.DMA((9,)),
            pltpu.SemaphoreType.DMA((4, 6)),
            pltpu.SemaphoreType.DMA((4, 6)),
        ],
        compiler_params=pltpu.CompilerParams(
            collective_id=0, has_side_effects=True, vmem_limit_bytes=VMEM_LIMIT
        ),
    )(
        counts,
        positions.reshape((3,) + rows),
        velocities.reshape((3,) + rows),
        spins.reshape((3,) + rows),
        radii.reshape(rows),
        springs.reshape((3 * HIST,) + rows),
        partners.reshape((HIST,) + rows),
        cells.reshape(rows),
        departures.reshape(6, 1, SLOTS),
        fluid_velocity,
        pressure,
        pressure_source,
    )
    places, speeds, turning, last_springs, force, new_pressure, arrived, codes = pl.pallas_call(
        finish,
        out_shape=results,
        in_specs=[far] * 8,
        out_specs=(far,) * 8,
        scratch_shapes=[pltpu.VMEM(result.shape, result.dtype) for result in results]
        + [pltpu.SemaphoreType.DMA((10,)), pltpu.SemaphoreType.DMA((10,))],
        compiler_params=pltpu.CompilerParams(vmem_limit_bytes=VMEM_LIMIT),
    )(*made)
    return (
        places.reshape(positions.shape),
        speeds.reshape(positions.shape),
        turning.reshape(positions.shape),
        last_springs.reshape(springs.shape),
        force,
        new_pressure,
        arrived.reshape(1, 1, 1, 22, 6, SLOTS),
        jnp.swapaxes(codes, 0, 1)[None, None, None],
    )


def solution(mesh):
    return jax.shard_map(
        body,
        mesh=mesh,
        in_specs=(
            P(None, "gx", "gy", "gz", None),
            P(None, "gx", "gy", "gz", None),
            P(None, "gx", "gy", "gz", None),
            P("gx", "gy", "gz", None),
            P("gx", "gy", "gz"),
            P(None, None, "gx", "gy", "gz", None),
            P(None, "gx", "gy", "gz", None),
            P("gx", "gy", "gz", None),
            P("gx", "gy", "gz", None, None),
            P(None, "gx", "gy", "gz"),
            P("gx", "gy", "gz"),
            P("gx", "gy", "gz"),
        ),
        out_specs=(
            P(None, "gx", "gy", "gz", None),
            P(None, "gx", "gy", "gz", None),
            P(None, "gx", "gy", "gz", None),
            P(None, None, "gx", "gy", "gz", None),
            P(None, "gx", "gy", "gz"),
            P("gx", "gy", "gz"),
            P("gx", "gy", "gz", None, None, None),
            P("gx", "gy", "gz", None, None, None),
        ),
        check_vma=False,
    )
```

```python
import functools
import math

import jax
import jax.numpy as jnp
from jax import lax
from jax.experimental import pallas as pl
from jax.experimental.pallas import tpu as pltpu
from jax.sharding import PartitionSpec as P

SUBSTEPS = 2
HIST = 4
BINS = 8
SLOTS = 128
VMEM_LIMIT = 64 * 1024 * 1024

normal_stiff = 100.0
normal_damp = 2.0
shear_stiff = 30.0
friction = 0.5
time_step = 0.05
drag_coeff = 0.8
gravity = 1.0
soft_length = 0.05
force_floor = 0.5
volume_coeff = 100.0
drag_weight = 1.0

NOBODY = -10.0
TINY = 1e-30
SPEED_SCALE = normal_damp / normal_stiff
AXES = ("gx", "gy", "gz")
MESH = pl.DeviceIdType.MESH


def neighbour(direction):
    axis = AXES[direction // 2]
    size = lax.axis_size(axis)
    here = lax.axis_index(axis)
    if direction % 2 == 0:
        return {axis: lax.rem(here + size - 1, size)}, here > 0
    return {axis: lax.rem(here + 1, size)}, here < size - 1


def bin_bits():
    row = lax.broadcasted_iota(jnp.int32, (BINS, SLOTS), 0)
    return [lax.shift_right_logical(row, 2 - axis) & 1 for axis in range(3)]


def swapped(value, axis):
    step = 4 >> axis
    if axis == 0:
        return pltpu.roll(value, step, 0)
    upper = bin_bits()[axis] == 1
    return jnp.where(upper, pltpu.roll(value, step, 0), pltpu.roll(value, BINS - step, 0))


def live_mask(counts_ref):
    row = lax.broadcasted_iota(jnp.int32, (BINS, SLOTS), 0)
    slot = lax.broadcasted_iota(jnp.int32, (BINS, SLOTS), 1)
    limit = jnp.zeros((BINS, SLOTS), jnp.int32)
    for b in range(BINS):
        limit = jnp.where(row == b, counts_ref[b // 4, b // 2 % 2, b % 2], limit)
    return slot < limit


def halves(value):
    high = value.astype(jnp.bfloat16).astype(jnp.float32)
    return high, value - high


def one_hot(index_row):
    rows = lax.broadcasted_iota(jnp.int32, (SLOTS, SLOTS), 0)
    return rows == index_row


def cross(a, b):
    return [
        a[1] * b[2] - a[2] * b[1],
        a[2] * b[0] - a[0] * b[2],
        a[0] * b[1] - a[1] * b[0],
    ]


def dot(a, b):
    return a[0] * b[0] + a[1] * b[1] + a[2] * b[2]


def spread(table_ref, radii_ref, mine_ref, b):
    for f in range(7):
        row = radii_ref[b : b + 1, :] if f == 6 else table_ref[0, f, b : b + 1, :]
        if f in (3, 4, 5):
            row = row * SPEED_SCALE
        mine_ref[f, b] = jnp.broadcast_to(row, (SLOTS, SLOTS)).T


def bin_pairs(mine_ref, table_ref, scaled_ref, tables, sums_ref, first, b):
    row = pl.ds(b, 1)
    for c in range(SLOTS // 8):
        rows = slice(c * 8, c * 8 + 8)
        mine = [mine_ref[f, b, rows, :] for f in range(7)]
        total = None if first else [sums_ref[i, b, rows, :] for i in range(3)]
        for t in tables:
            other = [
                jnp.broadcast_to(ref[t, f, row, :], (8, SLOTS))
                for ref, f in (
                    (table_ref, 0),
                    (table_ref, 1),
                    (table_ref, 2),
                    (scaled_ref, 0),
                    (scaled_ref, 1),
                    (scaled_ref, 2),
                    (table_ref, 9),
                )
            ]
            sep = [mine[i] - other[i] for i in range(3)]
            square = dot(sep, sep) + soft_length**2
            inverse = lax.rsqrt(square)
            overlap = mine[6] + other[6] - square * inverse
            delta = jnp.maximum(overlap, 0.0)
            root = delta * lax.rsqrt(jnp.maximum(overlap, TINY))
            vrel = [mine[3 + i] - other[3 + i] for i in range(3)]
            approach = dot(vrel, sep) * inverse
            weight = (delta - approach) * (root * inverse)
            term = [weight * sep[i] for i in range(3)]
            total = term if total is None else [total[i] + term[i] for i in range(3)]
        for i in range(3):
            sums_ref[i, b, rows, :] = total[i]


def inner_pairs(radii_ref, mine_ref, table_ref, scaled_ref, sums_ref):
    spread(table_ref, radii_ref, mine_ref, 0)
    for b in range(BINS):
        if b < BINS - 1:
            spread(table_ref, radii_ref, mine_ref, b + 1)
        bin_pairs(mine_ref, table_ref, scaled_ref, (0, 1, 2, 3), sums_ref, True, b)


def outer_pairs(mine_ref, table_ref, scaled_ref, tables, sums_ref):
    def one(b, carry):
        bin_pairs(mine_ref, table_ref, scaled_ref, tables, sums_ref, False, b)
        return carry

    lax.fori_loop(0, BINS, one, 0)


def lane_sums(sums_ref, i):
    row = lax.broadcasted_iota(jnp.int32, (BINS, 2 * SLOTS), 0)
    total = jnp.zeros((BINS, SLOTS), jnp.float32)
    for b in range(BINS):
        high, low = halves(sums_ref[i, b])
        right = jnp.concatenate([high.astype(jnp.bfloat16), low.astype(jnp.bfloat16)], axis=1)
        left = jnp.where(row == b, 1.0, 0.0).astype(jnp.bfloat16)
        total = total + lax.dot_general(
            left, right, (((1,), (1,)), ((), ())), preferred_element_type=jnp.float32
        )
    return total


def gathered(table_ref, tables, which, masks, member, got):
    for f in range(10):
        value = got[f]
        for t in tables:
            picked = jnp.take_along_axis(
                table_ref[t, f], member, axis=1, mode="promise_in_bounds"
            )
            value = jnp.where(masks[t], picked, value)
        got[f] = value
    return got


def particles(
    counts_hbm,
    pos_hbm,
    vel_hbm,
    spin_hbm,
    radii_hbm,
    springs_hbm,
    partners_hbm,
    cells_hbm,
    departures_hbm,
    gas_hbm,
    pressure_hbm,
    source_hbm,
    places_out,
    speeds_out,
    turning_out,
    new_springs_out,
    force_out,
    result_out,
    arrived_out,
    codes_out,
    state_out,
    springs_out,
    gas_out,
    counts_ref,
    pos_ref,
    vel_ref,
    spin_ref,
    radii_ref,
    springs_ref,
    partners_ref,
    cells_ref,
    departures_ref,
    gas_ref,
    pressure_ref,
    source_ref,
    force_ref,
    result_ref,
    arrived_ref,
    codes_ref,
    table_ref,
    scaled_ref,
    mine_ref,
    sums_ref,
    own_ref,
    own_2_ref,
    packed_ref,
    halo_ref,
    picked_ref,
    gone_ref,
    come_ref,
    send_y_ref,
    send_z_ref,
    face_x_ref,
    face_y_ref,
    face_z_ref,
    local_sem,
    store_sem,
    send_sem,
    recv_sem,
):
    loads = [
        pltpu.make_async_copy(source, target, local_sem.at[n])
        for n, (source, target) in enumerate(
            (
                (pos_hbm, pos_ref),
                (vel_hbm, vel_ref),
                (spin_hbm, spin_ref),
                (radii_hbm, radii_ref),
                (counts_hbm, counts_ref),
                (pressure_hbm, pressure_ref),
                (partners_hbm, partners_ref),
                (springs_hbm, springs_ref),
                (cells_hbm, cells_ref),
                (departures_hbm, departures_ref),
                (gas_hbm, gas_ref),
                (source_hbm, source_ref),
            )
        )
    ]
    for load in loads:
        load.start()

    there = [neighbour(d) for d in range(6)]

    barrier = pltpu.get_barrier_semaphore()
    for d in range(6):

        @pl.when(there[d][1])
        def _():
            pl.semaphore_signal(barrier, inc=1, device_id=there[d][0], device_id_type=MESH)

    def halo_copy(step, d):
        return pltpu.make_async_remote_copy(
            src_ref=packed_ref.at[step, d],
            dst_ref=halo_ref.at[step, d ^ 1],
            send_sem=send_sem.at[step, d],
            recv_sem=recv_sem.at[step, d ^ 1],
            device_id=there[d][0],
            device_id_type=MESH,
        )

    def moved_copy(d):
        return pltpu.make_async_remote_copy(
            src_ref=gone_ref.at[d],
            dst_ref=come_ref.at[d],
            send_sem=send_sem.at[2, d],
            recv_sem=recv_sem.at[2, d],
            device_id=there[d][0],
            device_id_type=MESH,
        )

    def face_copy(d):
        side = d % 2
        if d < 2:
            source = pressure_ref.at[0 if side == 0 else pressure_ref.shape[0] - 1]
            target = face_x_ref.at[1 - side]
        elif d < 4:
            source, target = send_y_ref.at[side], face_y_ref.at[1 - side]
        else:
            source, target = send_z_ref.at[side], face_z_ref.at[1 - side]
        return pltpu.make_async_remote_copy(
            src_ref=source,
            dst_ref=target,
            send_sem=send_sem.at[3, d],
            recv_sem=recv_sem.at[3, d ^ 1],
            device_id=there[d][0],
            device_id_type=MESH,
        )

    for load in loads[:5]:
        load.wait()
    live = live_mask(counts_ref)
    radius = radii_ref[...]
    partner_radius = jnp.where(live, radius, NOBODY)
    for i in range(3):
        own_ref[i] = pos_ref[i]
        own_ref[3 + i] = vel_ref[i]
        own_ref[6 + i] = spin_ref[i]
    bits = bin_bits()

    def send_halo(step, fields):
        for d in range(6):
            axis = d // 2
            for n in range(5):
                packed_ref[step, d, n] = jnp.where(
                    bits[axis] == d % 2, fields[2 * n], swapped(fields[2 * n + 1], axis)
                )
        if step == 0:
            pl.semaphore_wait(barrier, sum(there[d][1].astype(jnp.int32) for d in range(6)))
        for d in range(6):

            @pl.when(there[d][1])
            def _():
                halo_copy(step, d).start()


    for s in range(6):

        @pl.when(jnp.logical_not(there[s][1]))
        def _():
            for step in range(SUBSTEPS):
                halo_ref[step, s] = jnp.zeros((5, BINS, SLOTS), jnp.float32)
                halo_ref[step, s, 4] = jnp.full((BINS, SLOTS), NOBODY, jnp.float32)
            come_ref[s ^ 1] = jnp.zeros((32, SLOTS), jnp.float32)
            face = (face_x_ref, face_y_ref, face_z_ref)[s // 2]
            face[s % 2] = jnp.zeros(face.shape[1:], jnp.float32)

    send_halo(0, [own_ref[f] for f in range(9)] + [partner_radius])
    for load in loads[5:10]:
        load.wait()
    code = [partners_ref[k] for k in range(HIST)]
    valid = [jnp.where(code[k] >= 0, 1.0, 0.0) for k in range(HIST)]
    member = [jnp.maximum(code[k], 0) & (SLOTS - 1) for k in range(HIST)]
    which = [lax.shift_right_logical(jnp.maximum(code[k], 0), 7) for k in range(HIST)]

    def masks_of(k):
        found = [which[k] == 0]
        for axis in range(3):
            found.append(which[k] == 2 * axis + 2 - bits[axis])
        for axis in range(3):
            found.append(which[k] == 2 * axis + 1 + bits[axis])
        return found

    safe = jnp.where(radius > 0.0, radius, 1.0)
    mass = safe * 10.0
    mass = mass * mass * mass
    inertia = 0.4 * mass * safe * safe

    def inner_tables(fields):
        for f in range(10):
            table_ref[0, f] = fields[f]
            for axis in range(3):
                value = swapped(fields[f], axis)
                if f == axis:
                    value = value + jnp.where(bits[axis] == 0, 1.0, -1.0)
                table_ref[1 + axis, f] = value
        for t in range(4):
            for i in range(3):
                scaled_ref[t, i] = table_ref[t, 3 + i] * SPEED_SCALE

    def outer_tables(step, axes):
        for axis in axes:
            for n in range(5):
                low, high = halo_ref[step, 2 * axis, n], halo_ref[step, 2 * axis + 1, n]
                first = jnp.where(bits[axis] == 0, swapped(low, axis), swapped(high, axis))
                second = jnp.where(bits[axis] == 0, low, high)
                for f, value in ((2 * n, first), (2 * n + 1, second)):
                    if f == axis:
                        value = value + jnp.where(bits[axis] == 0, -1.0, 1.0)
                    table_ref[4 + axis, f] = value
                    if f in (3, 4, 5):
                        scaled_ref[4 + axis, f - 3] = value * SPEED_SCALE

    cells_x, cells_y, cells_z = pressure_ref.shape

    def send_faces():
        lane = lax.broadcasted_iota(jnp.int32, (cells_y, SLOTS), 1)
        for side in range(2):
            send_y_ref[side] = pressure_ref[:, 0 if side == 0 else cells_y - 1, :]
            face = jnp.zeros((cells_y, SLOTS), jnp.float32)
            for x in range(cells_x):
                if side == 0:
                    column = pressure_ref[x, :, 0:SLOTS][:, 0:1]
                else:
                    column = pressure_ref[x, :, cells_z - SLOTS : cells_z][:, SLOTS - 1 : SLOTS]
                face = jnp.where(lane == x, jnp.broadcast_to(column, (cells_y, SLOTS)), face)
            send_z_ref[side] = face
        for d in range(6):

            @pl.when(there[d][1])
            def _():
                face_copy(d).start()

    zero = jnp.zeros((BINS, SLOTS), jnp.float32)
    for step in range(SUBSTEPS):
        source = own_ref if step == 0 else own_2_ref
        fields = [source[f] for f in range(9)] + [partner_radius]
        inner_tables(fields)
        inner_pairs(radii_ref, mine_ref, table_ref, scaled_ref, sums_ref)

        if step == 0:
            send_faces()
            loads[10].wait()
            for b in range(BINS):
                bx, by, bz = b // 4, b // 2 % 2, b % 2
                size_x, size_y = cells_x // 2, cells_y // 2
                block = gas_ref[
                    :,
                    bx * size_x : (bx + 1) * size_x,
                    by * size_y : (by + 1) * size_y,
                    bz * SLOTS : (bz + 1) * SLOTS,
                ].reshape(3 * SLOTS, SLOTS)
                cell = cells_ref[b : b + 1, :]
                high, low = halves(block)
                left = jnp.concatenate(
                    [high.astype(jnp.bfloat16), low.astype(jnp.bfloat16)], axis=1
                )
                lanes = jnp.where(one_hot(cell & (SLOTS - 1)), 1.0, 0.0).astype(jnp.bfloat16)
                right = jnp.concatenate([lanes, lanes], axis=0)
                product = jnp.dot(left, right, preferred_element_type=jnp.float32)
                rows = one_hot(lax.shift_right_logical(cell, 7))
                for i in range(3):
                    gas_out[i, b : b + 1, :] = jnp.sum(
                        jnp.where(rows, product[i * SLOTS : (i + 1) * SLOTS], 0.0),
                        axis=0,
                        keepdims=True,
                    )

        if step == 1:
            for d in range(6):

                @pl.when(there[d][1])
                def _():
                    face_copy(d ^ 1).wait_recv()

            loads[11].wait()
            sweep(pressure_ref, source_ref, face_x_ref, face_y_ref, face_z_ref, result_ref)

        for axes in ((1, 2), (0,)):
            for d in [2 * axis + side for axis in axes for side in range(2)]:

                @pl.when(there[d][1])
                def _():
                    halo_copy(step, d ^ 1).wait_recv()

            outer_tables(step, axes)
            outer_pairs(mine_ref, table_ref, scaled_ref, [4 + axis for axis in axes], sums_ref)
        normal = [lane_sums(sums_ref, i) for i in range(3)]

        places, speeds, turning = fields[0:3], fields[3:6], fields[6:9]
        spring_source = springs_ref if step == 0 else springs_out
        shear_sum = [zero] * 3
        torque_sum = [zero] * 3
        for k in range(HIST):
            other = gathered(
                table_ref, range(7), which[k], masks_of(k), member[k], [zero] * 10
            )
            sep = [places[i] - other[i] for i in range(3)]
            square = dot(sep, sep) + soft_length**2
            inverse = lax.rsqrt(square)
            unit = [sep[i] * inverse for i in range(3)]
            overlap = radius + other[9] - square * inverse
            delta = jnp.maximum(overlap, 0.0)
            root = delta * lax.rsqrt(jnp.maximum(overlap, TINY))
            relative = [speeds[i] - other[3 + i] for i in range(3)]
            approach = dot(relative, unit)
            pressing = root * (normal_stiff * delta - normal_damp * approach)
            lever = [radius * turning[i] + other[9] * other[6 + i] for i in range(3)]
            spun = cross(lever, unit)
            contact = [relative[i] - spun[i] for i in range(3)]
            along = dot(contact, unit)
            sliding = [contact[i] - along * unit[i] for i in range(3)]
            spring = [spring_source[i * HIST + k] for i in range(3)]
            tilt = dot(spring, unit)
            stretched = [
                spring[i] - tilt * unit[i] + time_step * sliding[i] for i in range(3)
            ]
            length = jnp.sqrt(dot(stretched, stretched))
            limit = jnp.minimum(
                1.0, friction * jnp.abs(pressing) / jnp.maximum(shear_stiff * length, force_floor)
            )
            scale = valid[k] * limit
            fresh = [scale * stretched[i] for i in range(3)]
            shear = [-shear_stiff * fresh[i] for i in range(3)]
            twist = cross(shear, unit)
            for i in range(3):
                springs_out[i * HIST + k] = fresh[i]
            shear_sum = [shear_sum[i] + shear[i] for i in range(3)]
            torque_sum = [torque_sum[i] + twist[i] for i in range(3)]

        for i in range(3):
            push = normal_stiff * normal[i] + shear_sum[i]
            push = push + drag_coeff * (gas_out[i] - speeds[i])
            speed = speeds[i] + time_step * (push / mass - (gravity if i == 2 else 0.0))
            spin = turning[i] + time_step * (radius * torque_sum[i]) / inertia
            target = own_2_ref if step == 0 else state_out
            target[3 + i] = speed
            target[6 + i] = spin
            target[i] = places[i] + time_step * speed
        if step == 0:
            send_halo(1, [own_2_ref[f] for f in range(9)] + [partner_radius])

    stores = [
        pltpu.make_async_copy(source, target, store_sem.at[n])
        for n, (source, target) in enumerate(
            (
                (state_out.at[0:3], places_out),
                (state_out.at[3:6], speeds_out),
                (state_out.at[6:9], turning_out),
                (springs_out, new_springs_out),
                (force_ref, force_out),
                (result_ref, result_out),
                (arrived_ref, arrived_out),
                (codes_ref, codes_out),
            )
        )
    ]
    for store in stores[:4]:
        store.start()

    for f in range(9):
        picked_ref[:, f, :] = state_out[f]
    picked_ref[:, 9, :] = radius
    for f in range(3 * HIST):
        picked_ref[:, 10 + f, :] = springs_out[f]
    for k in range(HIST):
        picked_ref[:, 22 + k, :] = (code[k] + 1).astype(jnp.float32)
    for f in range(26, 32):
        picked_ref[:, f, :] = zero
    for d in range(6):
        entry = jnp.broadcast_to(departures_ref[d], (8, SLOTS))
        slot = entry & (SLOTS - 1)
        home = lax.shift_right_arithmetic(entry, 7)
        for g in range(4):
            value = zero
            for b in range(BINS):
                taken = jnp.take_along_axis(
                    picked_ref[b, g * 8 : g * 8 + 8, :], slot, axis=1, mode="promise_in_bounds"
                )
                value = jnp.where(home == b, taken, value)
            gone_ref[d, g * 8 : g * 8 + 8, :] = value

        @pl.when(there[d][1])
        def _():
            moved_copy(d).start()

    deposit(counts_ref, radii_ref, cells_ref, state_out, gas_out, force_ref, result_ref)
    stores[4].start()
    stores[5].start()
    for d in range(6):

        @pl.when(there[d][1])
        def _():
            for step in range(SUBSTEPS):
                halo_copy(step, d).wait_send()
            face_copy(d).wait_send()
            moved_copy(d).wait_send()
            moved_copy(d ^ 1).wait_recv()

    for d in range(6):
        codes_ref[d] = come_ref[d, 22:26, :].astype(jnp.int32) - 1
        for f in range(22):
            arrived_ref[f * 6 + d] = come_ref[d, f : f + 1, :]
    for store in stores[6:]:
        store.start()
    for store in stores:
        store.wait()


def deposit(counts_ref, radii_ref, cells_ref, state_ref, gas_ref, force_ref, result_ref):
    size_x, size_y = result_ref.shape[0] // 2, result_ref.shape[1] // 2
    live = jnp.where(live_mask(counts_ref), 1.0, 0.0)
    radius = radii_ref[...]
    values = [drag_coeff * (state_ref[3 + i] - gas_ref[i]) * live for i in range(3)]
    values.append(4.0 / 3.0 * math.pi * (radius * radius * radius) * live)
    values = [halves(value) for value in values]
    for b in range(BINS):
        bx, by, bz = b // 4, b // 2 % 2, b % 2
        block = (
            slice(bx * size_x, (bx + 1) * size_x),
            slice(by * size_y, (by + 1) * size_y),
            slice(bz * SLOTS, (bz + 1) * SLOTS),
        )
        cell = cells_ref[b : b + 1, :]
        rows = one_hot(lax.shift_right_logical(cell, 7))
        lanes = jnp.where(one_hot(cell & (SLOTS - 1)), 1.0, 0.0).astype(jnp.bfloat16)
        right = jnp.concatenate([lanes, lanes], axis=1)
        left = jnp.concatenate(
            [
                jnp.concatenate(
                    [
                        jnp.where(rows, part[b : b + 1, :], 0.0).astype(jnp.bfloat16)
                        for part in value
                    ],
                    axis=1,
                )
                for value in values
            ],
            axis=0,
        )
        product = lax.dot_general(
            left, right, (((1,), (1,)), ((), ())), preferred_element_type=jnp.float32
        )
        parts = [
            product[i * SLOTS : (i + 1) * SLOTS].reshape(size_x, size_y, SLOTS) for i in range(4)
        ]
        for i in range(3):
            force_ref[(i,) + block] = parts[i]
        result_ref[block] = (
            result_ref[block] + volume_coeff * parts[3] + drag_weight * parts[2]
        ) / 6.0


def sweep(pressure_ref, source_ref, face_x_ref, face_y_ref, face_z_ref, result_ref):
    cells_x, cells_y, cells_z = pressure_ref.shape
    row = lax.broadcasted_iota(jnp.int32, (cells_y, cells_z), 0)
    lane = lax.broadcasted_iota(jnp.int32, (cells_y, cells_z), 1)
    for x in range(cells_x):
        here = pressure_ref[x]
        total = pressure_ref[x - 1] if x > 0 else face_x_ref[0]
        total = total + (pressure_ref[x + 1] if x < cells_x - 1 else face_x_ref[1])
        total = total + jnp.where(row == 0, face_y_ref[0, x : x + 1, :], pltpu.roll(here, 1, 0))
        total = total + jnp.where(
            row == cells_y - 1, face_y_ref[1, x : x + 1, :], pltpu.roll(here, cells_y - 1, 0)
        )
        total = total + jnp.where(
            lane == 0,
            jnp.broadcast_to(face_z_ref[0][:, x : x + 1], here.shape),
            pltpu.roll(here, 1, 1),
        )
        total = total + jnp.where(
            lane == cells_z - 1,
            jnp.broadcast_to(face_z_ref[1][:, x : x + 1], here.shape),
            pltpu.roll(here, cells_z - 1, 1),
        )
        result_ref[x] = total + source_ref[x]


def finish(*refs):
    sources, targets, held = refs[0:8], refs[8:16], refs[16:24]
    load_sem, store_sem = refs[24:26]
    parts = [(4, i) for i in range(3)] + [(n, None) for n in (5, 3, 6, 0, 1, 2, 7)]

    def piece(ref, part):
        return ref if part is None else ref.at[part]

    loads, stores = [], []
    for m, (n, part) in enumerate(parts):
        middle = piece(held[n], part)
        loads.append(pltpu.make_async_copy(piece(sources[n], part), middle, load_sem.at[m]))
        stores.append(pltpu.make_async_copy(middle, piece(targets[n], part), store_sem.at[m]))
    for load in loads:
        load.start()
    for load, store in zip(loads, stores):
        load.wait()
        store.start()
    for store in stores:
        store.wait()


def body(
    positions,
    velocities,
    spins,
    radii,
    counts,
    springs,
    partners,
    cells,
    departures,
    fluid_velocity,
    pressure,
    pressure_source,
):
    cells_x, cells_y, cells_z = pressure.shape
    f32 = jnp.float32
    far = pl.BlockSpec(memory_space=pltpu.HBM)
    shape = jax.ShapeDtypeStruct
    rows = (BINS, SLOTS)
    results = (
        shape((3,) + rows, f32),
        shape((3,) + rows, f32),
        shape((3,) + rows, f32),
        shape((3 * HIST,) + rows, f32),
        shape(fluid_velocity.shape, f32),
        shape(pressure.shape, f32),
        shape((132, 1, SLOTS), f32),
        shape((6, 4, SLOTS), jnp.int32),
    )
    made = pl.pallas_call(
        particles,
        out_shape=results,
        in_specs=[far] * 12,
        out_specs=(far,) * 8,
        scratch_shapes=[
            pltpu.VMEM((9,) + rows, f32),
            pltpu.VMEM((3 * HIST,) + rows, f32),
            pltpu.VMEM((3,) + rows, f32),
            pltpu.SMEM(counts.shape, jnp.int32),
            pltpu.VMEM((3,) + rows, f32),
            pltpu.VMEM((3,) + rows, f32),
            pltpu.VMEM((3,) + rows, f32),
            pltpu.VMEM(rows, f32),
            pltpu.VMEM((3 * HIST,) + rows, f32),
            pltpu.VMEM((HIST,) + rows, jnp.int32),
            pltpu.VMEM(rows, jnp.int32),
            pltpu.VMEM((6, 1, SLOTS), jnp.int32),
            pltpu.VMEM(fluid_velocity.shape, f32),
            pltpu.VMEM(pressure.shape, f32),
            pltpu.VMEM(pressure.shape, f32),
            pltpu.VMEM(fluid_velocity.shape, f32),
            pltpu.VMEM(pressure.shape, f32),
            pltpu.VMEM((132, 1, SLOTS), f32),
            pltpu.VMEM((6, 4, SLOTS), jnp.int32),
            pltpu.VMEM((7, 10) + rows, f32),
            pltpu.VMEM((7, 3) + rows, f32),
            pltpu.VMEM((7, BINS, SLOTS, SLOTS), f32),
            pltpu.VMEM((3, BINS, SLOTS, SLOTS), f32),
            pltpu.VMEM((9,) + rows, f32),
            pltpu.VMEM((9,) + rows, f32),
            pltpu.VMEM((SUBSTEPS, 6, 5) + rows, f32),
            pltpu.VMEM((SUBSTEPS, 6, 5) + rows, f32),
            pltpu.VMEM((BINS, 32, SLOTS), f32),
            pltpu.VMEM((6, 32, SLOTS), f32),
            pltpu.VMEM((6, 32, SLOTS), f32),
            pltpu.VMEM((2, cells_x, cells_z), f32),
            pltpu.VMEM((2, cells_y, SLOTS), f32),
            pltpu.VMEM((2, cells_y, cells_z), f32),
            pltpu.VMEM((2, cells_x, cells_z), f32),
            pltpu.VMEM((2, cells_y, SLOTS), f32),
            pltpu.SemaphoreType.DMA((12,)),
            pltpu.SemaphoreType.DMA((9,)),
            pltpu.SemaphoreType.DMA((4, 6)),
            pltpu.SemaphoreType.DMA((4, 6)),
        ],
        compiler_params=pltpu.CompilerParams(
            collective_id=0, has_side_effects=True, vmem_limit_bytes=VMEM_LIMIT
        ),
    )(
        counts,
        positions.reshape((3,) + rows),
        velocities.reshape((3,) + rows),
        spins.reshape((3,) + rows),
        radii.reshape(rows),
        springs.reshape((3 * HIST,) + rows),
        partners.reshape((HIST,) + rows),
        cells.reshape(rows),
        departures.reshape(6, 1, SLOTS),
        fluid_velocity,
        pressure,
        pressure_source,
    )
    places, speeds, turning, last_springs, force, new_pressure, arrived, codes = pl.pallas_call(
        finish,
        out_shape=results,
        in_specs=[far] * 8,
        out_specs=(far,) * 8,
        scratch_shapes=[pltpu.VMEM(result.shape, result.dtype) for result in results]
        + [pltpu.SemaphoreType.DMA((10,)), pltpu.SemaphoreType.DMA((10,))],
        compiler_params=pltpu.CompilerParams(vmem_limit_bytes=VMEM_LIMIT),
    )(*made)
    return (
        places.reshape(positions.shape),
        speeds.reshape(positions.shape),
        turning.reshape(positions.shape),
        last_springs.reshape(springs.shape),
        force,
        new_pressure,
        arrived.reshape(1, 1, 1, 22, 6, SLOTS),
        jnp.swapaxes(codes, 0, 1)[None, None, None],
    )


def solution(mesh):
    return jax.shard_map(
        body,
        mesh=mesh,
        in_specs=(
            P(None, "gx", "gy", "gz", None),
            P(None, "gx", "gy", "gz", None),
            P(None, "gx", "gy", "gz", None),
            P("gx", "gy", "gz", None),
            P("gx", "gy", "gz"),
            P(None, None, "gx", "gy", "gz", None),
            P(None, "gx", "gy", "gz", None),
            P("gx", "gy", "gz", None),
            P("gx", "gy", "gz", None, None),
            P(None, "gx", "gy", "gz"),
            P("gx", "gy", "gz"),
            P("gx", "gy", "gz"),
        ),
        out_specs=(
            P(None, "gx", "gy", "gz", None),
            P(None, "gx", "gy", "gz", None),
            P(None, "gx", "gy", "gz", None),
            P(None, None, "gx", "gy", "gz", None),
            P(None, "gx", "gy", "gz"),
            P("gx", "gy", "gz"),
            P("gx", "gy", "gz", None, None, None),
            P("gx", "gy", "gz", None, None, None),
        ),
        check_vma=False,
    )
```

```python
import functools
import math

import jax
import jax.numpy as jnp
from jax import lax
from jax.experimental import pallas as pl
from jax.experimental.pallas import tpu as pltpu
from jax.sharding import PartitionSpec as P

SUBSTEPS = 2
HIST = 4
BINS = 8
SLOTS = 128
VMEM_LIMIT = 64 * 1024 * 1024

normal_stiff = 100.0
normal_damp = 2.0
shear_stiff = 30.0
friction = 0.5
time_step = 0.05
drag_coeff = 0.8
gravity = 1.0
soft_length = 0.05
force_floor = 0.5
volume_coeff = 100.0
drag_weight = 1.0

NOBODY = -10.0
TINY = 1e-30
SPEED_SCALE = normal_damp / normal_stiff
AXES = ("gx", "gy", "gz")
MESH = pl.DeviceIdType.MESH


def neighbour(direction):
    axis = AXES[direction // 2]
    size = lax.axis_size(axis)
    here = lax.axis_index(axis)
    if direction % 2 == 0:
        return {axis: lax.rem(here + size - 1, size)}, here > 0
    return {axis: lax.rem(here + 1, size)}, here < size - 1


def bin_bits():
    row = lax.broadcasted_iota(jnp.int32, (BINS, SLOTS), 0)
    return [lax.shift_right_logical(row, 2 - axis) & 1 for axis in range(3)]


def swapped(value, axis):
    step = 4 >> axis
    if axis == 0:
        return pltpu.roll(value, step, 0)
    upper = bin_bits()[axis] == 1
    return jnp.where(upper, pltpu.roll(value, step, 0), pltpu.roll(value, BINS - step, 0))


def live_mask(counts_ref):
    row = lax.broadcasted_iota(jnp.int32, (BINS, SLOTS), 0)
    slot = lax.broadcasted_iota(jnp.int32, (BINS, SLOTS), 1)
    limit = jnp.zeros((BINS, SLOTS), jnp.int32)
    for b in range(BINS):
        limit = jnp.where(row == b, counts_ref[b // 4, b // 2 % 2, b % 2], limit)
    return slot < limit


def halves(value):
    high = value.astype(jnp.bfloat16).astype(jnp.float32)
    return high, value - high


def one_hot(index_row):
    rows = lax.broadcasted_iota(jnp.int32, (SLOTS, SLOTS), 0)
    return rows == index_row


def cross(a, b):
    return [
        a[1] * b[2] - a[2] * b[1],
        a[2] * b[0] - a[0] * b[2],
        a[0] * b[1] - a[1] * b[0],
    ]


def dot(a, b):
    return a[0] * b[0] + a[1] * b[1] + a[2] * b[2]


def spread(table_ref, radii_ref, mine_ref, b):
    for f in range(7):
        row = radii_ref[b : b + 1, :] if f == 6 else table_ref[0, f, b : b + 1, :]
        if f in (3, 4, 5):
            row = row * SPEED_SCALE
        mine_ref[f, b] = jnp.broadcast_to(row, (SLOTS, SLOTS)).T


def bin_pairs(mine_ref, table_ref, scaled_ref, tables, sums_ref, first, b):
    row = pl.ds(b, 1)
    for c in range(SLOTS // 8):
        rows = slice(c * 8, c * 8 + 8)
        mine = [mine_ref[f, b, rows, :] for f in range(7)]
        total = None if first else [sums_ref[i, b, rows, :] for i in range(3)]
        for t in tables:
            other = [
                jnp.broadcast_to(ref[t, f, row, :], (8, SLOTS))
                for ref, f in (
                    (table_ref, 0),
                    (table_ref, 1),
                    (table_ref, 2),
                    (scaled_ref, 0),
                    (scaled_ref, 1),
                    (scaled_ref, 2),
                    (table_ref, 9),
                )
            ]
            sep = [mine[i] - other[i] for i in range(3)]
            square = dot(sep, sep) + soft_length**2
            inverse = lax.rsqrt(square)
            overlap = mine[6] + other[6] - square * inverse
            delta = jnp.maximum(overlap, 0.0)
            root = delta * lax.rsqrt(jnp.maximum(overlap, TINY))
            vrel = [mine[3 + i] - other[3 + i] for i in range(3)]
            approach = dot(vrel, sep) * inverse
            weight = (delta - approach) * (root * inverse)
            term = [weight * sep[i] for i in range(3)]
            total = term if total is None else [total[i] + term[i] for i in range(3)]
        for i in range(3):
            sums_ref[i, b, rows, :] = total[i]


def inner_pairs(radii_ref, mine_ref, table_ref, scaled_ref, sums_ref):
    spread(table_ref, radii_ref, mine_ref, 0)
    for b in range(BINS):
        if b < BINS - 1:
            spread(table_ref, radii_ref, mine_ref, b + 1)
        bin_pairs(mine_ref, table_ref, scaled_ref, (0, 1, 2, 3), sums_ref, True, b)


def outer_pairs(mine_ref, table_ref, scaled_ref, sums_ref):
    def one(b, carry):
        bin_pairs(mine_ref, table_ref, scaled_ref, (4, 5, 6), sums_ref, False, b)
        return carry

    lax.fori_loop(0, BINS, one, 0)


def lane_sums(sums_ref, i):
    row = lax.broadcasted_iota(jnp.int32, (BINS, 2 * SLOTS), 0)
    total = jnp.zeros((BINS, SLOTS), jnp.float32)
    for b in range(BINS):
        high, low = halves(sums_ref[i, b])
        right = jnp.concatenate([high.astype(jnp.bfloat16), low.astype(jnp.bfloat16)], axis=1)
        left = jnp.where(row == b, 1.0, 0.0).astype(jnp.bfloat16)
        total = total + lax.dot_general(
            left, right, (((1,), (1,)), ((), ())), preferred_element_type=jnp.float32
        )
    return total


def gathered(table_ref, tables, which, masks, member, got):
    for f in range(10):
        value = got[f]
        for t in tables:
            picked = jnp.take_along_axis(
                table_ref[t, f], member, axis=1, mode="promise_in_bounds"
            )
            value = jnp.where(masks[t], picked, value)
        got[f] = value
    return got


def particles(
    counts_hbm,
    pos_hbm,
    vel_hbm,
    spin_hbm,
    radii_hbm,
    springs_hbm,
    partners_hbm,
    cells_hbm,
    departures_hbm,
    gas_hbm,
    pressure_hbm,
    source_hbm,
    places_out,
    speeds_out,
    turning_out,
    new_springs_out,
    force_out,
    result_out,
    arrived_out,
    codes_out,
    state_out,
    springs_out,
    gas_out,
    counts_ref,
    pos_ref,
    vel_ref,
    spin_ref,
    radii_ref,
    springs_ref,
    partners_ref,
    cells_ref,
    departures_ref,
    gas_ref,
    pressure_ref,
    source_ref,
    force_ref,
    result_ref,
    arrived_ref,
    codes_ref,
    table_ref,
    scaled_ref,
    mine_ref,
    sums_ref,
    own_ref,
    own_2_ref,
    packed_ref,
    halo_ref,
    picked_ref,
    gone_ref,
    come_ref,
    send_y_ref,
    send_z_ref,
    face_x_ref,
    face_y_ref,
    face_z_ref,
    local_sem,
    store_sem,
    send_sem,
    recv_sem,
):
    loads = [
        pltpu.make_async_copy(source, target, local_sem.at[n])
        for n, (source, target) in enumerate(
            (
                (pos_hbm, pos_ref),
                (vel_hbm, vel_ref),
                (spin_hbm, spin_ref),
                (radii_hbm, radii_ref),
                (counts_hbm, counts_ref),
                (pressure_hbm, pressure_ref),
                (partners_hbm, partners_ref),
                (springs_hbm, springs_ref),
                (cells_hbm, cells_ref),
                (departures_hbm, departures_ref),
                (gas_hbm, gas_ref),
                (source_hbm, source_ref),
            )
        )
    ]
    for load in loads:
        load.start()

    there = [neighbour(d) for d in range(6)]

    barrier = pltpu.get_barrier_semaphore()
    for d in range(6):

        @pl.when(there[d][1])
        def _():
            pl.semaphore_signal(barrier, inc=1, device_id=there[d][0], device_id_type=MESH)

    def halo_copy(step, d):
        return pltpu.make_async_remote_copy(
            src_ref=packed_ref.at[step, d],
            dst_ref=halo_ref.at[step, d ^ 1],
            send_sem=send_sem.at[step, d],
            recv_sem=recv_sem.at[step, d ^ 1],
            device_id=there[d][0],
            device_id_type=MESH,
        )

    def moved_copy(d):
        return pltpu.make_async_remote_copy(
            src_ref=gone_ref.at[d],
            dst_ref=come_ref.at[d],
            send_sem=send_sem.at[2, d],
            recv_sem=recv_sem.at[2, d],
            device_id=there[d][0],
            device_id_type=MESH,
        )

    def face_copy(d):
        side = d % 2
        if d < 2:
            source = pressure_ref.at[0 if side == 0 else pressure_ref.shape[0] - 1]
            target = face_x_ref.at[1 - side]
        elif d < 4:
            source, target = send_y_ref.at[side], face_y_ref.at[1 - side]
        else:
            source, target = send_z_ref.at[side], face_z_ref.at[1 - side]
        return pltpu.make_async_remote_copy(
            src_ref=source,
            dst_ref=target,
            send_sem=send_sem.at[3, d],
            recv_sem=recv_sem.at[3, d ^ 1],
            device_id=there[d][0],
            device_id_type=MESH,
        )

    for load in loads[:5]:
        load.wait()
    live = live_mask(counts_ref)
    radius = radii_ref[...]
    partner_radius = jnp.where(live, radius, NOBODY)
    for i in range(3):
        own_ref[i] = pos_ref[i]
        own_ref[3 + i] = vel_ref[i]
        own_ref[6 + i] = spin_ref[i]
    bits = bin_bits()

    def inner_tables(fields):
        for f in range(10):
            table_ref[0, f] = fields[f]
            for axis in range(3):
                value = swapped(fields[f], axis)
                if f == axis:
                    value = value + jnp.where(bits[axis] == 0, 1.0, -1.0)
                table_ref[1 + axis, f] = value
        for t in range(4):
            for i in range(3):
                scaled_ref[t, i] = table_ref[t, 3 + i] * SPEED_SCALE

    def send_halo(step, fields):
        for d in range(6):
            axis = d // 2
            for n in range(5):
                packed_ref[step, d, n] = jnp.where(
                    bits[axis] == d % 2, fields[2 * n], swapped(fields[2 * n + 1], axis)
                )
        if step == 0:
            inner_tables(fields)
            pl.semaphore_wait(barrier, sum(there[d][1].astype(jnp.int32) for d in range(6)))
        for d in range(6):

            @pl.when(there[d][1])
            def _():
                halo_copy(step, d).start()


    for s in range(6):

        @pl.when(jnp.logical_not(there[s][1]))
        def _():
            for step in range(SUBSTEPS):
                halo_ref[step, s] = jnp.zeros((5, BINS, SLOTS), jnp.float32)
                halo_ref[step, s, 4] = jnp.full((BINS, SLOTS), NOBODY, jnp.float32)
            come_ref[s ^ 1] = jnp.zeros((32, SLOTS), jnp.float32)
            face = (face_x_ref, face_y_ref, face_z_ref)[s // 2]
            face[s % 2] = jnp.zeros(face.shape[1:], jnp.float32)

    send_halo(0, [own_ref[f] for f in range(9)] + [partner_radius])
    for load in loads[5:10]:
        load.wait()
    code = [partners_ref[k] for k in range(HIST)]
    valid = [jnp.where(code[k] >= 0, 1.0, 0.0) for k in range(HIST)]
    member = [jnp.maximum(code[k], 0) & (SLOTS - 1) for k in range(HIST)]
    which = [lax.shift_right_logical(jnp.maximum(code[k], 0), 7) for k in range(HIST)]

    def masks_of(k):
        found = [which[k] == 0]
        for axis in range(3):
            found.append(which[k] == 2 * axis + 2 - bits[axis])
        for axis in range(3):
            found.append(which[k] == 2 * axis + 1 + bits[axis])
        return found

    safe = jnp.where(radius > 0.0, radius, 1.0)
    mass = safe * 10.0
    mass = mass * mass * mass
    inertia = 0.4 * mass * safe * safe

    def outer_tables(step):
        for axis in range(3):
            for n in range(5):
                low, high = halo_ref[step, 2 * axis, n], halo_ref[step, 2 * axis + 1, n]
                first = jnp.where(bits[axis] == 0, swapped(low, axis), swapped(high, axis))
                second = jnp.where(bits[axis] == 0, low, high)
                for f, value in ((2 * n, first), (2 * n + 1, second)):
                    if f == axis:
                        value = value + jnp.where(bits[axis] == 0, -1.0, 1.0)
                    table_ref[4 + axis, f] = value
                    if f in (3, 4, 5):
                        scaled_ref[4 + axis, f - 3] = value * SPEED_SCALE

    cells_x, cells_y, cells_z = pressure_ref.shape

    def send_faces():
        lane = lax.broadcasted_iota(jnp.int32, (cells_y, SLOTS), 1)
        for side in range(2):
            send_y_ref[side] = pressure_ref[:, 0 if side == 0 else cells_y - 1, :]
            face = jnp.zeros((cells_y, SLOTS), jnp.float32)
            for x in range(cells_x):
                if side == 0:
                    column = pressure_ref[x, :, 0:SLOTS][:, 0:1]
                else:
                    column = pressure_ref[x, :, cells_z - SLOTS : cells_z][:, SLOTS - 1 : SLOTS]
                face = jnp.where(lane == x, jnp.broadcast_to(column, (cells_y, SLOTS)), face)
            send_z_ref[side] = face
        for d in range(6):

            @pl.when(there[d][1])
            def _():
                face_copy(d).start()

    zero = jnp.zeros((BINS, SLOTS), jnp.float32)
    for step in range(SUBSTEPS):
        source = own_ref if step == 0 else own_2_ref
        fields = [source[f] for f in range(9)] + [partner_radius]
        if step > 0:
            inner_tables(fields)
        inner_pairs(radii_ref, mine_ref, table_ref, scaled_ref, sums_ref)

        if step == 0:
            send_faces()
            loads[10].wait()
            for b in range(BINS):
                bx, by, bz = b // 4, b // 2 % 2, b % 2
                size_x, size_y = cells_x // 2, cells_y // 2
                block = gas_ref[
                    :,
                    bx * size_x : (bx + 1) * size_x,
                    by * size_y : (by + 1) * size_y,
                    bz * SLOTS : (bz + 1) * SLOTS,
                ].reshape(3 * SLOTS, SLOTS)
                cell = cells_ref[b : b + 1, :]
                high, low = halves(block)
                left = jnp.concatenate(
                    [high.astype(jnp.bfloat16), low.astype(jnp.bfloat16)], axis=1
                )
                lanes = jnp.where(one_hot(cell & (SLOTS - 1)), 1.0, 0.0).astype(jnp.bfloat16)
                right = jnp.concatenate([lanes, lanes], axis=0)
                product = jnp.dot(left, right, preferred_element_type=jnp.float32)
                rows = one_hot(lax.shift_right_logical(cell, 7))
                for i in range(3):
                    gas_out[i, b : b + 1, :] = jnp.sum(
                        jnp.where(rows, product[i * SLOTS : (i + 1) * SLOTS], 0.0),
                        axis=0,
                        keepdims=True,
                    )

        for d in range(6):

            @pl.when(there[d][1])
            def _():
                halo_copy(step, d ^ 1).wait_recv()

        outer_tables(step)
        outer_pairs(mine_ref, table_ref, scaled_ref, sums_ref)
        normal = [lane_sums(sums_ref, i) for i in range(3)]

        places, speeds, turning = fields[0:3], fields[3:6], fields[6:9]
        spring_source = springs_ref if step == 0 else springs_out
        shear_sum = [zero] * 3
        torque_sum = [zero] * 3
        for k in range(HIST):
            other = gathered(
                table_ref, range(7), which[k], masks_of(k), member[k], [zero] * 10
            )
            sep = [places[i] - other[i] for i in range(3)]
            square = dot(sep, sep) + soft_length**2
            inverse = lax.rsqrt(square)
            unit = [sep[i] * inverse for i in range(3)]
            overlap = radius + other[9] - square * inverse
            delta = jnp.maximum(overlap, 0.0)
            root = delta * lax.rsqrt(jnp.maximum(overlap, TINY))
            relative = [speeds[i] - other[3 + i] for i in range(3)]
            approach = dot(relative, unit)
            pressing = root * (normal_stiff * delta - normal_damp * approach)
            lever = [radius * turning[i] + other[9] * other[6 + i] for i in range(3)]
            spun = cross(lever, unit)
            contact = [relative[i] - spun[i] for i in range(3)]
            along = dot(contact, unit)
            sliding = [contact[i] - along * unit[i] for i in range(3)]
            spring = [spring_source[i * HIST + k] for i in range(3)]
            tilt = dot(spring, unit)
            stretched = [
                spring[i] - tilt * unit[i] + time_step * sliding[i] for i in range(3)
            ]
            length = jnp.sqrt(dot(stretched, stretched))
            limit = jnp.minimum(
                1.0, friction * jnp.abs(pressing) / jnp.maximum(shear_stiff * length, force_floor)
            )
            scale = valid[k] * limit
            fresh = [scale * stretched[i] for i in range(3)]
            shear = [-shear_stiff * fresh[i] for i in range(3)]
            twist = cross(shear, unit)
            for i in range(3):
                springs_out[i * HIST + k] = fresh[i]
            shear_sum = [shear_sum[i] + shear[i] for i in range(3)]
            torque_sum = [torque_sum[i] + twist[i] for i in range(3)]

        for i in range(3):
            push = normal_stiff * normal[i] + shear_sum[i]
            push = push + drag_coeff * (gas_out[i] - speeds[i])
            speed = speeds[i] + time_step * (push / mass - (gravity if i == 2 else 0.0))
            spin = turning[i] + time_step * (radius * torque_sum[i]) / inertia
            target = own_2_ref if step == 0 else state_out
            target[3 + i] = speed
            target[6 + i] = spin
            target[i] = places[i] + time_step * speed
        if step == 0:
            send_halo(1, [own_2_ref[f] for f in range(9)] + [partner_radius])

    stores = [
        pltpu.make_async_copy(source, target, store_sem.at[n])
        for n, (source, target) in enumerate(
            (
                (state_out.at[0:3], places_out),
                (state_out.at[3:6], speeds_out),
                (state_out.at[6:9], turning_out),
                (springs_out, new_springs_out),
                (force_ref, force_out),
                (result_ref, result_out),
                (arrived_ref, arrived_out),
                (codes_ref, codes_out),
            )
        )
    ]
    for store in stores[:4]:
        store.start()

    for f in range(9):
        picked_ref[:, f, :] = state_out[f]
    picked_ref[:, 9, :] = radius
    for f in range(3 * HIST):
        picked_ref[:, 10 + f, :] = springs_out[f]
    for k in range(HIST):
        picked_ref[:, 22 + k, :] = (code[k] + 1).astype(jnp.float32)
    for f in range(26, 32):
        picked_ref[:, f, :] = zero
    for d in range(6):
        entry = jnp.broadcast_to(departures_ref[d], (8, SLOTS))
        slot = entry & (SLOTS - 1)
        home = lax.shift_right_arithmetic(entry, 7)
        for g in range(4):
            value = zero
            for b in range(BINS):
                taken = jnp.take_along_axis(
                    picked_ref[b, g * 8 : g * 8 + 8, :], slot, axis=1, mode="promise_in_bounds"
                )
                value = jnp.where(home == b, taken, value)
            gone_ref[d, g * 8 : g * 8 + 8, :] = value

        @pl.when(there[d][1])
        def _():
            moved_copy(d).start()

    deposit(counts_ref, radii_ref, cells_ref, state_out, gas_out, force_ref, result_ref)
    stores[4].start()
    for d in range(6):

        @pl.when(there[d][1])
        def _():
            face_copy(d ^ 1).wait_recv()

    loads[11].wait()
    sweep(pressure_ref, source_ref, face_x_ref, face_y_ref, face_z_ref, result_ref)
    stores[5].start()
    for d in range(6):

        @pl.when(there[d][1])
        def _():
            for step in range(SUBSTEPS):
                halo_copy(step, d).wait_send()
            face_copy(d).wait_send()
            moved_copy(d).wait_send()
            moved_copy(d ^ 1).wait_recv()

    for d in range(6):
        codes_ref[d] = come_ref[d, 22:26, :].astype(jnp.int32) - 1
        for f in range(22):
            arrived_ref[f * 6 + d] = come_ref[d, f : f + 1, :]
    for store in stores[6:]:
        store.start()
    for store in stores:
        store.wait()


def deposit(counts_ref, radii_ref, cells_ref, state_ref, gas_ref, force_ref, result_ref):
    size_x, size_y = result_ref.shape[0] // 2, result_ref.shape[1] // 2
    live = jnp.where(live_mask(counts_ref), 1.0, 0.0)
    radius = radii_ref[...]
    values = [drag_coeff * (state_ref[3 + i] - gas_ref[i]) * live for i in range(3)]
    values.append(4.0 / 3.0 * math.pi * (radius * radius * radius) * live)
    values = [halves(value) for value in values]
    for b in range(BINS):
        bx, by, bz = b // 4, b // 2 % 2, b % 2
        block = (
            slice(bx * size_x, (bx + 1) * size_x),
            slice(by * size_y, (by + 1) * size_y),
            slice(bz * SLOTS, (bz + 1) * SLOTS),
        )
        cell = cells_ref[b : b + 1, :]
        rows = one_hot(lax.shift_right_logical(cell, 7))
        lanes = jnp.where(one_hot(cell & (SLOTS - 1)), 1.0, 0.0).astype(jnp.bfloat16)
        right = jnp.concatenate([lanes, lanes], axis=1)
        left = jnp.concatenate(
            [
                jnp.concatenate(
                    [
                        jnp.where(rows, part[b : b + 1, :], 0.0).astype(jnp.bfloat16)
                        for part in value
                    ],
                    axis=1,
                )
                for value in values
            ],
            axis=0,
        )
        product = lax.dot_general(
            left, right, (((1,), (1,)), ((), ())), preferred_element_type=jnp.float32
        )
        parts = [
            product[i * SLOTS : (i + 1) * SLOTS].reshape(size_x, size_y, SLOTS) for i in range(4)
        ]
        for i in range(3):
            force_ref[(i,) + block] = parts[i]
        result_ref[block] = volume_coeff * parts[3] + drag_weight * parts[2]


def sweep(pressure_ref, source_ref, face_x_ref, face_y_ref, face_z_ref, result_ref):
    cells_x, cells_y, cells_z = pressure_ref.shape
    row = lax.broadcasted_iota(jnp.int32, (cells_y, cells_z), 0)
    lane = lax.broadcasted_iota(jnp.int32, (cells_y, cells_z), 1)
    for x in range(cells_x):
        here = pressure_ref[x]
        total = pressure_ref[x - 1] if x > 0 else face_x_ref[0]
        total = total + (pressure_ref[x + 1] if x < cells_x - 1 else face_x_ref[1])
        total = total + jnp.where(row == 0, face_y_ref[0, x : x + 1, :], pltpu.roll(here, 1, 0))
        total = total + jnp.where(
            row == cells_y - 1, face_y_ref[1, x : x + 1, :], pltpu.roll(here, cells_y - 1, 0)
        )
        total = total + jnp.where(
            lane == 0,
            jnp.broadcast_to(face_z_ref[0][:, x : x + 1], here.shape),
            pltpu.roll(here, 1, 1),
        )
        total = total + jnp.where(
            lane == cells_z - 1,
            jnp.broadcast_to(face_z_ref[1][:, x : x + 1], here.shape),
            pltpu.roll(here, cells_z - 1, 1),
        )
        result_ref[x] = (total + source_ref[x] + result_ref[x]) / 6.0


def finish(*refs):
    sources, targets, held = refs[0:8], refs[8:16], refs[16:24]
    load_sem, store_sem = refs[24:26]
    parts = [(4, i) for i in range(3)] + [(n, None) for n in (5, 3, 6, 0, 1, 2, 7)]

    def piece(ref, part):
        return ref if part is None else ref.at[part]

    loads, stores = [], []
    for m, (n, part) in enumerate(parts):
        middle = piece(held[n], part)
        loads.append(pltpu.make_async_copy(piece(sources[n], part), middle, load_sem.at[m]))
        stores.append(pltpu.make_async_copy(middle, piece(targets[n], part), store_sem.at[m]))
    for load in loads:
        load.start()
    for load, store in zip(loads, stores):
        load.wait()
        store.start()
    for store in stores:
        store.wait()


def body(
    positions,
    velocities,
    spins,
    radii,
    counts,
    springs,
    partners,
    cells,
    departures,
    fluid_velocity,
    pressure,
    pressure_source,
):
    cells_x, cells_y, cells_z = pressure.shape
    f32 = jnp.float32
    far = pl.BlockSpec(memory_space=pltpu.HBM)
    shape = jax.ShapeDtypeStruct
    rows = (BINS, SLOTS)
    results = (
        shape((3,) + rows, f32),
        shape((3,) + rows, f32),
        shape((3,) + rows, f32),
        shape((3 * HIST,) + rows, f32),
        shape(fluid_velocity.shape, f32),
        shape(pressure.shape, f32),
        shape((132, 1, SLOTS), f32),
        shape((6, 4, SLOTS), jnp.int32),
    )
    made = pl.pallas_call(
        particles,
        out_shape=results,
        in_specs=[far] * 12,
        out_specs=(far,) * 8,
        scratch_shapes=[
            pltpu.VMEM((9,) + rows, f32),
            pltpu.VMEM((3 * HIST,) + rows, f32),
            pltpu.VMEM((3,) + rows, f32),
            pltpu.SMEM(counts.shape, jnp.int32),
            pltpu.VMEM((3,) + rows, f32),
            pltpu.VMEM((3,) + rows, f32),
            pltpu.VMEM((3,) + rows, f32),
            pltpu.VMEM(rows, f32),
            pltpu.VMEM((3 * HIST,) + rows, f32),
            pltpu.VMEM((HIST,) + rows, jnp.int32),
            pltpu.VMEM(rows, jnp.int32),
            pltpu.VMEM((6, 1, SLOTS), jnp.int32),
            pltpu.VMEM(fluid_velocity.shape, f32),
            pltpu.VMEM(pressure.shape, f32),
            pltpu.VMEM(pressure.shape, f32),
            pltpu.VMEM(fluid_velocity.shape, f32),
            pltpu.VMEM(pressure.shape, f32),
            pltpu.VMEM((132, 1, SLOTS), f32),
            pltpu.VMEM((6, 4, SLOTS), jnp.int32),
            pltpu.VMEM((7, 10) + rows, f32),
            pltpu.VMEM((7, 3) + rows, f32),
            pltpu.VMEM((7, BINS, SLOTS, SLOTS), f32),
            pltpu.VMEM((3, BINS, SLOTS, SLOTS), f32),
            pltpu.VMEM((9,) + rows, f32),
            pltpu.VMEM((9,) + rows, f32),
            pltpu.VMEM((SUBSTEPS, 6, 5) + rows, f32),
            pltpu.VMEM((SUBSTEPS, 6, 5) + rows, f32),
            pltpu.VMEM((BINS, 32, SLOTS), f32),
            pltpu.VMEM((6, 32, SLOTS), f32),
            pltpu.VMEM((6, 32, SLOTS), f32),
            pltpu.VMEM((2, cells_x, cells_z), f32),
            pltpu.VMEM((2, cells_y, SLOTS), f32),
            pltpu.VMEM((2, cells_y, cells_z), f32),
            pltpu.VMEM((2, cells_x, cells_z), f32),
            pltpu.VMEM((2, cells_y, SLOTS), f32),
            pltpu.SemaphoreType.DMA((12,)),
            pltpu.SemaphoreType.DMA((9,)),
            pltpu.SemaphoreType.DMA((4, 6)),
            pltpu.SemaphoreType.DMA((4, 6)),
        ],
        compiler_params=pltpu.CompilerParams(
            collective_id=0, has_side_effects=True, vmem_limit_bytes=VMEM_LIMIT
        ),
    )(
        counts,
        positions.reshape((3,) + rows),
        velocities.reshape((3,) + rows),
        spins.reshape((3,) + rows),
        radii.reshape(rows),
        springs.reshape((3 * HIST,) + rows),
        partners.reshape((HIST,) + rows),
        cells.reshape(rows),
        departures.reshape(6, 1, SLOTS),
        fluid_velocity,
        pressure,
        pressure_source,
    )
    places, speeds, turning, last_springs, force, new_pressure, arrived, codes = pl.pallas_call(
        finish,
        out_shape=results,
        in_specs=[far] * 8,
        out_specs=(far,) * 8,
        scratch_shapes=[pltpu.VMEM(result.shape, result.dtype) for result in results]
        + [pltpu.SemaphoreType.DMA((10,)), pltpu.SemaphoreType.DMA((10,))],
        compiler_params=pltpu.CompilerParams(vmem_limit_bytes=VMEM_LIMIT),
    )(*made)
    return (
        places.reshape(positions.shape),
        speeds.reshape(positions.shape),
        turning.reshape(positions.shape),
        last_springs.reshape(springs.shape),
        force,
        new_pressure,
        arrived.reshape(1, 1, 1, 22, 6, SLOTS),
        jnp.swapaxes(codes, 0, 1)[None, None, None],
    )


def solution(mesh):
    return jax.shard_map(
        body,
        mesh=mesh,
        in_specs=(
            P(None, "gx", "gy", "gz", None),
            P(None, "gx", "gy", "gz", None),
            P(None, "gx", "gy", "gz", None),
            P("gx", "gy", "gz", None),
            P("gx", "gy", "gz"),
            P(None, None, "gx", "gy", "gz", None),
            P(None, "gx", "gy", "gz", None),
            P("gx", "gy", "gz", None),
            P("gx", "gy", "gz", None, None),
            P(None, "gx", "gy", "gz"),
            P("gx", "gy", "gz"),
            P("gx", "gy", "gz"),
        ),
        out_specs=(
            P(None, "gx", "gy", "gz", None),
            P(None, "gx", "gy", "gz", None),
            P(None, "gx", "gy", "gz", None),
            P(None, None, "gx", "gy", "gz", None),
            P(None, "gx", "gy", "gz"),
            P("gx", "gy", "gz"),
            P("gx", "gy", "gz", None, None, None),
            P("gx", "gy", "gz", None, None, None),
        ),
        check_vma=False,
    )
```
